512 devices in a mesh: dp: 32 (over y_hi, x, core), blk: 16 (over z, y_lo).
Axes of the slice: x: 4, y: 8 (y_hi: 4, y_lo: 2; y = y_hi * 2 + y_lo), z: 8, core: 2. Of those that a mesh axis runs over, the one named last changes fastest.
Arguments:
- tokens: bfloat16 [6144, 4096], P(('dp', 'blk')), may hold values from -6 to 6
- sequence_labels: int32 [512, 12], P(('dp', 'blk')), may hold values from 0 to 3, never falling along the last dimension, each value on 1 to 6 neighbouring positions
- response_mask: int32 [512, 12], P(('dp', 'blk')), may hold values 0 or 1
- frozen_gate_up: bfloat16 [2, 4096, 14336], P(None, 'dp', 'blk'), may hold values from -0.09375 to 0.09375
- adapter_down_maps: bfloat16 [4096, 32], replicated, may hold values from -0.09375 to 0.09375
- adapter_up_maps: bfloat16 [32, 14336], P(None, 'blk'), may hold values from -0.59765625 to 0.59765625
- readout: bfloat16 [14336], P('blk'), may hold values from -0.046875 to 0.046875
Outputs:
- dpo_loss: float32 [], replicated
- grad_a: float32 [4096, 32], P('dp')
- grad_b: float32 [32, 14336], P('dp', 'blk')
The draws below stay inside these ranges and needn't reach their ends.
Inputs may be any that keep to these rules, and one draw needn't show every extreme that they name: `sequence_labels`: within each block the sequence numbers never fall; every number of 0 to 3 covers 1 to 6 rows, one exactly 6.
All inputs are finite; a program needn't handle non-finite values. No bound on the sum of `response_mask` on one device may be relied on, other than what follows from the above.
Results may differ from the reference program's by a relative error of at most 0.0033.
Values may be sent and summed in bfloat16 or wider, within the bound.
No kernel may reach another device: no remote copies, remote signals or barrier semaphores. Data moves between devices by JAX's collectives and lax.ppermute only.
A program may use at most 64 MiB of HBM per device.

```python
import math
import jax
import jax.numpy as jnp
import numpy as np
from jax import lax

MODEL_WIDTH = 4096
ADAPTER_RANK = 16
SEQS = 4
ROWS = 12
BLOCKS = 512
TOKENS = 6144
HIDDEN_UNITS = 14336
N_BLK = 16


def with_ends(result, key, low, top_value):
    extent = result.shape
    place = [jax.random.randint(jax.random.fold_in(key, axis), (), 0, extent[axis]) for axis in range(len(extent))]
    result = result.at[tuple(place)].set(low)
    longest = extent.index(max(extent))
    place[longest] = (place[longest] + 1) % extent[longest]
    return result.at[tuple(place)].set(top_value)


def block_levels(own_key, dims, cuts, low, high):
    loudness, own = 1.0, jax.random.fold_in(own_key, 6)
    for position, shards_of in cuts:
        heights = jnp.exp(jax.random.uniform(jax.random.fold_in(own, position), (shards_of,), jnp.float32, low / len(cuts), high / len(cuts)))
        loudness = loudness * jnp.repeat(heights, dims[position] // shards_of).reshape([-1 if axis == position else 1 for axis in range(len(dims))])
    return loudness


def length_profile(amount, total, bound, skew):
    loads = [(1 << 20) // math.isqrt(grade ** skew) + 1 for grade in range(2, amount + 1)]
    rest, holding = total - bound - (amount - 1), [1] * (amount - 1)
    while rest > 0:
        free = [i for i in range(amount - 1) if holding[i] < bound]
        whole, left = sum([loads[i] for i in free]), rest
        for i in free:
            addition = min(bound - holding[i], max(1, left * loads[i] // whole), rest)
            holding[i] = holding[i] + addition
            rest = rest - addition
    return np.array([bound] + holding)


def ragged(key, count, total, limit, skew):
    if count == 2:
        one = jax.random.randint(key, (), max(1, total - limit), min(limit, total - 1) + 1)
        return jnp.stack([one, total - one])
    tallies = jnp.asarray(length_profile(count, total, limit, skew), jnp.int32)
    twos = (count - 1) // 2
    giver, taker = tallies[1:1 + 2 * twos:2], tallies[2:2 + 2 * twos:2]
    slack = jnp.minimum(giver - 1, limit - taker)
    moved = jax.random.randint(jax.random.fold_in(key, 1), (twos,), 0, 1 << 20) % (slack + 1)
    tallies = tallies.at[1:1 + 2 * twos:2].set(giver - moved).at[2:2 + 2 * twos:2].set(taker + moved)
    return tallies[jax.random.permutation(jax.random.fold_in(key, 2), count)]


def bell_draw(rng, extent, width, bound, shards=(), kind=jnp.bfloat16):
    factor_of = block_levels(rng, extent, shards, -0.22, 0.18) if shards else 1.0
    result = jax.random.normal(rng, extent, jnp.float32) * width * factor_of
    return jnp.minimum(jnp.maximum(result, -bound), bound).astype(kind)


def setup_inputs(seed: int = 0) -> dict:
    keys = jax.random.split(jax.random.key(seed), 8)
    tokens = bell_draw(keys[0], (TOKENS, MODEL_WIDTH), 1.0, 6.0, ((0, 512),))
    sequence_labels = jax.vmap(lambda own: jnp.searchsorted(jnp.cumsum(ragged(own, SEQS, ROWS, ROWS // 2, 2)), jnp.arange(ROWS), side="right"))(jax.random.split(keys[1], BLOCKS)).reshape((BLOCKS, ROWS)).astype(jnp.int32)
    response_mask = with_ends((jax.random.randint(keys[2], (BLOCKS, ROWS), 0, 4) < 3).astype(jnp.int32), jax.random.fold_in(keys[2], 1), 0, 1)
    frozen_gate_up = bell_draw(keys[3], (2, MODEL_WIDTH, HIDDEN_UNITS), MODEL_WIDTH ** -0.5, 0.09375, ((1, 32), (2, 16)))
    adapter_down_maps = bell_draw(keys[4], (MODEL_WIDTH, 2 * ADAPTER_RANK), MODEL_WIDTH ** -0.5, 0.09375)
    adapter_up_maps = bell_draw(keys[5], (2 * ADAPTER_RANK, HIDDEN_UNITS), 0.1, 0.59765625, ((1, 16),))
    readout = bell_draw(keys[6], (HIDDEN_UNITS,), HIDDEN_UNITS ** -0.5, 0.046875, ((0, 16),))
    return {"tokens": tokens, "sequence_labels": sequence_labels, "response_mask": response_mask, "frozen_gate_up": frozen_gate_up, "adapter_down_maps": adapter_down_maps, "adapter_up_maps": adapter_up_maps, "readout": readout}


dpo_beta = 0.1
loss_scale = 1024.0
highest = lax.Precision.HIGHEST


def span_terms(tokens_part, low_part, w_gate, w_up, gate_adapter_up, up_adapter_rows, readout_f):
    low_rank_output = gate_adapter_up.shape[0]
    gate_ref = jnp.dot(tokens_part, w_gate, preferred_element_type=jnp.float32)
    up_ref = jnp.dot(tokens_part, w_up, preferred_element_type=jnp.float32)
    gate_pol = gate_ref + jnp.dot(low_part[:, :low_rank_output], gate_adapter_up, preferred_element_type=jnp.float32)
    up_pol = up_ref + jnp.dot(low_part[:, low_rank_output:], up_adapter_rows, preferred_element_type=jnp.float32)
    sig_ref = jax.nn.sigmoid(gate_ref)
    sig_pol = jax.nn.sigmoid(gate_pol)
    score_ref = jnp.dot(gate_ref * sig_ref * up_ref, readout_f, precision=highest)
    score_pol = jnp.dot(gate_pol * sig_pol * up_pol, readout_f, precision=highest)
    k_gate = readout_f * sig_pol * (1.0 + gate_pol * (1.0 - sig_pol)) * up_pol
    k_up = readout_f * gate_pol * sig_pol
    mixed_terms = jnp.concatenate([jnp.dot(k_gate, gate_adapter_up.astype(jnp.float32).T, precision=highest), jnp.dot(k_up, up_adapter_rows.astype(jnp.float32).T, precision=highest)], axis=1)
    return jnp.stack([score_ref, score_pol], axis=1), mixed_terms, k_gate, k_up


def pair_margins(scores, sequence_labels, response_mask):
    block_total, row_count = sequence_labels.shape
    onehot = ((sequence_labels[:, :, None] == jnp.arange(SEQS, dtype=jnp.int32)[None, None, :]) & (response_mask[:, :, None] > 0)).astype(jnp.float32)
    seq_sums = jnp.einsum("brs,brk->bsk", onehot, scores.reshape(block_total, row_count, 2), precision=highest)
    filled = jnp.sum(onehot, axis=1)
    change = seq_sums[:, :, 1] - seq_sums[:, :, 0]
    margin_gap = change[:, 0::2] - change[:, 1::2]
    pair_valid = ((filled[:, 0::2] > 0.5) & (filled[:, 1::2] > 0.5)).astype(jnp.float32)
    return margin_gap, pair_valid, onehot


def row_cotangents(scaled, onehot):
    block_total = scaled.shape[0]
    signed = jnp.stack([scaled, -scaled], axis=2).reshape(block_total, -1)
    return jnp.einsum("brs,bs->br", onehot, signed, precision=highest)


def reference(tokens, sequence_labels, response_mask, frozen_gate_up, adapter_down_maps, adapter_up_maps, readout):
    block_total, row_count = sequence_labels.shape
    low_rank_output = adapter_down_maps.shape[1] // 2
    group_rows = row_count * N_BLK
    groups_in = tokens.reshape(-1, group_rows, tokens.shape[1])
    w_gate = frozen_gate_up[0]
    w_up = frozen_gate_up[1]
    gate_adapter_up = adapter_up_maps[:low_rank_output]
    up_adapter_rows = adapter_up_maps[low_rank_output:]
    readout_f = readout.astype(jnp.float32)

    def forward(device_group):
        input_low_rank = jnp.dot(device_group, adapter_down_maps, preferred_element_type=jnp.float32).astype(jnp.bfloat16)
        return span_terms(device_group, input_low_rank, w_gate, w_up, gate_adapter_up, up_adapter_rows, readout_f)[0]

    scores = lax.map(forward, groups_in).reshape(block_total * row_count, 2)
    margin_gap, pair_valid, onehot = pair_margins(scores, sequence_labels, response_mask)
    pair_total = jnp.maximum(jnp.sum(pair_valid), 1.0)
    logit_arg = dpo_beta * margin_gap
    log_total = jnp.sum(pair_valid * jax.nn.log_sigmoid(logit_arg))
    dpo_loss = -log_total / pair_total
    scaled = -loss_scale * dpo_beta * pair_valid * jax.nn.sigmoid(-logit_arg) / pair_total
    cotangent = row_cotangents(scaled, onehot).reshape(-1, group_rows)

    def backward(running, item):
        device_group, group_cot = item
        input_low_rank = jnp.dot(device_group, adapter_down_maps, preferred_element_type=jnp.float32).astype(jnp.bfloat16)
        score_part, mixed_terms, k_gate, k_up = span_terms(device_group, input_low_rank, w_gate, w_up, gate_adapter_up, up_adapter_rows, readout_f)
        weighted = input_low_rank.astype(jnp.float32) * group_cot[:, None]
        grad_b_block = jnp.concatenate([jnp.dot(weighted[:, :low_rank_output].T, k_gate, precision=highest), jnp.dot(weighted[:, low_rank_output:].T, k_up, precision=highest)], axis=0)
        projected = (group_cot[:, None] * mixed_terms).astype(jnp.bfloat16)
        grad_a_block = jnp.dot(device_group.T, projected, preferred_element_type=jnp.float32)
        return (running[0] + grad_a_block, running[1] + grad_b_block), None

    initial_carry = (jnp.zeros((tokens.shape[1], 2 * low_rank_output), jnp.float32), jnp.zeros((2 * low_rank_output, adapter_up_maps.shape[1]), jnp.float32))
    totals, unused = lax.scan(backward, initial_carry, (groups_in, cotangent))
    return dpo_loss, totals[0], totals[1]
```

```python
import jax
import jax.numpy as jnp
from jax import lax
from jax.sharding import Mesh, PartitionSpec as P

SEQS = 4
ROWS = 12
RANK = 16
WIDTH = 4096
DPO_BETA = 0.1
LOSS_SCALE = 1024.0
HIGHEST = lax.Precision.HIGHEST
F32 = jnp.float32
BF16 = jnp.bfloat16

AXES = ("yh", "x", "c", "z", "yl")
SIZES = (4, 4, 2, 8, 2)
DP = ("yh", "x", "c")
BLK = ("z", "yl")
SWAP = [(0, 1), (1, 0)]


def split_terms(value):
    high = value.astype(BF16)
    low = (value - high.astype(F32)).astype(BF16)
    return high, low


def on_device(tokens, sequence_labels, response_mask, frozen, down, up, readout):
    n_blk, n_dp = 16, 32
    core = lax.axis_index("c")
    units = frozen.shape[2]

    own = lax.all_to_all(frozen, "c", split_axis=0, concat_axis=0)
    weights = lax.all_gather(own.reshape(-1, units), ("yh", "x"), axis=0, tiled=True)

    code = jnp.where(response_mask > 0, sequence_labels, SEQS).astype(BF16)
    block = jnp.concatenate(
        [tokens, jnp.pad(code, ((0, 3), (0, WIDTH - ROWS)))], axis=0
    )
    everyone = lax.all_to_all(
        jnp.broadcast_to(block[None], (n_blk,) + block.shape), BLK, split_axis=0, concat_axis=0
    )
    codes = everyone[:, ROWS, :ROWS].astype(jnp.int32)
    mine = everyone[:, :ROWS].reshape(n_blk * ROWS, WIDTH)
    theirs = lax.ppermute(mine, "c", SWAP)

    low = jnp.dot(mine, down, preferred_element_type=F32).astype(BF16)
    far_half = jnp.dot(theirs, weights, preferred_element_type=F32)
    from_partner = lax.ppermute(far_half, "c", SWAP)
    near_half = jnp.dot(mine, weights, preferred_element_type=F32)
    gate_ref = jnp.where(core == 0, near_half, from_partner)
    up_ref = jnp.where(core == 0, from_partner, near_half)

    b_gate, b_up = up[:RANK], up[RANK:]
    readout_f = readout.astype(F32)
    gate_pol = gate_ref + jnp.dot(low[:, :RANK], b_gate, preferred_element_type=F32)
    up_pol = up_ref + jnp.dot(low[:, RANK:], b_up, preferred_element_type=F32)
    sig_ref = jax.nn.sigmoid(gate_ref)
    sig_pol = jax.nn.sigmoid(gate_pol)
    act_pol = gate_pol * sig_pol
    change = jnp.sum((act_pol * up_pol - gate_ref * sig_ref * up_ref) * readout_f, axis=1)
    k_gate = readout_f * sig_pol * (1.0 + gate_pol * (1.0 - sig_pol)) * up_pol
    k_up = readout_f * act_pol
    contract_last = (((1,), (1,)), ((), ()))
    mixed = jnp.concatenate(
        [
            lax.dot_general(k_gate, b_gate.astype(F32), contract_last, precision=HIGHEST),
            lax.dot_general(k_up, b_up.astype(F32), contract_last, precision=HIGHEST),
        ],
        axis=1,
    )

    pairs = jnp.arange(SEQS // 2, dtype=jnp.int32)
    chosen = (codes[:, :, None] == 2 * pairs).astype(F32)
    rejected = (codes[:, :, None] == 2 * pairs + 1).astype(F32)
    signs = chosen - rejected
    valid = (jnp.max(chosen, axis=1) * jnp.max(rejected, axis=1)).reshape(-1)
    gap_part = jnp.sum(signs * change.reshape(n_blk, ROWS, 1), axis=1).reshape(-1)

    per_peer = mixed.reshape(-1, n_blk, 2).transpose(1, 2, 0).reshape(n_blk, -1)
    gaps_out = jnp.broadcast_to(jnp.pad(gap_part, (0, 96))[None], (n_blk, 128))
    arrived = lax.all_to_all(
        jnp.concatenate([per_peer, gaps_out], axis=1), BLK, split_axis=0, concat_axis=0, tiled=True
    )
    total = jnp.sum(arrived, axis=0)
    columns = total[: 2 * n_blk * ROWS].reshape(2, -1)
    logit = DPO_BETA * total[2 * n_blk * ROWS : 2 * n_blk * ROWS + 2 * n_blk]
    log_sum = jnp.sum(valid * jax.nn.log_sigmoid(logit))
    scaled = -LOSS_SCALE * DPO_BETA * valid * jax.nn.sigmoid(-logit)
    cotangent = jnp.sum(signs * scaled.reshape(n_blk, 1, -1), axis=2).reshape(-1)

    weighted = low.astype(F32) * cotangent[:, None]
    contract_first = (((0,), (0,)), ((), ()))
    grad_b_part = jnp.concatenate(
        [
            lax.dot_general(weighted[:, :RANK], k_gate, contract_first, precision=HIGHEST),
            lax.dot_general(weighted[:, RANK:], k_up, contract_first, precision=HIGHEST),
        ],
        axis=0,
    )
    projected = columns * cotangent[None]
    terms = jnp.dot(
        jnp.concatenate(split_terms(projected), axis=0), mine, preferred_element_type=F32
    )
    grad_a_part = terms[:2] + terms[2:]

    scalars = jnp.concatenate([log_sum[None], jnp.sum(valid)[None], jnp.zeros((126,), F32)])
    outgoing = jnp.concatenate(
        [
            grad_b_part,
            grad_a_part.reshape(2, n_dp, -1).transpose(1, 0, 2).reshape(n_dp, -1),
            jnp.broadcast_to(scalars[None], (n_dp, 128)),
        ],
        axis=1,
    )
    summed = jnp.sum(
        lax.all_to_all(outgoing, DP, split_axis=0, concat_axis=0, tiled=True), axis=0
    )
    rows_a = WIDTH // n_dp
    log_total, count = summed[units + 2 * rows_a], summed[units + 2 * rows_a + 1]
    pair_total = jnp.maximum(count, 1.0)
    grad_b = (summed[:units] / pair_total)[None]
    two = (summed[units : units + 2 * rows_a] / pair_total).reshape(1, 2, rows_a)
    grad_a = lax.all_to_all(
        jnp.broadcast_to(two, (n_blk, 2, rows_a)), BLK, split_axis=0, concat_axis=0
    )
    return -log_total / pair_total, grad_a.reshape(2 * n_blk, rows_a).T, grad_b


def solution(mesh):
    fine = Mesh(mesh.devices.reshape(SIZES), AXES)
    in_specs = (
        P(AXES, None),
        P(AXES, None),
        P(AXES, None),
        P(None, DP, BLK),
        P(),
        P(None, BLK),
        P(BLK),
    )
    out_specs = (P(), P(DP, None), P(DP, BLK))
    return jax.shard_map(
        on_device, mesh=fine, in_specs=in_specs, out_specs=out_specs, check_vma=False
    )
```

```python
import jax
import jax.numpy as jnp
from jax import lax
from jax.experimental import pallas as pl
from jax.experimental.pallas import tpu as pltpu
from jax.sharding import Mesh, PartitionSpec as P

SEQS = 4
ROWS = 12
RANK = 16
WIDTH = 4096
DPO_BETA = 0.1
LOSS_SCALE = 1024.0
HIGHEST = lax.Precision.HIGHEST
F32 = jnp.float32
BF16 = jnp.bfloat16

AXES = ("s", "t", "x", "c", "z", "yl")
SIZES = (2, 2, 4, 2, 8, 2)
DP = ("s", "t", "x", "c")
BLK = ("z", "yl")
YH = ("s", "t")
SWAP = [(0, 1), (1, 0)]

SLICE = 128
HALF = WIDTH // 2
LANES = 128
COLS = 512
SKIP = 384
GROUP = 384
BLOCKS = GROUP // ROWS
WIDE = 2 * COLS + LANES


def fetch(value, axes, size, k):
    return lax.ppermute(value, axes, [((i + k) % size, i) for i in range(size)])


def products(place, tok, own, own1, own3, own2g, own2u, rest, rest1, rest3, rest2a, rest2b, down, count,
             far, near_x, near_code, w, far_x):
    yh, x, core = place[0], place[1], place[2]
    row_of = {1: 0, 3: 2 * SLICE, 2: 4 * SLICE}

    def piece(k, j, part):
        begin = part * SLICE if k == 0 else row_of[k] + part * SLICE
        if k == 0:
            if j == 2:
                return (own2g, own2u)[part][...]
            return {0: own, 1: own1, 3: own3}[j][pl.ds(begin, SLICE), :]
        if j == 2:
            if begin < 3 * SLICE:
                return rest2a[pl.ds(begin, SLICE), :]
            return rest2b[pl.ds(begin - 3 * SLICE, SLICE), :]
        return {0: rest, 1: rest1, 3: rest3}[j][pl.ds(begin, SLICE), :]

    for k in range(4):
        for j in range(4):
            place_k = (k * 4 + j) * SLICE
            rows = pl.ds(place_k, SLICE)
            w[rows, 0:COLS] = piece(k, j, 0)
            w[rows, COLS : 2 * COLS] = piece(k, j, 1)
            source = lax.rem(yh + k, 4) * 4 + lax.rem(x + j, 4)
            w[rows, 2 * COLS : WIDE] = down[pl.ds(pl.multiple_of((source * 2 + core) * SLICE, SLICE), SLICE), :]
            columns = pl.ds(pl.multiple_of(source * SLICE, SLICE), SLICE)
            for z in range(8):
                lines = pl.ds(z * 48, 48)
                near_x[lines, place_k : place_k + SLICE] = tok[z, core, :, columns]
                far_x[lines, place_k : place_k + SLICE] = tok[z, 1 - core, :, columns]
    for z in range(8):
        near_code[pl.ds(z * 48, 48), :] = tok[z, core, :, HALF : HALF + LANES]
    for n in range(3):
        part = slice(n * GROUP, (n + 1) * GROUP)
        far[:, part] = jnp.dot(far_x[...], w[:, part], preferred_element_type=F32)
    far[:, 2 * COLS : WIDE] = far[:, 2 * COLS : WIDE] + count[...]


def on_device(tokens, sequence_labels, response_mask, frozen, down, up, readout):
    s, t, x, core = (lax.axis_index(a) for a in ("s", "t", "x", "c"))
    code = jnp.where(response_mask > 0, sequence_labels, SEQS)

    by_core = tokens.reshape(ROWS, WIDTH // (2 * SLICE), 2, SLICE).transpose(2, 0, 1, 3)
    code_lanes = jnp.pad(code.reshape(ROWS, 1).astype(BF16), ((0, 0), (0, LANES - 1)))
    message = jnp.concatenate(
        [by_core.reshape(2, ROWS, HALF), jnp.broadcast_to(code_lanes[None], (2, ROWS, LANES))], axis=2
    )
    message = jnp.broadcast_to(message[:, None], (2, 4, ROWS, HALF + LANES))
    eight = lax.all_to_all(
        message.reshape(8, ROWS, HALF + LANES), ("c", "t", "yl"), split_axis=0, concat_axis=0
    )
    eight, frozen, sequence_labels = lax.optimization_barrier((eight, frozen, sequence_labels))
    tok = lax.all_gather(eight.reshape(8 * ROWS, HALF + LANES), "z", axis=0, tiled=True)
    tok = tok.reshape(8, 2, 4 * ROWS, HALF + LANES)

    has = [jnp.max((code == q).astype(F32)) for q in range(SEQS)]
    count = has[0] * has[1] + has[2] * has[3]

    low_half, high_half = frozen[:, :, :COLS], frozen[:, :, SKIP:]
    mine = jnp.where(t == 0, low_half, high_half).reshape(2 * SLICE, COLS)
    other = jnp.where(t == 0, high_half, low_half).reshape(2 * SLICE, COLS)
    count_rows = jnp.broadcast_to(count.astype(BF16), (16, COLS))
    y1 = fetch(other, YH, 4, 1)
    y3 = fetch(other, YH, 4, 3)
    y2 = fetch(jnp.concatenate([mine, count_rows], axis=0), YH, 4, 2)
    own1 = fetch(mine, "x", 4, 1)
    own3 = fetch(mine, "x", 4, 3)
    own2g = fetch(own3[:SLICE], "x", 4, 3)
    own2u = fetch(own1[SLICE:], "x", 4, 1)
    pair_rows = y2[2 * SLICE :] + count_rows
    rest = jnp.concatenate([y1, y3, y2[: 2 * SLICE], pair_rows], axis=0)
    rest1 = fetch(rest, "x", 4, 1)
    rest3 = fetch(rest, "x", 4, 3)
    rest2a = fetch(rest3[: 3 * SLICE], "x", 4, 3)
    rest2b = fetch(rest1[3 * SLICE :], "x", 4, 1)
    count = sum(p[-1, 0].astype(F32) for p in (rest, rest1, rest3, rest2b))
    count_lanes = jnp.where(jnp.arange(LANES) == 2 * RANK, count, 0.0).reshape(1, LANES)

    vmem = pl.BlockSpec(memory_space=pltpu.VMEM)
    smem = pl.BlockSpec(memory_space=pltpu.SMEM)
    far, near_x, near_code, w = pl.pallas_call(
        products,
        out_shape=(
            jax.ShapeDtypeStruct((GROUP, WIDE), F32),
            jax.ShapeDtypeStruct((GROUP, HALF), BF16),
            jax.ShapeDtypeStruct((GROUP, LANES), BF16),
            jax.ShapeDtypeStruct((HALF, WIDE), BF16),
        ),
        in_specs=[smem] + [vmem] * 13,
        out_specs=(vmem,) * 4,
        scratch_shapes=[pltpu.VMEM((GROUP, HALF), BF16)],
        compiler_params=pltpu.CompilerParams(vmem_limit_bytes=40 * 1024 * 1024),
        cost_estimate=pl.CostEstimate(flops=2 * GROUP * HALF * WIDE, bytes_accessed=20_000_000, transcendentals=0),
    )(
        jnp.stack([2 * s + t, x, core]).astype(jnp.int32), tok, mine, own1, own3, own2g, own2u,
        rest, rest1, rest3, rest2a, rest2b, jnp.pad(down, ((0, 0), (0, LANES - 2 * RANK))), count_lanes,
    )
    from_partner = lax.ppermute(far, "c", SWAP)
    both = jnp.dot(near_x, w, preferred_element_type=F32) + from_partner
    gate_ref, up_ref = both[:, :COLS], both[:, COLS : 2 * COLS]
    low = both[:, 2 * COLS : 2 * COLS + 2 * RANK].astype(BF16)
    count = count + from_partner[0, 2 * COLS + 2 * RANK]

    units = jnp.where(t == 0, up[:, :COLS], up[:, SKIP:])
    b_gate, b_up = units[:RANK], units[RANK:]
    shared = jnp.where(jnp.arange(COLS) < 2 * COLS - readout.shape[0], 0.0, 1.0)
    readout_f = jnp.where(t == 0, readout[:COLS].astype(F32), readout[SKIP:].astype(F32) * shared)
    gate_pol = gate_ref + jnp.dot(low[:, :RANK], b_gate, preferred_element_type=F32)
    up_pol = up_ref + jnp.dot(low[:, RANK:], b_up, preferred_element_type=F32)
    sig_ref = jax.nn.sigmoid(gate_ref)
    sig_pol = jax.nn.sigmoid(gate_pol)
    act_pol = gate_pol * sig_pol
    change = jnp.sum((act_pol * up_pol - gate_ref * sig_ref * up_ref) * readout_f, axis=1)
    k_gate = readout_f * sig_pol * (1.0 + gate_pol * (1.0 - sig_pol)) * up_pol
    k_up = readout_f * act_pol
    contract_last = (((1,), (1,)), ((), ()))
    mixed = jnp.concatenate(
        [
            lax.dot_general(b_gate.astype(F32), k_gate, contract_last, precision=HIGHEST),
            lax.dot_general(b_up.astype(F32), k_up, contract_last, precision=HIGHEST),
        ],
        axis=0,
    )

    codes = near_code[:, 0].astype(jnp.int32).reshape(BLOCKS, ROWS)
    pairs = jnp.arange(SEQS // 2, dtype=jnp.int32)
    chosen = (codes[:, :, None] == 2 * pairs).astype(F32)
    rejected = (codes[:, :, None] == 2 * pairs + 1).astype(F32)
    signs = chosen - rejected
    valid = (jnp.max(chosen, axis=1) * jnp.max(rejected, axis=1)).reshape(-1)
    gap_part = jnp.sum(signs * change.reshape(BLOCKS, ROWS, 1), axis=1).reshape(-1)

    for_all = jnp.concatenate([gap_part, count[None], jnp.zeros((63,), F32)])
    arrived = lax.all_to_all(
        jnp.concatenate([mixed, jnp.broadcast_to(for_all[None], (32, LANES))], axis=1),
        ("t", "z", "yl"), split_axis=0, concat_axis=0, tiled=True,
    )
    total = jnp.sum(arrived, axis=0)
    pair_total = jnp.maximum(total[GROUP + 64], 1.0)
    logit = DPO_BETA * total[GROUP : GROUP + 64]
    log_sum = jnp.sum(valid * jax.nn.log_sigmoid(logit))
    scaled = -LOSS_SCALE * DPO_BETA * valid * jax.nn.sigmoid(-logit) / pair_total
    cotangent = jnp.sum(signs * scaled.reshape(BLOCKS, 1, -1), axis=2).reshape(-1)

    projected = (total[:GROUP] * cotangent).astype(BF16)[None]
    partner_projected = lax.ppermute(projected, "c", SWAP)
    weighted = low.astype(F32) * cotangent[:, None]
    contract_first = (((0,), (0,)), ((), ()))
    grad_b_part = jnp.concatenate(
        [
            lax.dot_general(weighted[:, :RANK], k_gate, contract_first, precision=HIGHEST),
            lax.dot_general(weighted[:, RANK:], k_up, contract_first, precision=HIGHEST),
        ],
        axis=0,
    )
    first = jnp.where(core == 0, projected, partner_projected).reshape(1, 8, 1, 48)
    second = jnp.where(core == 0, partner_projected, projected).reshape(1, 8, 1, 48)
    all_projected = jnp.concatenate([first, second], axis=2).reshape(1, 2 * GROUP)
    grad_a_part = jnp.dot(
        all_projected, tok.reshape(2 * GROUP, -1)[:, :HALF], preferred_element_type=F32
    )

    mine_a = jnp.where(jnp.arange(2) == core, 1.0, 0.0).reshape(1, 2, 1)
    slices = (grad_a_part.reshape(16, 1, SLICE) * mine_a).reshape(32, SLICE)
    outgoing = jnp.concatenate(
        [grad_b_part, slices, jnp.broadcast_to(log_sum, (32, LANES))], axis=1
    )
    arrived = lax.all_to_all(outgoing, DP, split_axis=0, concat_axis=0, tiled=True)
    summed = jnp.sum(arrived.reshape(2, 2, 8, -1), axis=(0, 2))
    spare = readout.shape[0] - COLS
    grad_b = jnp.pad(summed[0, :COLS], (0, spare)) + jnp.pad(summed[1, :COLS], (spare, 0))
    columns = summed[:, COLS : COLS + SLICE]
    log_total = summed[0, COLS + SLICE]
    grad_a = lax.all_to_all(
        jnp.broadcast_to(columns[None], (16, 2, SLICE)), BLK, split_axis=0, concat_axis=0
    )
    grad_a = grad_a.transpose(2, 1, 0).reshape(SLICE, 2 * RANK)
    return -log_total / pair_total, grad_a, grad_b[None]


def solution(mesh):
    fine = Mesh(mesh.devices.reshape(SIZES), AXES)
    in_specs = (
        P(AXES, None),
        P(AXES, None),
        P(AXES, None),
        P(None, DP, BLK),
        P(),
        P(None, BLK),
        P(BLK),
    )
    out_specs = (P(), P(DP, None), P(DP, BLK))
    return jax.shard_map(
        on_device, mesh=fine, in_specs=in_specs, out_specs=out_specs, check_vma=False
    )
```

```python
import functools

import jax
import jax.numpy as jnp
from jax import lax
from jax.experimental import pallas as pl
from jax.experimental.pallas import tpu as pltpu
from jax.sharding import Mesh, PartitionSpec as P

SEQS = 4
ROWS = 12
RANK = 16
WIDTH = 4096
DPO_BETA = 0.1
LOSS_SCALE = 1024.0
F32 = jnp.float32
BF16 = jnp.bfloat16

AXES = ("s", "t", "x", "c", "z", "yl")
SIZES = (2, 2, 4, 2, 8, 2)
DP = ("s", "t", "x", "c")
BLK = ("z", "yl")
YH = ("s", "t")
SWAP = [(0, 1), (1, 0)]

SLICE = 128
HALF = WIDTH // 2
LANES = 128
COLS = 512
SKIP = 384
GROUP = 384
BLOCKS = GROUP // ROWS
WIDE = 2 * COLS + LANES
CONTRACT_LAST = (((1,), (1,)), ((), ()))


def fetch(value, axes, size, k):
    return lax.ppermute(value, axes, [((i + k) % size, i) for i in range(size)])


def swapped(value, axis, index):
    far = lax.ppermute(value, axis, SWAP)
    return jnp.where(index == 0, jnp.stack([value, far]), jnp.stack([far, value]))


def split(value, terms):
    parts = []
    for _ in range(terms):
        parts.append(value.astype(BF16))
        value = value - parts[-1].astype(F32)
    return parts


def dot(a, b, dims=(((1,), (0,)), ((), ()))):
    return lax.dot_general(a, b, dims, preferred_element_type=F32)


def source_of(place, k, j):
    return lax.rem(place[0] + k, 4) * 4 + lax.rem(place[1] + j, 4)


def down_rows(down, place, source):
    return down[pl.ds(pl.multiple_of((source * 2 + place[2]) * SLICE, SLICE), SLICE), :]


def columns_of(source):
    return pl.ds(pl.multiple_of(source * SLICE, SLICE), SLICE)


def early_products(place, tok, own, own1, own3, own2g, own2u, rest, rest1, rest3, down, acc, w, lined):
    pieces = []
    for j, ref in ((0, own), (1, own1), (3, own3)):
        pieces.append((0, j, ref[0:SLICE, :], ref[SLICE : 2 * SLICE, :]))
    pieces.append((0, 2, own2g[...], own2u[...]))
    for j, ref in ((0, rest), (1, rest1), (3, rest3)):
        for at, k in enumerate((1, 3, 2)):
            begin = 2 * at * SLICE
            pieces.append((k, j, ref[begin : begin + SLICE, :], ref[begin + SLICE : begin + 2 * SLICE, :]))
    for at, (k, j, gate, up) in enumerate(pieces):
        source = source_of(place, k, j)
        w[at * SLICE : (at + 1) * SLICE, 0:COLS] = gate
        w[at * SLICE : (at + 1) * SLICE, COLS : 2 * COLS] = up
        w[at * SLICE : (at + 1) * SLICE, 2 * COLS : WIDE] = down_rows(down, place, source)
        lined[:, at * SLICE : (at + 1) * SLICE] = tok[:, columns_of(source)]
    for n in range(3):
        part = slice(n * GROUP, (n + 1) * GROUP)
        acc[:, part] = dot(lined[...], w[:, part])


def late_products(far, place, tok, acc, rest2a, rest2b, down, out, w, lined):
    core = place[2]
    half = 1 - core if far else core
    rows = pl.ds(pl.multiple_of(half * GROUP, GROUP), GROUP)
    pieces = (
        (1, rest2a[0:SLICE, :], rest2a[SLICE : 2 * SLICE, :]),
        (3, rest2a[2 * SLICE : 3 * SLICE, :], rest2b[0:SLICE, :]),
        (2, rest2b[SLICE : 2 * SLICE, :], rest2b[2 * SLICE : 3 * SLICE, :]),
    )
    for at, (k, gate, up) in enumerate(pieces):
        source = source_of(place, k, 2)
        w[at * SLICE : (at + 1) * SLICE, 0:COLS] = gate
        w[at * SLICE : (at + 1) * SLICE, COLS : 2 * COLS] = up
        w[at * SLICE : (at + 1) * SLICE, 2 * COLS : WIDE] = down_rows(down, place, source)
        lined[:, at * SLICE : (at + 1) * SLICE] = tok[rows, columns_of(source)]
    for n in range(3):
        part = slice(n * GROUP, (n + 1) * GROUP)
        out[:, part] = acc[rows, part] + dot(lined[...], w[:, part])


def score(place, near, partner, b_gate, b_up, readout, signs, count, message, gate_high, gate_low, up_high,
          up_low, low_t):
    low = near[:, 2 * COLS : WIDE] + partner[:, 2 * COLS : WIDE]
    low_b = low.astype(BF16)
    gate_ref = near[:, 0:COLS] + partner[:, 0:COLS]
    up_ref = near[:, COLS : 2 * COLS] + partner[:, COLS : 2 * COLS]
    gate_pol = gate_ref + dot(low_b, b_gate[...])
    up_pol = up_ref + dot(low_b, b_up[...])
    sig_ref = jax.nn.sigmoid(gate_ref)
    sig_pol = jax.nn.sigmoid(gate_pol)
    act_pol = gate_pol * sig_pol
    read = readout[...].astype(F32)
    change = act_pol * up_pol - gate_ref * sig_ref * up_ref
    k_gate = read * sig_pol * (1.0 + gate_pol * (1.0 - sig_pol)) * up_pol
    k_up = read * act_pol
    read_b = jnp.broadcast_to(readout[...], (8, COLS))
    change_row = sum(dot(read_b, part, CONTRACT_LAST) for part in split(change, 3))
    sign = signs[place[2]]
    gaps = sum(dot(part, sign, CONTRACT_LAST) for part in split(change_row, 3))
    message[:, GROUP : GROUP + LANES] = jnp.broadcast_to(gaps[0:1, :] + count[...], (2 * RANK, LANES))
    high, rest = split(k_gate, 2)
    gate_high[...], gate_low[...] = high, rest
    mixed = dot(b_gate[0 : 2 * RANK, :], high, CONTRACT_LAST) + dot(b_gate[0 : 2 * RANK, :], rest, CONTRACT_LAST)
    high, rest = split(k_up, 2)
    up_high[...], up_low[...] = high, rest
    mixed_up = dot(b_up[0 : 2 * RANK, :], high, CONTRACT_LAST) + dot(b_up[0 : 2 * RANK, :], rest, CONTRACT_LAST)
    message[:, 0:GROUP] = mixed + mixed_up
    low_t[...] = low_b.astype(F32).T[0 : 2 * RANK, :]


def close(place, arrived, signs, valid, low_t, gate_high, gate_low, up_high, up_low, tok, out, total_out):
    core = place[2]
    totals = [jnp.sum(arrived[h], axis=0, keepdims=True) for h in range(2)]
    tails = [total[:, GROUP : GROUP + LANES] for total in totals]
    pair_total = jnp.maximum(tails[0][:, 64:65] + tails[1][:, 64:65], 1.0)
    logs, cotangents, terms = 0.0, [], []
    for h in range(2):
        logit = DPO_BETA * tails[h]
        logs = logs + jnp.sum(
            valid[h] * (jnp.minimum(logit, 0.0) - jnp.log1p(jnp.exp(-jnp.abs(logit)))), axis=1, keepdims=True
        )
        scaled = -LOSS_SCALE * DPO_BETA * valid[h] * jax.nn.sigmoid(-logit) / pair_total
        scaled = jnp.broadcast_to(scaled, (8, LANES))
        cotangent = sum(dot(part, signs[h]) for part in split(scaled, 3))
        cotangents.append(cotangent[0:1, :])
        projected = jnp.broadcast_to(totals[h][:, 0:GROUP], (8, GROUP)) * cotangent
        terms.append(dot(projected.astype(BF16), tok[h * GROUP : (h + 1) * GROUP, 0:HALF]))
    grad_a = (terms[0] + terms[1])[0:1, :]
    own = jnp.where(core == 0, cotangents[0], cotangents[1])
    high, rest = split(low_t[...] * own, 2)
    gate = dot(high[0:RANK], gate_high[...]) + dot(high[0:RANK], gate_low[...]) + dot(rest[0:RANK], gate_high[...])
    up = dot(high[RANK:], up_high[...]) + dot(high[RANK:], up_low[...]) + dot(rest[RANK:], up_high[...])
    out[0:RANK, 0:COLS] = gate
    out[RANK : 2 * RANK, 0:COLS] = up
    line = lax.broadcasted_iota(jnp.int32, (2 * RANK, SLICE), 0)
    slices = jnp.zeros((2 * RANK, SLICE), F32)
    for i in range(RANK):
        here = jnp.broadcast_to(grad_a[:, i * SLICE : (i + 1) * SLICE], (2 * RANK, SLICE))
        slices = jnp.where(line == 2 * i + core, here, slices)
    out[:, COLS : COLS + SLICE] = slices
    out[:, COLS + SLICE :] = jnp.broadcast_to(0.5 * logs, (2 * RANK, LANES))
    total_out[...] = jnp.broadcast_to(pair_total, (8, LANES))


def kernel(function, shapes, scratch, arguments, flops):
    vmem = pl.BlockSpec(memory_space=pltpu.VMEM)
    smem = pl.BlockSpec(memory_space=pltpu.SMEM)
    return pl.pallas_call(
        function,
        out_shape=tuple(jax.ShapeDtypeStruct(*s) for s in shapes),
        in_specs=[smem] + [vmem] * (len(arguments) - 1),
        out_specs=(vmem,) * len(shapes),
        scratch_shapes=[pltpu.VMEM(*s) for s in scratch],
        compiler_params=pltpu.CompilerParams(vmem_limit_bytes=48 * 1024 * 1024),
        cost_estimate=pl.CostEstimate(flops=flops, bytes_accessed=10_000_000, transcendentals=0),
    )(*arguments)


def on_device(tokens, sequence_labels, response_mask, frozen, down, up, readout):
    s, t, x, core, yl = (lax.axis_index(a) for a in ("s", "t", "x", "c", "yl"))
    code = jnp.where(response_mask > 0, sequence_labels, SEQS)

    by_core = tokens.reshape(ROWS, WIDTH // (2 * SLICE), 2, SLICE).transpose(2, 0, 1, 3).reshape(2, ROWS, HALF)
    code_lanes = jnp.pad(code.reshape(ROWS, 1).astype(BF16), ((0, 0), (0, LANES - 1)))
    keep = jnp.concatenate([jnp.where(core == 0, by_core[0], by_core[1]), code_lanes], axis=1)
    give = jnp.concatenate([jnp.where(core == 0, by_core[1], by_core[0]), code_lanes], axis=1)
    take = lax.ppermute(give, "c", SWAP)
    pair = jnp.where(
        core == 0, jnp.concatenate([keep, take], axis=0), jnp.concatenate([take, keep], axis=0)
    )
    eight = swapped(swapped(pair, "yl", yl), "t", t)
    tok = lax.all_gather(eight.reshape(8 * ROWS, HALF + LANES), "z", axis=0, tiled=True)

    has = [jnp.max((code == q).astype(F32)) for q in range(SEQS)]
    count = has[0] * has[1] + has[2] * has[3]

    low_half, high_half = frozen[:, :, :COLS], frozen[:, :, SKIP:]
    mine = jnp.where(t == 0, low_half, high_half).reshape(2 * SLICE, COLS)
    other = jnp.where(t == 0, high_half, low_half).reshape(2 * SLICE, COLS)
    count_rows = jnp.broadcast_to(count.astype(BF16), (16, COLS))
    y1 = fetch(other, YH, 4, 1)
    y3 = fetch(other, YH, 4, 3)
    y2 = fetch(jnp.concatenate([mine, count_rows], axis=0), YH, 4, 2)
    own1 = fetch(mine, "x", 4, 1)
    own3 = fetch(mine, "x", 4, 3)
    y1, y2, y3, own1, own3 = lax.optimization_barrier((y1, y2, y3, own1, own3))
    rest = jnp.concatenate([y1, y3, y2[: 2 * SLICE], y2[2 * SLICE :] + count_rows], axis=0)
    rest1 = fetch(rest, "x", 4, 1)
    rest3 = fetch(rest, "x", 4, 3)
    own2g = fetch(own3[:SLICE], "x", 4, 3)
    own2u = fetch(own1[SLICE:], "x", 4, 1)
    rest2a = fetch(rest3[: 3 * SLICE], "x", 4, 3)
    rest2b = fetch(rest1[3 * SLICE :], "x", 4, 1)
    count = sum(p[-1, 0].astype(F32) for p in (rest, rest1, rest3, rest2b))
    count_lanes = jnp.where(jnp.arange(LANES) == 64, count, 0.0).reshape(1, LANES)

    place = jnp.stack([2 * s + t, x, core]).astype(jnp.int32)
    down_wide = jnp.pad(down, ((0, 0), (0, LANES - 2 * RANK)))
    (acc,) = kernel(
        early_products,
        [((2 * GROUP, WIDE), F32)],
        [((13 * SLICE, WIDE), BF16), ((2 * GROUP, 13 * SLICE), BF16)],
        (place, tok, mine, own1, own3, own2g, own2u, rest, rest1, rest3, down_wide),
        4 * GROUP * 13 * SLICE * WIDE,
    )
    late = [((3 * SLICE, WIDE), BF16), ((GROUP, 3 * SLICE), BF16)]
    late_in = (place, tok, acc, rest2a, rest2b, down_wide)
    late_flops = 2 * GROUP * 3 * SLICE * WIDE
    (far,) = kernel(functools.partial(late_products, True), [((GROUP, WIDE), F32)], late, late_in, late_flops)
    partner = lax.ppermute(far, "c", SWAP)
    (near,) = kernel(functools.partial(late_products, False), [((GROUP, WIDE), F32)], late, late_in, late_flops)

    units = jnp.where(t == 0, up[:, :COLS], up[:, SKIP:])
    b_gate = jnp.pad(units[:RANK], ((0, LANES - RANK), (0, 0)))
    b_up = jnp.pad(units[RANK:], ((RANK, LANES - 2 * RANK), (0, 0)))
    shared = (jnp.arange(COLS) >= 2 * COLS - readout.shape[0]).astype(BF16)
    read = jnp.where(t == 0, readout[:COLS], readout[SKIP:] * shared).reshape(1, COLS)

    codes = tok[:, HALF].astype(jnp.int32).reshape(2, GROUP)
    pair_of = jnp.arange(LANES, dtype=jnp.int32)
    block_of = jnp.arange(GROUP, dtype=jnp.int32) // ROWS
    inside = (pair_of[:, None] // 2 == block_of[None, :])[None]
    chosen = inside & (codes[:, None, :] == 2 * (pair_of % 2)[None, :, None])
    rejected = inside & (codes[:, None, :] == 2 * (pair_of % 2)[None, :, None] + 1)
    signs = chosen.astype(BF16) - rejected.astype(BF16)
    valid = (jnp.any(chosen, axis=2) & jnp.any(rejected, axis=2)).astype(F32).reshape(2, 1, LANES)

    message, gate_high, gate_low, up_high, up_low, low_t = kernel(
        score,
        [((2 * RANK, GROUP + LANES), F32)] + [((GROUP, COLS), BF16)] * 4 + [((2 * RANK, GROUP), F32)],
        [],
        (place, near, partner, b_gate, b_up, read, signs, count_lanes),
        8 * GROUP * COLS * LANES,
    )
    arrived = lax.all_to_all(
        jnp.broadcast_to(message[None], (2, 2 * RANK, GROUP + LANES)).reshape(4 * RANK, -1),
        ("c", "t", "z", "yl"), split_axis=0, concat_axis=0, tiled=True,
    ).reshape(2, 2 * RANK, -1)
    outgoing, pair_total = kernel(
        close,
        [((2 * RANK, COLS + SLICE + LANES), F32), ((8, LANES), F32)],
        [],
        (place, arrived, signs, valid, low_t, gate_high, gate_low, up_high, up_low, tok),
        16 * GROUP * HALF * 2,
    )

    arrived = lax.all_to_all(outgoing, DP, split_axis=0, concat_axis=0, tiled=True)
    summed = jnp.sum(arrived.reshape(2, 2, 8, -1), axis=(0, 2))
    spare = readout.shape[0] - COLS
    grad_b = jnp.pad(summed[0, :COLS], (0, spare)) + jnp.pad(summed[1, :COLS], (spare, 0))
    columns = summed[:, COLS : COLS + SLICE]
    log_total = summed[0, COLS + SLICE]
    grad_a = lax.all_to_all(
        jnp.broadcast_to(columns[None], (16, 2, SLICE)), BLK, split_axis=0, concat_axis=0
    )
    grad_a = grad_a.transpose(2, 1, 0).reshape(SLICE, 2 * RANK)
    return -log_total / pair_total[0, 0], grad_a, grad_b[None]


def solution(mesh):
    fine = Mesh(mesh.devices.reshape(SIZES), AXES)
    in_specs = (
        P(AXES, None),
        P(AXES, None),
        P(AXES, None),
        P(None, DP, BLK),
        P(),
        P(None, BLK),
        P(BLK),
    )
    out_specs = (P(), P(DP, None), P(DP, BLK))
    return jax.shard_map(
        on_device, mesh=fine, in_specs=in_specs, out_specs=out_specs, check_vma=False
    )
```

```python
import functools

import jax
import jax.numpy as jnp
from jax import lax
from jax.experimental import pallas as pl
from jax.experimental.pallas import tpu as pltpu
from jax.sharding import Mesh, PartitionSpec as P

SEQS = 4
ROWS = 12
RANK = 16
WIDTH = 4096
DPO_BETA = 0.1
LOSS_SCALE = 1024.0
F32 = jnp.float32
BF16 = jnp.bfloat16

AXES = ("s", "t", "x", "c", "z", "yl")
SIZES = (2, 2, 4, 2, 8, 2)
DP = ("s", "t", "x", "c")
BLK = ("z", "yl")
YH = ("s", "t")
SWAP = [(0, 1), (1, 0)]

SLICE = 128
HALF = WIDTH // 2
LANES = 128
COLS = 512
SKIP = 384
GROUP = 384
BLOCKS = GROUP // ROWS
WIDE = 2 * COLS + LANES
CONTRACT_LAST = (((1,), (1,)), ((), ()))


def fetch(value, axes, size, k):
    return lax.ppermute(value, axes, [((i + k) % size, i) for i in range(size)])


def swapped(value, axis, index):
    far = lax.ppermute(value, axis, SWAP)
    return jnp.where(index == 0, jnp.stack([value, far]), jnp.stack([far, value]))


def split(value, terms):
    parts = []
    for _ in range(terms):
        parts.append(value.astype(BF16))
        value = value - parts[-1].astype(F32)
    return parts


def dot(a, b, dims=(((1,), (0,)), ((), ()))):
    return lax.dot_general(a, b, dims, preferred_element_type=F32)


def assemble(place, own, own1, own3, own2g, own2u, rest, rest1, rest3, rest2a, rest2b, w):
    pieces = []
    for j, ref in ((0, own), (1, own1), (3, own3)):
        pieces.append((0, j, ref[0:SLICE, :], ref[SLICE : 2 * SLICE, :]))
    pieces.append((0, 2, own2g[...], own2u[...]))
    for j, ref in ((0, rest), (1, rest1), (3, rest3)):
        for at, k in enumerate((1, 3, 2)):
            begin = 2 * at * SLICE
            pieces.append((k, j, ref[begin : begin + SLICE, :], ref[begin + SLICE : begin + 2 * SLICE, :]))
    pieces.append((1, 2, rest2a[0:SLICE, :], rest2a[SLICE : 2 * SLICE, :]))
    pieces.append((3, 2, rest2a[2 * SLICE : 3 * SLICE, :], rest2b[0:SLICE, :]))
    pieces.append((2, 2, rest2b[SLICE : 2 * SLICE, :], rest2b[2 * SLICE : 3 * SLICE, :]))
    for k, j, gate, up in pieces:
        source = lax.rem(place[0] + k, 4) * 4 + lax.rem(place[1] + j, 4)
        rows = pl.ds(pl.multiple_of(source * SLICE, SLICE), SLICE)
        w[rows, 0:COLS] = gate
        w[rows, COLS : 2 * COLS] = up


def products(far, place, tok, w, down, out):
    half = 1 - place[2] if far else place[2]
    rows = pl.ds(pl.multiple_of(half * GROUP, GROUP), GROUP)
    for n in range(4):
        part = slice(n * COLS // 2, (n + 1) * COLS // 2)
        out[:, part] = dot(tok[rows, 0:HALF], w[:, part])
    out[:, 2 * COLS : WIDE] = dot(tok[rows, 0:HALF], down[...])


def score(place, near, partner, b_gate, b_up, readout, signs, count, message, gate_high, gate_low, up_high,
          up_low, low_t):
    low = near[:, 2 * COLS : WIDE] + partner[:, 2 * COLS : WIDE]
    low_b = low.astype(BF16)
    gate_ref = near[:, 0:COLS] + partner[:, 0:COLS]
    up_ref = near[:, COLS : 2 * COLS] + partner[:, COLS : 2 * COLS]
    gate_pol = gate_ref + dot(low_b, b_gate[...])
    up_pol = up_ref + dot(low_b, b_up[...])
    sig_ref = jax.nn.sigmoid(gate_ref)
    sig_pol = jax.nn.sigmoid(gate_pol)
    act_pol = gate_pol * sig_pol
    read = readout[...].astype(F32)
    change = act_pol * up_pol - gate_ref * sig_ref * up_ref
    k_gate = read * sig_pol * (1.0 + gate_pol * (1.0 - sig_pol)) * up_pol
    k_up = read * act_pol
    read_b = jnp.broadcast_to(readout[...], (8, COLS))
    change_row = sum(dot(read_b, part, CONTRACT_LAST) for part in split(change, 3))
    sign = signs[place[2]]
    gaps = sum(dot(part, sign, CONTRACT_LAST) for part in split(change_row, 3))
    tail = jnp.broadcast_to(gaps[0:1, :] + count[...], (2 * RANK, LANES))
    high, rest = split(k_gate, 2)
    gate_high[...], gate_low[...] = high, rest
    mixed = dot(b_gate[0 : 2 * RANK, :], high, CONTRACT_LAST) + dot(b_gate[0 : 2 * RANK, :], rest, CONTRACT_LAST)
    high, rest = split(k_up, 2)
    up_high[...], up_low[...] = high, rest
    mixed_up = dot(b_up[0 : 2 * RANK, :], high, CONTRACT_LAST) + dot(b_up[0 : 2 * RANK, :], rest, CONTRACT_LAST)
    mixed = mixed + mixed_up
    for core in range(2):
        lines = slice(2 * RANK * core, 2 * RANK * (core + 1))
        for i in range(3):
            message[lines, i, :] = mixed[:, i * LANES : (i + 1) * LANES]
        message[lines, 3, :] = tail
    low_t[...] = low_b.astype(F32).T[0 : 2 * RANK, :]


def close(place, arrived, signs, valid, low_t, gate_high, gate_low, up_high, up_low, tok, out, total_out):
    core = place[2]
    sums = [jnp.sum(arrived[2 * RANK * h : 2 * RANK * (h + 1)], axis=0) for h in range(2)]
    totals = [jnp.concatenate([total[i : i + 1, :] for i in range(3)], axis=1) for total in sums]
    tails = [total[3:4, :] for total in sums]
    pair_total = jnp.maximum(tails[0][:, 64:65] + tails[1][:, 64:65], 1.0)
    logs, cotangents, terms = 0.0, [], []
    for h in range(2):
        logit = DPO_BETA * tails[h]
        logs = logs + jnp.sum(
            valid[h] * (jnp.minimum(logit, 0.0) - jnp.log1p(jnp.exp(-jnp.abs(logit)))), axis=1, keepdims=True
        )
        scaled = -LOSS_SCALE * DPO_BETA * valid[h] * jax.nn.sigmoid(-logit) / pair_total
        scaled = jnp.broadcast_to(scaled, (8, LANES))
        cotangent = sum(dot(part, signs[h]) for part in split(scaled, 3))
        cotangents.append(cotangent[0:1, :])
        projected = jnp.broadcast_to(totals[h], (8, GROUP)) * cotangent
        terms.append(dot(projected.astype(BF16), tok[h * GROUP : (h + 1) * GROUP, 0:HALF]))
    grad_a = (terms[0] + terms[1])[0:1, :]
    own = jnp.where(core == 0, cotangents[0], cotangents[1])
    high, rest = split(low_t[...] * own, 2)
    gate = dot(high[0:RANK], gate_high[...]) + dot(high[0:RANK], gate_low[...]) + dot(rest[0:RANK], gate_high[...])
    up = dot(high[RANK:], up_high[...]) + dot(high[RANK:], up_low[...]) + dot(rest[RANK:], up_high[...])
    for i in range(4):
        out[0:RANK, i, :] = gate[:, i * LANES : (i + 1) * LANES]
        out[RANK : 2 * RANK, i, :] = up[:, i * LANES : (i + 1) * LANES]
    line = lax.broadcasted_iota(jnp.int32, (2 * RANK, SLICE), 0)
    slices = jnp.zeros((2 * RANK, SLICE), F32)
    for i in range(RANK):
        here = jnp.broadcast_to(grad_a[:, i * SLICE : (i + 1) * SLICE], (2 * RANK, SLICE))
        slices = jnp.where(line == 2 * i + core, here, slices)
    out[:, 4, :] = slices
    out[:, 5, :] = jnp.broadcast_to(0.5 * logs, (2 * RANK, LANES))
    total_out[...] = jnp.broadcast_to(pair_total, (8, LANES))


def kernel(function, shapes, arguments, flops, grant):
    vmem = pl.BlockSpec(memory_space=pltpu.VMEM)
    smem = pl.BlockSpec(memory_space=pltpu.SMEM)
    return pl.pallas_call(
        function,
        out_shape=tuple(jax.ShapeDtypeStruct(*s) for s in shapes),
        in_specs=[smem] + [vmem] * (len(arguments) - 1),
        out_specs=(vmem,) * len(shapes),
        compiler_params=pltpu.CompilerParams(vmem_limit_bytes=grant * 1024 * 1024),
        cost_estimate=pl.CostEstimate(flops=flops, bytes_accessed=10_000_000, transcendentals=0),
    )(*arguments)


def on_device(tokens, sequence_labels, response_mask, frozen, down, up, readout):
    s, t, x, core, yl = (lax.axis_index(a) for a in ("s", "t", "x", "c", "yl"))
    code = jnp.where(response_mask > 0, sequence_labels, SEQS)

    by_core = tokens.reshape(ROWS, WIDTH // (2 * SLICE), 2, SLICE).transpose(2, 0, 1, 3).reshape(2, ROWS, HALF)
    code_lanes = jnp.pad(code.reshape(ROWS, 1).astype(BF16), ((0, 0), (0, LANES - 1)))
    keep = jnp.concatenate([jnp.where(core == 0, by_core[0], by_core[1]), code_lanes], axis=1)
    give = jnp.concatenate([jnp.where(core == 0, by_core[1], by_core[0]), code_lanes], axis=1)
    take = lax.ppermute(give, "c", SWAP)
    pair = jnp.where(
        core == 0, jnp.concatenate([keep, take], axis=0), jnp.concatenate([take, keep], axis=0)
    )
    eight = swapped(swapped(pair, "yl", yl), "t", t)
    has = [jnp.max((code == q).astype(F32)) for q in range(SEQS)]
    count = has[0] * has[1] + has[2] * has[3]

    low_half, high_half = frozen[:, :, :COLS], frozen[:, :, SKIP:]
    mine = jnp.where(t == 0, low_half, high_half).reshape(2 * SLICE, COLS)
    other = jnp.where(t == 0, high_half, low_half).reshape(2 * SLICE, COLS)
    count_rows = jnp.broadcast_to(count.astype(BF16), (16, COLS))
    y1 = fetch(other, YH, 4, 1)
    y3 = fetch(other, YH, 4, 3)
    y2 = fetch(jnp.concatenate([mine, count_rows], axis=0), YH, 4, 2)
    own1 = fetch(mine, "x", 4, 1)
    own3 = fetch(mine, "x", 4, 3)
    eight, y1, y2, y3, own1, own3 = lax.optimization_barrier((eight, y1, y2, y3, own1, own3))
    tok = lax.all_gather(eight.reshape(8 * ROWS, HALF + LANES), "z", axis=0, tiled=True)
    rest = jnp.concatenate([y1, y3, y2[: 2 * SLICE], y2[2 * SLICE :] + count_rows], axis=0)
    rest1 = fetch(rest, "x", 4, 1)
    rest3 = fetch(rest, "x", 4, 3)
    own2g = fetch(own3[:SLICE], "x", 4, 3)
    own2u = fetch(own1[SLICE:], "x", 4, 1)
    rest2a = fetch(rest3[: 3 * SLICE], "x", 4, 3)
    rest2b = fetch(rest1[3 * SLICE :], "x", 4, 1)
    count = sum(p[-1, 0].astype(F32) for p in (rest, rest1, rest3, rest2b))
    count_lanes = jnp.where(jnp.arange(LANES) == 64, count, 0.0).reshape(1, LANES)

    place = jnp.stack([2 * s + t, x, core]).astype(jnp.int32)
    down_half = down.reshape(16, 2, SLICE, 2 * RANK)
    down_half = jnp.where(core == 0, down_half[:, 0], down_half[:, 1]).reshape(HALF, 2 * RANK)
    down_half = jnp.pad(down_half, ((0, 0), (0, LANES - 2 * RANK)))
    (w,) = kernel(
        assemble,
        [((HALF, 2 * COLS), BF16)],
        (place, mine, own1, own3, own2g, own2u, rest, rest1, rest3, rest2a, rest2b),
        0, 8,
    )
    flops = 2 * GROUP * HALF * WIDE
    (far,) = kernel(functools.partial(products, True), [((GROUP, WIDE), F32)], (place, tok, w, down_half), flops, 12)
    partner = lax.ppermute(far, "c", SWAP)
    (near,) = kernel(functools.partial(products, False), [((GROUP, WIDE), F32)], (place, tok, w, down_half), flops, 12)

    units = jnp.where(t == 0, up[:, :COLS], up[:, SKIP:])
    b_gate = jnp.pad(units[:RANK], ((0, LANES - RANK), (0, 0)))
    b_up = jnp.pad(units[RANK:], ((RANK, LANES - 2 * RANK), (0, 0)))
    shared = (jnp.arange(COLS) >= 2 * COLS - readout.shape[0]).astype(BF16)
    read = jnp.where(t == 0, readout[:COLS], readout[SKIP:] * shared).reshape(1, COLS)

    codes = tok[:, HALF].astype(jnp.int32).reshape(2, GROUP)
    pair_of = jnp.arange(LANES, dtype=jnp.int32)
    block_of = jnp.arange(GROUP, dtype=jnp.int32) // ROWS
    inside = (pair_of[:, None] // 2 == block_of[None, :])[None]
    chosen = inside & (codes[:, None, :] == 2 * (pair_of % 2)[None, :, None])
    rejected = inside & (codes[:, None, :] == 2 * (pair_of % 2)[None, :, None] + 1)
    signs = chosen.astype(BF16) - rejected.astype(BF16)
    valid = (jnp.any(chosen, axis=2) & jnp.any(rejected, axis=2)).astype(F32).reshape(2, 1, LANES)

    message, gate_high, gate_low, up_high, up_low, low_t = kernel(
        score,
        [((4 * RANK, 4, LANES), F32)] + [((GROUP, COLS), BF16)] * 4 + [((2 * RANK, GROUP), F32)],
        (place, near, partner, b_gate, b_up, read, signs, count_lanes),
        8 * GROUP * COLS * LANES, 16,
    )
    arrived = lax.all_to_all(message, ("c", "t", "z", "yl"), split_axis=0, concat_axis=0)
    outgoing, pair_total = kernel(
        close,
        [((2 * RANK, 6, LANES), F32), ((8, LANES), F32)],
        (place, arrived, signs, valid, low_t, gate_high, gate_low, up_high, up_low, tok),
        16 * GROUP * HALF * 2, 12,
    )

    arrived = lax.all_to_all(outgoing, DP, split_axis=0, concat_axis=0)
    summed = jnp.sum(arrived.reshape(2, 2, 8, 6, LANES), axis=(0, 2))
    grad_b = jnp.pad(summed[0, :4], ((0, 3), (0, 0))) + jnp.pad(summed[1, :4], ((3, 0), (0, 0)))
    columns = summed[:, 4]
    log_total = summed[0, 5, 0]
    grad_a = lax.all_to_all(
        jnp.broadcast_to(columns[None], (16, 2, SLICE)), BLK, split_axis=0, concat_axis=0
    )
    grad_a = grad_a.transpose(2, 1, 0).reshape(SLICE, 2 * RANK)
    return -log_total / pair_total[0, 0], grad_a, grad_b.reshape(1, 7 * LANES)


def solution(mesh):
    fine = Mesh(mesh.devices.reshape(SIZES), AXES)
    in_specs = (
        P(AXES, None),
        P(AXES, None),
        P(AXES, None),
        P(None, DP, BLK),
        P(),
        P(None, BLK),
        P(BLK),
    )
    out_specs = (P(), P(DP, None), P(DP, BLK))
    return jax.shard_map(
        on_device, mesh=fine, in_specs=in_specs, out_specs=out_specs, check_vma=False
    )
```

```python
import functools

import jax
import jax.numpy as jnp
from jax import lax
from jax.experimental import pallas as pl
from jax.experimental.pallas import tpu as pltpu
from jax.sharding import Mesh, PartitionSpec as P

SEQS = 4
ROWS = 12
RANK = 16
WIDTH = 4096
DPO_BETA = 0.1
LOSS_SCALE = 1024.0
F32 = jnp.float32
BF16 = jnp.bfloat16

AXES = ("s", "t", "x", "c", "z", "yl")
SIZES = (2, 2, 4, 2, 8, 2)
DP = ("s", "t", "x", "c")
BLK = ("z", "yl")
SWAP = [(0, 1), (1, 0)]

SLICE = 128
HALF = WIDTH // 2
LANES = 128
COLS = 512
SKIP = 384
GROUP = 384
BLOCKS = GROUP // ROWS
CONTRACT_LAST = (((1,), (1,)), ((), ()))


def swapped(value, axis, index):
    far = lax.ppermute(value, axis, SWAP)
    return jnp.where(index == 0, jnp.stack([value, far]), jnp.stack([far, value]))


def split(value, terms):
    parts = []
    for _ in range(terms):
        parts.append(value.astype(BF16))
        value = value - parts[-1].astype(F32)
    return parts


def dot(a, b, dims=(((1,), (0,)), ((), ()))):
    return lax.dot_general(a, b, dims, preferred_element_type=F32)


def early_products(place, w, down, p0, r1, l1, r2, l2, r3, l3, r4, l4, tok, acc, low):
    z = place[1]

    def put(k, begin, value):
        start = lax.rem(z + 8 + k, 8) * 8 * ROWS + begin
        tok[pl.ds(pl.multiple_of(start, 48), value.shape[0]), :] = value

    put(0, 0, p0[...])
    for k, (right, left) in enumerate(((r1, l1), (r2, l2), (r3, l3)), 1):
        put(-k, 0, right[...])
        put(k, 0, left[...])
    put(4, 0, r4[...])
    put(4, 4 * ROWS, l4[...])
    for n in range(4):
        part = slice(n * COLS // 2, (n + 1) * COLS // 2)
        acc[:, part] = dot(tok[:, 0 : HALF // 2], w[:, part])
    low[...] = dot(tok[:, 0:HALF], down[...])


def late_products(place, rows, w, acc, out):
    out[...] = acc[...] + dot(rows[...], w[...])


def products(far, place, tok, w, acc):
    half = (lambda place: 1 - place[0]) if far else (lambda place: place[0])
    part = COLS // 2
    return pl.pallas_call(
        late_products,
        grid_spec=pltpu.PrefetchScalarGridSpec(
            num_scalar_prefetch=1,
            grid=(4,),
            in_specs=[
                pl.BlockSpec((GROUP, HALF // 2), lambda n, place: (half(place), 1)),
                pl.BlockSpec((HALF // 2, part), lambda n, place: (0, n)),
                pl.BlockSpec((GROUP, part), lambda n, place: (half(place), n)),
            ],
            out_specs=pl.BlockSpec((GROUP, part), lambda n, place: (0, n)),
        ),
        out_shape=jax.ShapeDtypeStruct((GROUP, 2 * COLS), F32),
        compiler_params=pltpu.CompilerParams(vmem_limit_bytes=12 * 1024 * 1024),
        cost_estimate=pl.CostEstimate(flops=GROUP * HALF * 2 * COLS, bytes_accessed=6_000_000, transcendentals=0),
    )(place, tok, w, acc)


def score(place, near, partner, low_ref, b_gate, b_up, readout, signs, count, message, low_t, k_out, k, sems):
    low_b = low_ref[...]
    gate_ref = near[:, 0:COLS] + partner[:, 0:COLS]
    up_ref = near[:, COLS : 2 * COLS] + partner[:, COLS : 2 * COLS]
    gate_pol = gate_ref + dot(low_b, b_gate[...])
    up_pol = up_ref + dot(low_b, b_up[...])
    sig_ref = jax.nn.sigmoid(gate_ref)
    sig_pol = jax.nn.sigmoid(gate_pol)
    act_pol = gate_pol * sig_pol
    read = readout[...].astype(F32)
    change = act_pol * up_pol - gate_ref * sig_ref * up_ref
    k_gate = read * sig_pol * (1.0 + gate_pol * (1.0 - sig_pol)) * up_pol
    k_up = read * act_pol
    read_b = jnp.broadcast_to(readout[...], (8, COLS))
    change_row = sum(dot(read_b, part, CONTRACT_LAST) for part in split(change, 3))
    sign = signs[place[0]]
    gaps = sum(dot(part, sign, CONTRACT_LAST) for part in split(change_row, 3))
    tail = jnp.broadcast_to(gaps[0:1, :] + count[...], (2 * RANK, LANES))
    high, rest = split(k_gate, 2)
    k[0], k[1] = high, rest
    copies = [pltpu.make_async_copy(k.at[i], k_out.at[i], sems.at[i]) for i in range(4)]
    copies[0].start()
    copies[1].start()
    mixed = dot(b_gate[0 : 2 * RANK, :], high, CONTRACT_LAST) + dot(b_gate[0 : 2 * RANK, :], rest, CONTRACT_LAST)
    high, rest = split(k_up, 2)
    k[2], k[3] = high, rest
    copies[2].start()
    copies[3].start()
    mixed_up = dot(b_up[0 : 2 * RANK, :], high, CONTRACT_LAST) + dot(b_up[0 : 2 * RANK, :], rest, CONTRACT_LAST)
    mixed = mixed + mixed_up
    for core in range(2):
        lines = slice(2 * RANK * core, 2 * RANK * (core + 1))
        for i in range(3):
            message[lines, i, :] = mixed[:, i * LANES : (i + 1) * LANES]
        message[lines, 3, :] = tail
    low_t[...] = low_b.astype(F32).T[0 : 2 * RANK, :]
    for copy in copies:
        copy.wait()


def close(place, arrived, signs, valid, low_t, k_in, tok_in, out, total_out, k, tok, sems):
    tok_copy = pltpu.make_async_copy(tok_in, tok, sems.at[0])
    k_copy = pltpu.make_async_copy(k_in, k, sems.at[1])
    tok_copy.start()
    k_copy.start()
    core = place[0]
    sums = [jnp.sum(arrived[2 * RANK * h : 2 * RANK * (h + 1)], axis=0) for h in range(2)]
    totals = [jnp.concatenate([total[i : i + 1, :] for i in range(3)], axis=1) for total in sums]
    tails = [total[3:4, :] for total in sums]
    pair_total = jnp.maximum(tails[0][:, 64:65] + tails[1][:, 64:65], 1.0)
    logs, cotangents, terms = 0.0, [], []
    for h in range(2):
        logit = DPO_BETA * tails[h]
        logs = logs + jnp.sum(
            valid[h] * (jnp.minimum(logit, 0.0) - jnp.log1p(jnp.exp(-jnp.abs(logit)))), axis=1, keepdims=True
        )
        scaled = -LOSS_SCALE * DPO_BETA * valid[h] * jax.nn.sigmoid(-logit) / pair_total
        scaled = jnp.broadcast_to(scaled, (8, LANES))
        cotangent = sum(dot(part, signs[h]) for part in split(scaled, 3))
        cotangents.append(cotangent[0:1, :])
        projected = jnp.broadcast_to(totals[h], (8, GROUP)) * cotangent
        if h == 0:
            tok_copy.wait()
        terms.append(dot(projected.astype(BF16), tok[h * GROUP : (h + 1) * GROUP, 0:HALF]))
    grad_a = (terms[0] + terms[1])[0:1, :]
    own = jnp.where(core == 0, cotangents[0], cotangents[1])
    high, rest = split(low_t[...] * own, 2)
    k_copy.wait()
    gate = dot(high[0:RANK], k[0]) + dot(high[0:RANK], k[1]) + dot(rest[0:RANK], k[0])
    up = dot(high[RANK:], k[2]) + dot(high[RANK:], k[3]) + dot(rest[RANK:], k[2])
    for i in range(4):
        out[0:RANK, i, :] = gate[:, i * LANES : (i + 1) * LANES]
        out[RANK : 2 * RANK, i, :] = up[:, i * LANES : (i + 1) * LANES]
    line = lax.broadcasted_iota(jnp.int32, (2 * RANK, SLICE), 0)
    slices = jnp.zeros((2 * RANK, SLICE), F32)
    for i in range(RANK):
        here = jnp.broadcast_to(grad_a[:, i * SLICE : (i + 1) * SLICE], (2 * RANK, SLICE))
        other_s, at_x, at_t = i // 8, i // 2 % 4, i % 2
        yh = 2 * (1 - place[2] if other_s else place[2]) + at_t
        slices = jnp.where(line == (yh * 4 + at_x) * 2 + core, here, slices)
    out[:, 4, :] = slices
    out[:, 5, :] = jnp.broadcast_to(0.5 * logs, (2 * RANK, LANES))
    total_out[...] = jnp.broadcast_to(pair_total, (8, LANES))


def kernel(function, shapes, arguments, flops, grant, scratch=(), in_hbm=0, out_hbm=0):
    vmem = pl.BlockSpec(memory_space=pltpu.VMEM)
    smem = pl.BlockSpec(memory_space=pltpu.SMEM)
    hbm = pl.BlockSpec(memory_space=pltpu.HBM)
    return pl.pallas_call(
        function,
        out_shape=tuple(jax.ShapeDtypeStruct(*s) for s in shapes),
        in_specs=[smem] + [vmem] * (len(arguments) - 1 - in_hbm) + [hbm] * in_hbm,
        out_specs=(vmem,) * (len(shapes) - out_hbm) + (hbm,) * out_hbm,
        scratch_shapes=list(scratch),
        compiler_params=pltpu.CompilerParams(vmem_limit_bytes=grant * 1024 * 1024),
        cost_estimate=pl.CostEstimate(flops=flops, bytes_accessed=10_000_000, transcendentals=0),
    )(*arguments)


def along(value, axis, k):
    n = lax.axis_size(axis)
    return lax.ppermute(value, axis, [(i, (i + k) % n) for i in range(n)])


def on_device(tokens, sequence_labels, response_mask, frozen, down, up, readout):
    s, t, core, z, yl = (lax.axis_index(a) for a in ("s", "t", "c", "z", "yl"))
    place = jnp.stack([core, z, s]).astype(jnp.int32)
    code = jnp.where(response_mask > 0, sequence_labels, SEQS)

    low_half = jnp.concatenate([frozen[0, :, :COLS], frozen[1, :, :COLS]], axis=1)
    high_half = jnp.concatenate([frozen[0, :, SKIP:], frozen[1, :, SKIP:]], axis=1)
    mine = jnp.where(t == 0, low_half, high_half)
    other = lax.ppermute(jnp.where(t == 0, high_half, low_half), "t", SWAP)
    pair_w = jnp.where(
        t == 0, jnp.concatenate([mine, other], axis=0), jnp.concatenate([other, mine], axis=0)
    )
    w_own = lax.all_gather(pair_w, "x", axis=0, tiled=True)

    by_core = tokens.reshape(ROWS, 2, 2, 4, 2, SLICE).transpose(4, 1, 0, 3, 2, 5)
    by_core = jnp.where(s == 0, by_core, by_core[:, ::-1]).transpose(0, 2, 1, 3, 4, 5)
    by_core = by_core.reshape(2, ROWS, HALF)
    code_lanes = jnp.pad(code.reshape(ROWS, 1).astype(BF16), ((0, 0), (0, LANES - 1)))
    keep = jnp.concatenate([jnp.where(core == 0, by_core[0], by_core[1]), code_lanes], axis=1)
    give = jnp.concatenate([jnp.where(core == 0, by_core[1], by_core[0]), code_lanes], axis=1)
    take = lax.ppermute(give, "c", SWAP)
    pair = jnp.where(
        core == 0, jnp.concatenate([keep, take], axis=0), jnp.concatenate([take, keep], axis=0)
    )
    eight = swapped(swapped(pair, "yl", yl), "t", t).reshape(8 * ROWS, HALF + LANES)

    eight, pair_w = lax.optimization_barrier((eight, pair_w))
    other_s = lax.ppermute(pair_w, "s", SWAP)
    right, left, ring = eight, eight, [eight]
    for step in range(3):
        right, left = along(right, "z", 1), along(left, "z", -1)
        ring += [right, left]
        if step == 1:
            right, left, other_s = lax.optimization_barrier((right, left, other_s))
    ring += [along(right[: 4 * ROWS], "z", 1), along(left[4 * ROWS :], "z", -1)]
    w_other = lax.all_gather(other_s, "x", axis=0, tiled=True)

    has = [jnp.max((code == q).astype(F32)) for q in range(SEQS)]
    count = jnp.where(jnp.arange(LANES) == 64, has[0] * has[1] + has[2] * has[3], 0.0).reshape(1, LANES)
    count = count + lax.ppermute(count, "s", SWAP)
    count = count + lax.ppermute(count, "x", [(0, 1), (1, 0), (2, 3), (3, 2)])
    count_lanes = count + lax.ppermute(count, "x", [(0, 2), (2, 0), (1, 3), (3, 1)])

    down_half = down.reshape(2, 2, 4, 2, SLICE, 2 * RANK).transpose(3, 0, 2, 1, 4, 5)
    down_half = jnp.where(core == 0, down_half[0], down_half[1])
    down_half = jnp.where(s == 0, down_half, down_half[::-1]).reshape(HALF, 2 * RANK)
    down_half = jnp.pad(down_half, ((0, 0), (0, LANES - 2 * RANK)))
    tok, acc, low_acc = kernel(
        early_products,
        [((2 * GROUP, HALF + LANES), BF16), ((2 * GROUP, 2 * COLS), F32), ((2 * GROUP, LANES), F32)],
        (place, w_own, down_half, *ring),
        2 * GROUP * HALF * 2 * COLS, 16,
    )
    low_acc = low_acc.reshape(2, GROUP, LANES)
    low_near = jnp.where(core == 0, low_acc[0], low_acc[1])
    low_far = jnp.where(core == 0, low_acc[1], low_acc[0])
    low = (low_near + lax.ppermute(low_far, "c", SWAP)).astype(BF16)

    units = jnp.where(t == 0, up[:, :COLS], up[:, SKIP:])
    b_gate = jnp.pad(units[:RANK], ((0, LANES - RANK), (0, 0)))
    b_up = jnp.pad(units[RANK:], ((RANK, LANES - 2 * RANK), (0, 0)))
    shared = (jnp.arange(COLS) >= 2 * COLS - readout.shape[0]).astype(BF16)
    read = jnp.where(t == 0, readout[:COLS], readout[SKIP:] * shared).reshape(1, COLS)

    codes = tok[:, HALF].astype(jnp.int32).reshape(2, GROUP)
    pair_of = jnp.arange(LANES, dtype=jnp.int32)
    block_of = jnp.arange(GROUP, dtype=jnp.int32) // ROWS
    inside = (pair_of[:, None] // 2 == block_of[None, :])[None]
    chosen = inside & (codes[:, None, :] == 2 * (pair_of % 2)[None, :, None])
    rejected = inside & (codes[:, None, :] == 2 * (pair_of % 2)[None, :, None] + 1)
    signs = chosen.astype(BF16) - rejected.astype(BF16)
    valid = (jnp.any(chosen, axis=2) & jnp.any(rejected, axis=2)).astype(F32).reshape(2, 1, LANES)

    w_other, low, b_gate, b_up, read, signs, valid, count_lanes = lax.optimization_barrier(
        (w_other, low, b_gate, b_up, read, signs, valid, count_lanes)
    )
    far = products(True, place, tok, w_other, acc)
    partner = lax.ppermute(far, "c", SWAP)
    near = products(False, place, tok, w_other, acc)
    message, low_t, k = kernel(
        score,
        [((4 * RANK, 4, LANES), F32), ((2 * RANK, GROUP), F32), ((4, GROUP, COLS), BF16)],
        (place, near, partner, low, b_gate, b_up, read, signs, count_lanes),
        8 * GROUP * COLS * LANES, 16,
        scratch=[pltpu.VMEM((4, GROUP, COLS), BF16), pltpu.SemaphoreType.DMA((4,))],
        out_hbm=1,
    )
    arrived = lax.all_to_all(message, ("c", "t", "z", "yl"), split_axis=0, concat_axis=0)
    outgoing, pair_total = kernel(
        close,
        [((2 * RANK, 6, LANES), F32), ((8, LANES), F32)],
        (place, arrived, signs, valid, low_t, k, tok),
        16 * GROUP * HALF * 2, 16,
        scratch=[
            pltpu.VMEM((4, GROUP, COLS), BF16),
            pltpu.VMEM((2 * GROUP, HALF + LANES), BF16),
            pltpu.SemaphoreType.DMA((2,)),
        ],
        in_hbm=2,
    )

    arrived = lax.all_to_all(outgoing, DP, split_axis=0, concat_axis=0)
    summed = jnp.sum(arrived.reshape(2, 2, 8, 6, LANES), axis=(0, 2))
    grad_b = jnp.pad(summed[0, :4], ((0, 3), (0, 0))) + jnp.pad(summed[1, :4], ((3, 0), (0, 0)))
    columns = summed[:, 4]
    log_total = summed[0, 5, 0]
    grad_a = lax.all_to_all(
        jnp.broadcast_to(columns[None], (16, 2, SLICE)), BLK, split_axis=0, concat_axis=0
    )
    grad_a = grad_a.transpose(2, 1, 0).reshape(SLICE, 2 * RANK)
    return -log_total / pair_total[0, 0], grad_a, grad_b.reshape(1, 7 * LANES)


def solution(mesh):
    fine = Mesh(mesh.devices.reshape(SIZES), AXES)
    in_specs = (
        P(AXES, None),
        P(AXES, None),
        P(AXES, None),
        P(None, DP, BLK),
        P(),
        P(None, BLK),
        P(BLK),
    )
    out_specs = (P(), P(DP, None), P(DP, BLK))
    return jax.shard_map(
        on_device, mesh=fine, in_specs=in_specs, out_specs=out_specs, check_vma=False
    )
```

```python
import functools

import jax
import jax.numpy as jnp
from jax import lax
from jax.experimental import pallas as pl
from jax.experimental.pallas import tpu as pltpu
from jax.sharding import Mesh, PartitionSpec as P

SEQS = 4
ROWS = 12
RANK = 16
WIDTH = 4096
DPO_BETA = 0.1
LOSS_SCALE = 1024.0
F32 = jnp.float32
BF16 = jnp.bfloat16

AXES = ("s", "t", "x", "c", "z", "yl")
SIZES = (2, 2, 4, 2, 8, 2)
DP = ("s", "t", "x", "c")
BLK = ("z", "yl")
SWAP = [(0, 1), (1, 0)]

SLICE = 128
HALF = WIDTH // 2
LANES = 128
COLS = 512
SKIP = 384
GROUP = 384
BLOCKS = GROUP // ROWS
CONTRACT_LAST = (((1,), (1,)), ((), ()))


def swapped(value, axis, index):
    far = lax.ppermute(value, axis, SWAP)
    return jnp.where(index == 0, jnp.stack([value, far]), jnp.stack([far, value]))


def split(value, terms):
    parts = []
    for _ in range(terms):
        parts.append(value.astype(BF16))
        value = value - parts[-1].astype(F32)
    return parts


def dot(a, b, dims=(((1,), (0,)), ((), ()))):
    return lax.dot_general(a, b, dims, preferred_element_type=F32)


def early_products(place, down, w_in, p0, r1, l1, r2, l2, r3, l3, r4, l4, low, tok_out, acc_out, tok, w, acc, sems):
    z = place[1]
    block = 8 * ROWS
    w_copy = pltpu.make_async_copy(w_in, w, sems.at[9])
    w_copy.start()
    moves = [(0, 0, p0), (-1, 0, r1), (1, 0, l1), (-2, 0, r2), (2, 0, l2), (-3, 0, r3), (3, 0, l3), (4, 0, r4), (4, 4 * ROWS, l4)]
    copies = []
    for n, (k, begin, ref) in enumerate(moves):
        start = pl.multiple_of(lax.rem(z + 8 + k, 8) * block + begin, 4 * ROWS)
        copies.append(pltpu.make_async_copy(ref, tok.at[pl.ds(start, ref.shape[0]), :], sems.at[n]))
        copies[-1].start()
    for copy in copies:
        copy.wait()
    tok_copy = pltpu.make_async_copy(tok, tok_out, sems.at[10])
    tok_copy.start()
    low[...] = dot(tok[:, 0:HALF], down[...])
    w_copy.wait()
    for n in range(4):
        part = slice(n * COLS // 2, (n + 1) * COLS // 2)
        acc[:, part] = dot(tok[:, 0 : HALF // 2], w[:, part])
    acc_copy = pltpu.make_async_copy(acc, acc_out, sems.at[11])
    acc_copy.start()
    acc_copy.wait()
    tok_copy.wait()


def late_products(place, rows, w, acc, out):
    out[...] = acc[...] + dot(rows[...], w[...].reshape(HALF // 2, COLS // 2))


def products(far, place, tok, w, acc):
    half = (lambda place: 1 - place[0]) if far else (lambda place: place[0])
    part = COLS // 2
    return pl.pallas_call(
        late_products,
        grid_spec=pltpu.PrefetchScalarGridSpec(
            num_scalar_prefetch=1,
            grid=(4,),
            in_specs=[
                pl.BlockSpec((GROUP, HALF // 2), lambda n, place: (half(place), 1)),
                pl.BlockSpec((4, 2 * SLICE, part), lambda n, place: (0, 0, n)),
                pl.BlockSpec((GROUP, part), lambda n, place: (half(place), n)),
            ],
            out_specs=pl.BlockSpec((GROUP, part), lambda n, place: (0, n)),
        ),
        out_shape=jax.ShapeDtypeStruct((GROUP, 2 * COLS), F32),
        compiler_params=pltpu.CompilerParams(vmem_limit_bytes=12 * 1024 * 1024),
        cost_estimate=pl.CostEstimate(flops=GROUP * HALF * 2 * COLS, bytes_accessed=6_000_000, transcendentals=0),
    )(place, tok, w, acc)


def score(place, near, partner, low_ref, b_gate, b_up, readout, signs, count, message, low_t, k_out, k, sems):
    low_b = low_ref[...]
    gate_ref = near[:, 0:COLS] + partner[:, 0:COLS]
    up_ref = near[:, COLS : 2 * COLS] + partner[:, COLS : 2 * COLS]
    gate_pol = gate_ref + dot(low_b, b_gate[...])
    up_pol = up_ref + dot(low_b, b_up[...])
    sig_ref = jax.nn.sigmoid(gate_ref)
    sig_pol = jax.nn.sigmoid(gate_pol)
    act_pol = gate_pol * sig_pol
    read = readout[...].astype(F32)
    change = act_pol * up_pol - gate_ref * sig_ref * up_ref
    k_gate = read * sig_pol * (1.0 + gate_pol * (1.0 - sig_pol)) * up_pol
    k_up = read * act_pol
    read_b = jnp.broadcast_to(readout[...], (8, COLS))
    change_row = sum(dot(read_b, part, CONTRACT_LAST) for part in split(change, 3))
    sign = signs[place[0]]
    gaps = sum(dot(part, sign, CONTRACT_LAST) for part in split(change_row, 3))
    tail = jnp.broadcast_to(gaps[0:1, :] + count[...], (2 * RANK, LANES))
    high, rest = split(k_gate, 2)
    k[0], k[1] = high, rest
    copies = [pltpu.make_async_copy(k.at[i], k_out.at[i], sems.at[i]) for i in range(4)]
    copies[0].start()
    copies[1].start()
    mixed = dot(b_gate[0 : 2 * RANK, :], high, CONTRACT_LAST) + dot(b_gate[0 : 2 * RANK, :], rest, CONTRACT_LAST)
    high, rest = split(k_up, 2)
    k[2], k[3] = high, rest
    copies[2].start()
    copies[3].start()
    mixed_up = dot(b_up[0 : 2 * RANK, :], high, CONTRACT_LAST) + dot(b_up[0 : 2 * RANK, :], rest, CONTRACT_LAST)
    mixed = mixed + mixed_up
    for core in range(2):
        lines = slice(2 * RANK * core, 2 * RANK * (core + 1))
        for i in range(3):
            message[lines, i, :] = mixed[:, i * LANES : (i + 1) * LANES]
        message[lines, 3, :] = tail
    low_t[...] = low_b.astype(F32).T[0 : 2 * RANK, :]
    for copy in copies:
        copy.wait()


def close(place, arrived, signs, valid, low_t, k_in, tok_in, out, total_out, k, tok, sems):
    tok_copy = pltpu.make_async_copy(tok_in, tok, sems.at[0])
    k_copy = pltpu.make_async_copy(k_in, k, sems.at[1])
    tok_copy.start()
    k_copy.start()
    core = place[0]
    sums = [jnp.sum(arrived[2 * RANK * h : 2 * RANK * (h + 1)], axis=0) for h in range(2)]
    totals = [jnp.concatenate([total[i : i + 1, :] for i in range(3)], axis=1) for total in sums]
    tails = [total[3:4, :] for total in sums]
    pair_total = jnp.maximum(tails[0][:, 64:65] + tails[1][:, 64:65], 1.0)
    logs, cotangents, terms = 0.0, [], []
    for h in range(2):
        logit = DPO_BETA * tails[h]
        logs = logs + jnp.sum(
            valid[h] * (jnp.minimum(logit, 0.0) - jnp.log1p(jnp.exp(-jnp.abs(logit)))), axis=1, keepdims=True
        )
        scaled = -LOSS_SCALE * DPO_BETA * valid[h] * jax.nn.sigmoid(-logit) / pair_total
        scaled = jnp.broadcast_to(scaled, (8, LANES))
        cotangent = sum(dot(part, signs[h]) for part in split(scaled, 3))
        cotangents.append(cotangent[0:1, :])
        projected = jnp.broadcast_to(totals[h], (8, GROUP)) * cotangent
        if h == 0:
            tok_copy.wait()
        terms.append(dot(projected.astype(BF16), tok[h * GROUP : (h + 1) * GROUP, 0:HALF]))
    grad_a = (terms[0] + terms[1])[0:1, :]
    own = jnp.where(core == 0, cotangents[0], cotangents[1])
    high, rest = split(low_t[...] * own, 2)
    k_copy.wait()
    gate = dot(high[0:RANK], k[0]) + dot(high[0:RANK], k[1]) + dot(rest[0:RANK], k[0])
    up = dot(high[RANK:], k[2]) + dot(high[RANK:], k[3]) + dot(rest[RANK:], k[2])
    for i in range(4):
        out[0:RANK, i, :] = gate[:, i * LANES : (i + 1) * LANES]
        out[RANK : 2 * RANK, i, :] = up[:, i * LANES : (i + 1) * LANES]
    line = lax.broadcasted_iota(jnp.int32, (2 * RANK, SLICE), 0)
    slices = jnp.zeros((2 * RANK, SLICE), F32)
    for i in range(RANK):
        here = jnp.broadcast_to(grad_a[:, i * SLICE : (i + 1) * SLICE], (2 * RANK, SLICE))
        other_s, at_x, at_t = i // 8, i // 2 % 4, i % 2
        yh = 2 * (1 - place[2] if other_s else place[2]) + at_t
        slices = jnp.where(line == (yh * 4 + at_x) * 2 + core, here, slices)
    out[:, 4, :] = slices
    out[:, 5, :] = jnp.broadcast_to(0.5 * logs, (2 * RANK, LANES))
    total_out[...] = jnp.broadcast_to(pair_total, (8, LANES))


def kernel(function, shapes, arguments, flops, grant, scratch=(), in_any=0, out_hbm=0):
    vmem = pl.BlockSpec(memory_space=pltpu.VMEM)
    smem = pl.BlockSpec(memory_space=pltpu.SMEM)
    hbm = pl.BlockSpec(memory_space=pltpu.HBM)
    return pl.pallas_call(
        function,
        out_shape=tuple(jax.ShapeDtypeStruct(*s) for s in shapes),
        in_specs=[smem] + [vmem] * (len(arguments) - 1 - in_any) + [pl.BlockSpec(memory_space=pl.ANY)] * in_any,
        out_specs=(vmem,) * (len(shapes) - out_hbm) + (hbm,) * out_hbm,
        scratch_shapes=list(scratch),
        compiler_params=pltpu.CompilerParams(vmem_limit_bytes=grant * 1024 * 1024),
        cost_estimate=pl.CostEstimate(flops=flops, bytes_accessed=10_000_000, transcendentals=0),
    )(*arguments)


def along(value, axis, k):
    n = lax.axis_size(axis)
    return lax.ppermute(value, axis, [(i, (i + k) % n) for i in range(n)])


def on_device(tokens, sequence_labels, response_mask, frozen, down, up, readout):
    s, t, core, z, yl = (lax.axis_index(a) for a in ("s", "t", "c", "z", "yl"))
    place = jnp.stack([core, z, s]).astype(jnp.int32)
    code = jnp.where(response_mask > 0, sequence_labels, SEQS)

    by_core = tokens.reshape(ROWS, 2, 2, 4, 2, SLICE).transpose(4, 1, 0, 3, 2, 5)
    by_core = jnp.where(s == 0, by_core, by_core[:, ::-1]).transpose(0, 2, 1, 3, 4, 5)
    by_core = by_core.reshape(2, ROWS, HALF)
    code_lanes = jnp.pad(code.reshape(ROWS, 1).astype(BF16), ((0, 0), (0, LANES - 1)))
    keep = jnp.concatenate([jnp.where(core == 0, by_core[0], by_core[1]), code_lanes], axis=1)
    give = jnp.concatenate([jnp.where(core == 0, by_core[1], by_core[0]), code_lanes], axis=1)
    take = lax.ppermute(give, "c", SWAP)
    pair = jnp.where(
        core == 0, jnp.concatenate([keep, take], axis=0), jnp.concatenate([take, keep], axis=0)
    )
    four = swapped(pair, "yl", yl)

    low_half = jnp.concatenate([frozen[0, :, :COLS], frozen[1, :, :COLS]], axis=1)
    high_half = jnp.concatenate([frozen[0, :, SKIP:], frozen[1, :, SKIP:]], axis=1)
    mine = jnp.where(t == 0, low_half, high_half)
    other = lax.ppermute(jnp.where(t == 0, high_half, low_half), "t", SWAP)
    four, other = lax.optimization_barrier((four, other))
    pair_w = jnp.where(
        t == 0, jnp.concatenate([mine, other], axis=0), jnp.concatenate([other, mine], axis=0)
    )
    w_own = lax.all_gather(pair_w, "x", axis=0, tiled=True)

    eight = swapped(four, "t", t).reshape(8 * ROWS, HALF + LANES)

    has = [jnp.max((code == q).astype(F32)) for q in range(SEQS)]
    count_rows = jnp.broadcast_to((has[0] * has[1] + has[2] * has[3]).astype(BF16), (16, 2 * COLS))
    eight, pair_w = lax.optimization_barrier((eight, pair_w))
    other_s = lax.ppermute(jnp.concatenate([pair_w, count_rows], axis=0), "s", SWAP)
    right, left, ring = eight, eight, [eight]
    for step in range(3):
        right, left = along(right, "z", 1), along(left, "z", -1)
        ring += [right, left]
        if step == 1:
            right, left, other_s = lax.optimization_barrier((right, left, other_s))
    ring += [along(right[: 4 * ROWS], "z", 1), along(left[4 * ROWS :], "z", -1)]
    other_s = jnp.concatenate([other_s[: 2 * SLICE], other_s[2 * SLICE :] + count_rows], axis=0)
    w_other = lax.all_gather(other_s, "x", axis=0, tiled=True).reshape(4, 2 * SLICE + 16, 2 * COLS)

    down_half = down.reshape(2, 2, 4, 2, SLICE, 2 * RANK).transpose(3, 0, 2, 1, 4, 5)
    down_half = jnp.where(core == 0, down_half[0], down_half[1])
    down_half = jnp.where(s == 0, down_half, down_half[::-1]).reshape(HALF, 2 * RANK)
    down_half = jnp.pad(down_half, ((0, 0), (0, LANES - 2 * RANK)))
    low_acc, tok, acc = kernel(
        early_products,
        [((2 * GROUP, LANES), F32), ((2 * GROUP, HALF + LANES), BF16), ((2 * GROUP, 2 * COLS), F32)],
        (place, down_half, w_own, *ring),
        2 * GROUP * HALF * 2 * COLS, 20,
        scratch=[
            pltpu.VMEM((2 * GROUP, HALF + LANES), BF16),
            pltpu.VMEM((HALF // 2, 2 * COLS), BF16),
            pltpu.VMEM((2 * GROUP, 2 * COLS), F32),
            pltpu.SemaphoreType.DMA((12,)),
        ],
        in_any=10, out_hbm=2,
    )
    low_acc = low_acc.reshape(2, GROUP, LANES)
    low_near = jnp.where(core == 0, low_acc[0], low_acc[1])
    low_far = jnp.where(core == 0, low_acc[1], low_acc[0])
    low = (low_near + lax.ppermute(low_far, "c", SWAP)).astype(BF16)

    units = jnp.where(t == 0, up[:, :COLS], up[:, SKIP:])
    b_gate = jnp.pad(units[:RANK], ((0, LANES - RANK), (0, 0)))
    b_up = jnp.pad(units[RANK:], ((RANK, LANES - 2 * RANK), (0, 0)))
    shared = (jnp.arange(COLS) >= 2 * COLS - readout.shape[0]).astype(BF16)
    read = jnp.where(t == 0, readout[:COLS], readout[SKIP:] * shared).reshape(1, COLS)

    codes = tok[:, HALF].astype(jnp.int32).reshape(2, GROUP)
    pair_of = jnp.arange(LANES, dtype=jnp.int32)
    block_of = jnp.arange(GROUP, dtype=jnp.int32) // ROWS
    inside = (pair_of[:, None] // 2 == block_of[None, :])[None]
    chosen = inside & (codes[:, None, :] == 2 * (pair_of % 2)[None, :, None])
    rejected = inside & (codes[:, None, :] == 2 * (pair_of % 2)[None, :, None] + 1)
    signs = chosen.astype(BF16) - rejected.astype(BF16)
    valid = (jnp.any(chosen, axis=2) & jnp.any(rejected, axis=2)).astype(F32).reshape(2, 1, LANES)

    w_other, low, b_gate, b_up, read, signs, valid = lax.optimization_barrier(
        (w_other, low, b_gate, b_up, read, signs, valid)
    )
    count = jnp.sum(w_other[:, 2 * SLICE, 0].astype(F32))
    count_lanes = jnp.where(jnp.arange(LANES) == 64, count, 0.0).reshape(1, LANES)
    far = products(True, place, tok, w_other, acc)
    partner = lax.ppermute(far, "c", SWAP)
    near = products(False, place, tok, w_other, acc)
    message, low_t, k = kernel(
        score,
        [((4 * RANK, 4, LANES), F32), ((2 * RANK, GROUP), F32), ((4, GROUP, COLS), BF16)],
        (place, near, partner, low, b_gate, b_up, read, signs, count_lanes),
        8 * GROUP * COLS * LANES, 16,
        scratch=[pltpu.VMEM((4, GROUP, COLS), BF16), pltpu.SemaphoreType.DMA((4,))],
        out_hbm=1,
    )
    arrived = lax.all_to_all(message, ("c", "t", "z", "yl"), split_axis=0, concat_axis=0)
    outgoing, pair_total = kernel(
        close,
        [((2 * RANK, 6, LANES), F32), ((8, LANES), F32)],
        (place, arrived, signs, valid, low_t, k, tok),
        16 * GROUP * HALF * 2, 16,
        scratch=[
            pltpu.VMEM((4, GROUP, COLS), BF16),
            pltpu.VMEM((2 * GROUP, HALF + LANES), BF16),
            pltpu.SemaphoreType.DMA((2,)),
        ],
        in_any=2,
    )

    arrived = lax.all_to_all(outgoing, DP, split_axis=0, concat_axis=0)
    summed = jnp.sum(arrived.reshape(2, 2, 8, 6, LANES), axis=(0, 2))
    grad_b = jnp.pad(summed[0, :4], ((0, 3), (0, 0))) + jnp.pad(summed[1, :4], ((3, 0), (0, 0)))
    columns = summed[:, 4]
    log_total = summed[0, 5, 0]
    grad_a = lax.all_to_all(
        jnp.broadcast_to(columns[None], (16, 2, SLICE)), BLK, split_axis=0, concat_axis=0
    )
    grad_a = grad_a.transpose(2, 1, 0).reshape(SLICE, 2 * RANK)
    return -log_total / pair_total[0, 0], grad_a, grad_b.reshape(1, 7 * LANES)


def solution(mesh):
    fine = Mesh(mesh.devices.reshape(SIZES), AXES)
    in_specs = (
        P(AXES, None),
        P(AXES, None),
        P(AXES, None),
        P(None, DP, BLK),
        P(),
        P(None, BLK),
        P(BLK),
    )
    out_specs = (P(), P(DP, None), P(DP, BLK))
    return jax.shard_map(
        on_device, mesh=fine, in_specs=in_specs, out_specs=out_specs, check_vma=False
    )
```

```python
import functools

import jax
import jax.numpy as jnp
from jax import lax
from jax.experimental import pallas as pl
from jax.experimental.pallas import tpu as pltpu
from jax.sharding import Mesh, PartitionSpec as P

SEQS = 4
ROWS = 12
RANK = 16
WIDTH = 4096
DPO_BETA = 0.1
LOSS_SCALE = 1024.0
F32 = jnp.float32
BF16 = jnp.bfloat16

AXES = ("s", "t", "x", "c", "z", "yl")
SIZES = (2, 2, 4, 2, 8, 2)
DP = ("s", "t", "x", "c")
BLK = ("z", "yl")
SWAP = [(0, 1), (1, 0)]

SLICE = 128
HALF = WIDTH // 2
LANES = 128
COLS = 512
SKIP = 384
GROUP = 384
BLOCKS = GROUP // ROWS
CONTRACT_LAST = (((1,), (1,)), ((), ()))


def swapped(value, axis, index):
    far = lax.ppermute(value, axis, SWAP)
    return jnp.where(index == 0, jnp.stack([value, far]), jnp.stack([far, value]))


def split(value, terms):
    parts = []
    for _ in range(terms):
        parts.append(value.astype(BF16))
        value = value - parts[-1].astype(F32)
    return parts


def dot(a, b, dims=(((1,), (0,)), ((), ()))):
    return lax.dot_general(a, b, dims, preferred_element_type=F32)


def early_products(place, down, w_in, p0, r1, l1, r2, l2, r3, l3, r4, l4, low, tok_out, acc_out, tok, w, acc, sems):
    z = place[1]
    block = 8 * ROWS
    w_copy = pltpu.make_async_copy(w_in.at[:, pl.ds(0, 2 * SLICE), :], w, sems.at[9])
    w_copy.start()
    moves = [(0, 0, p0), (-1, 0, r1), (1, 0, l1), (-2, 0, r2), (2, 0, l2), (-3, 0, r3), (3, 0, l3), (4, 0, r4), (4, 4 * ROWS, l4)]
    copies = []
    for n, (k, begin, ref) in enumerate(moves):
        start = pl.multiple_of(lax.rem(z + 8 + k, 8) * block + begin, 4 * ROWS)
        copies.append(pltpu.make_async_copy(ref, tok.at[pl.ds(start, ref.shape[0]), :], sems.at[n]))
        copies[-1].start()
    for copy in copies:
        copy.wait()
    tok_copy = pltpu.make_async_copy(tok, tok_out, sems.at[10])
    tok_copy.start()
    low[...] = dot(tok[:, 0:HALF], down[...])
    w_copy.wait()
    copies = [tok_copy]
    for n in range(4):
        part = pl.ds(n * COLS // 2, COLS // 2)
        acc[:, part] = dot(tok[:, 0 : HALF // 2], w[:, :, part].reshape(HALF // 2, COLS // 2))
        copies.append(pltpu.make_async_copy(acc.at[:, part], acc_out.at[:, part], sems.at[11 + n]))
        copies[-1].start()
    for copy in copies:
        copy.wait()


def late_products(far, place, tok, w_in, acc_in, out, rows, w, acc, sems):
    half = 1 - place[0] if far else place[0]
    mine = pl.ds(pl.multiple_of(half * GROUP, GROUP), GROUP)
    parts = [pl.ds(n * COLS // 2, COLS // 2) for n in range(4)]
    rows_copy = pltpu.make_async_copy(tok.at[mine, pl.ds(HALF // 2, HALF // 2)], rows, sems.at[0])
    rows_copy.start()
    copies = []
    for n, part in enumerate(parts):
        copies.append(
            (
                pltpu.make_async_copy(w_in.at[:, pl.ds(0, 2 * SLICE), part], w.at[:, :, part], sems.at[1 + n]),
                pltpu.make_async_copy(acc_in.at[mine, part], acc.at[:, part], sems.at[5 + n]),
            )
        )
        copies[-1][0].start()
        copies[-1][1].start()
    rows_copy.wait()
    for part, pair in zip(parts, copies):
        pair[0].wait()
        pair[1].wait()
        out[:, part] = acc[:, part] + dot(rows[...], w[:, :, part].reshape(HALF // 2, COLS // 2))


def products(far, place, tok, w, acc):
    return kernel(
        functools.partial(late_products, far),
        [((GROUP, 2 * COLS), F32)],
        (place, tok, w, acc),
        GROUP * HALF * 2 * COLS, 56,
        scratch=[
            pltpu.VMEM((GROUP, HALF // 2), BF16),
            pltpu.VMEM((4, 2 * SLICE, 2 * COLS), BF16),
            pltpu.VMEM((GROUP, 2 * COLS), F32),
            pltpu.SemaphoreType.DMA((9,)),
        ],
        in_hbm=3,
    )[0]


def score(place, near, partner, low_ref, b_gate, b_up, readout, signs, count, message, low_t, k_out, k, sems):
    low_b = low_ref[...]
    gate_ref = near[:, 0:COLS] + partner[:, 0:COLS]
    up_ref = near[:, COLS : 2 * COLS] + partner[:, COLS : 2 * COLS]
    gate_pol = gate_ref + dot(low_b, b_gate[...])
    up_pol = up_ref + dot(low_b, b_up[...])
    sig_ref = jax.nn.sigmoid(gate_ref)
    sig_pol = jax.nn.sigmoid(gate_pol)
    act_pol = gate_pol * sig_pol
    read = readout[...].astype(F32)
    change = act_pol * up_pol - gate_ref * sig_ref * up_ref
    k_gate = read * sig_pol * (1.0 + gate_pol * (1.0 - sig_pol)) * up_pol
    k_up = read * act_pol
    read_b = jnp.broadcast_to(readout[...], (8, COLS))
    change_row = sum(dot(read_b, part, CONTRACT_LAST) for part in split(change, 3))
    sign = signs[place[0]]
    gaps = sum(dot(part, sign, CONTRACT_LAST) for part in split(change_row, 3))
    tail = jnp.broadcast_to(gaps[0:1, :] + count[...], (2 * RANK, LANES))
    high, rest = split(k_gate, 2)
    k[0], k[1] = high, rest
    copies = [pltpu.make_async_copy(k.at[i], k_out.at[i], sems.at[i]) for i in range(4)]
    copies[0].start()
    copies[1].start()
    mixed = dot(b_gate[0 : 2 * RANK, :], high, CONTRACT_LAST) + dot(b_gate[0 : 2 * RANK, :], rest, CONTRACT_LAST)
    high, rest = split(k_up, 2)
    k[2], k[3] = high, rest
    copies[2].start()
    copies[3].start()
    mixed_up = dot(b_up[0 : 2 * RANK, :], high, CONTRACT_LAST) + dot(b_up[0 : 2 * RANK, :], rest, CONTRACT_LAST)
    mixed = mixed + mixed_up
    for core in range(2):
        lines = slice(2 * RANK * core, 2 * RANK * (core + 1))
        for i in range(3):
            message[lines, i, :] = mixed[:, i * LANES : (i + 1) * LANES]
        message[lines, 3, :] = tail
    low_t[...] = low_b.astype(F32).T[0 : 2 * RANK, :]
    for copy in copies:
        copy.wait()


def close(place, arrived, signs, valid, low_t, k_in, tok_in, out, total_out, k, tok, sems):
    tok_copy = pltpu.make_async_copy(tok_in, tok, sems.at[0])
    k_copy = pltpu.make_async_copy(k_in, k, sems.at[1])
    tok_copy.start()
    k_copy.start()
    core = place[0]
    sums = [jnp.sum(arrived[2 * RANK * h : 2 * RANK * (h + 1)], axis=0) for h in range(2)]
    totals = [jnp.concatenate([total[i : i + 1, :] for i in range(3)], axis=1) for total in sums]
    tails = [total[3:4, :] for total in sums]
    pair_total = jnp.maximum(tails[0][:, 64:65] + tails[1][:, 64:65], 1.0)
    logs, cotangents, terms = 0.0, [], []
    for h in range(2):
        logit = DPO_BETA * tails[h]
        logs = logs + jnp.sum(
            valid[h] * (jnp.minimum(logit, 0.0) - jnp.log1p(jnp.exp(-jnp.abs(logit)))), axis=1, keepdims=True
        )
        scaled = -LOSS_SCALE * DPO_BETA * valid[h] * jax.nn.sigmoid(-logit) / pair_total
        scaled = jnp.broadcast_to(scaled, (8, LANES))
        cotangent = sum(dot(part, signs[h]) for part in split(scaled, 3))
        cotangents.append(cotangent[0:1, :])
        projected = jnp.broadcast_to(totals[h], (8, GROUP)) * cotangent
        if h == 0:
            tok_copy.wait()
        terms.append(dot(projected.astype(BF16), tok[h * GROUP : (h + 1) * GROUP, 0:HALF]))
    grad_a = (terms[0] + terms[1])[0:1, :]
    own = jnp.where(core == 0, cotangents[0], cotangents[1])
    high, rest = split(low_t[...] * own, 2)
    k_copy.wait()
    gate = dot(high[0:RANK], k[0]) + dot(high[0:RANK], k[1]) + dot(rest[0:RANK], k[0])
    up = dot(high[RANK:], k[2]) + dot(high[RANK:], k[3]) + dot(rest[RANK:], k[2])
    for i in range(4):
        out[0:RANK, i, :] = gate[:, i * LANES : (i + 1) * LANES]
        out[RANK : 2 * RANK, i, :] = up[:, i * LANES : (i + 1) * LANES]
    line = lax.broadcasted_iota(jnp.int32, (2 * RANK, SLICE), 0)
    slices = jnp.zeros((2 * RANK, SLICE), F32)
    for i in range(RANK):
        here = jnp.broadcast_to(grad_a[:, i * SLICE : (i + 1) * SLICE], (2 * RANK, SLICE))
        other_s, at_x, at_t = i // 8, i // 2 % 4, i % 2
        yh = 2 * (1 - place[2] if other_s else place[2]) + at_t
        slices = jnp.where(line == (yh * 4 + at_x) * 2 + core, here, slices)
    out[:, 4, :] = slices
    out[:, 5, :] = jnp.broadcast_to(0.5 * logs, (2 * RANK, LANES))
    total_out[...] = jnp.broadcast_to(pair_total, (8, LANES))


def kernel(function, shapes, arguments, flops, grant, scratch=(), in_hbm=0, out_hbm=0):
    vmem = pl.BlockSpec(memory_space=pltpu.VMEM)
    smem = pl.BlockSpec(memory_space=pltpu.SMEM)
    hbm = pl.BlockSpec(memory_space=pltpu.HBM)
    return pl.pallas_call(
        function,
        out_shape=tuple(jax.ShapeDtypeStruct(*s) for s in shapes),
        in_specs=[smem] + [vmem] * (len(arguments) - 1 - in_hbm) + [hbm] * in_hbm,
        out_specs=(vmem,) * (len(shapes) - out_hbm) + (hbm,) * out_hbm,
        scratch_shapes=list(scratch),
        compiler_params=pltpu.CompilerParams(vmem_limit_bytes=grant * 1024 * 1024),
        cost_estimate=pl.CostEstimate(flops=flops, bytes_accessed=10_000_000, transcendentals=0),
    )(*arguments)


def along(value, axis, k):
    n = lax.axis_size(axis)
    return lax.ppermute(value, axis, [(i, (i + k) % n) for i in range(n)])


def on_device(tokens, sequence_labels, response_mask, frozen, down, up, readout):
    s, t, core, z, yl = (lax.axis_index(a) for a in ("s", "t", "c", "z", "yl"))
    place = jnp.stack([core, z, s]).astype(jnp.int32)
    code = jnp.where(response_mask > 0, sequence_labels, SEQS)

    by_core = tokens.reshape(ROWS, 2, 2, 4, 2, SLICE).transpose(4, 1, 0, 3, 2, 5)
    by_core = jnp.where(s == 0, by_core, by_core[:, ::-1]).transpose(0, 2, 1, 3, 4, 5)
    by_core = by_core.reshape(2, ROWS, HALF)
    code_lanes = jnp.pad(code.reshape(ROWS, 1).astype(BF16), ((0, 0), (0, LANES - 1)))
    keep = jnp.concatenate([jnp.where(core == 0, by_core[0], by_core[1]), code_lanes], axis=1)
    give = jnp.concatenate([jnp.where(core == 0, by_core[1], by_core[0]), code_lanes], axis=1)
    take = lax.ppermute(give, "c", SWAP)
    pair = jnp.where(
        core == 0, jnp.concatenate([keep, take], axis=0), jnp.concatenate([take, keep], axis=0)
    )
    four = swapped(pair, "yl", yl)

    low_half = jnp.concatenate([frozen[0, :, :COLS], frozen[1, :, :COLS]], axis=1)
    high_half = jnp.concatenate([frozen[0, :, SKIP:], frozen[1, :, SKIP:]], axis=1)
    mine = jnp.where(t == 0, low_half, high_half)
    other = lax.ppermute(jnp.where(t == 0, high_half, low_half), "t", SWAP)
    four, other = lax.optimization_barrier((four, other))
    has = [jnp.max((code == q).astype(F32)) for q in range(SEQS)]
    count_rows = jnp.broadcast_to((has[0] * has[1] + has[2] * has[3]).astype(BF16), (16, 2 * COLS))

    def both_t(mine, other):
        return jnp.concatenate(
            [jnp.where(t == 0, mine, other), jnp.where(t == 0, other, mine), count_rows], axis=0
        )

    pair_w = both_t(mine, other)
    w_own = lax.all_gather(pair_w, "x", axis=0, tiled=True).reshape(4, 2 * SLICE + 16, 2 * COLS)

    eight = swapped(four, "t", t).reshape(8 * ROWS, HALF + LANES)

    other_s = lax.ppermute(both_t(*lax.optimization_barrier((mine, other))), "s", SWAP)
    right, left, ring = eight, eight, [eight]
    for step in range(3):
        right, left = along(right, "z", 1), along(left, "z", -1)
        ring += [right, left]
        if step == 1:
            right, left, other_s = lax.optimization_barrier((right, left, other_s))
    ring += [along(right[: 4 * ROWS], "z", 1), along(left[4 * ROWS :], "z", -1)]
    w_other = lax.all_gather(other_s, "x", axis=0, tiled=True).reshape(4, 2 * SLICE + 16, 2 * COLS)

    down_half = down.reshape(2, 2, 4, 2, SLICE, 2 * RANK).transpose(3, 0, 2, 1, 4, 5)
    down_half = jnp.where(core == 0, down_half[0], down_half[1])
    down_half = jnp.where(s == 0, down_half, down_half[::-1]).reshape(HALF, 2 * RANK)
    down_half = jnp.pad(down_half, ((0, 0), (0, LANES - 2 * RANK)))
    low_acc, tok, acc = kernel(
        early_products,
        [((2 * GROUP, LANES), F32), ((2 * GROUP, HALF + LANES), BF16), ((2 * GROUP, 2 * COLS), F32)],
        (place, down_half, w_own, *ring),
        2 * GROUP * HALF * 2 * COLS, 56,
        scratch=[
            pltpu.VMEM((2 * GROUP, HALF + LANES), BF16),
            pltpu.VMEM((4, 2 * SLICE, 2 * COLS), BF16),
            pltpu.VMEM((2 * GROUP, 2 * COLS), F32),
            pltpu.SemaphoreType.DMA((15,)),
        ],
        in_hbm=10, out_hbm=2,
    )
    low_acc = low_acc.reshape(2, GROUP, LANES)
    low_near = jnp.where(core == 0, low_acc[0], low_acc[1])
    low_far = jnp.where(core == 0, low_acc[1], low_acc[0])
    low = (low_near + lax.ppermute(low_far, "c", SWAP)).astype(BF16)

    units = jnp.where(t == 0, up[:, :COLS], up[:, SKIP:])
    b_gate = jnp.pad(units[:RANK], ((0, LANES - RANK), (0, 0)))
    b_up = jnp.pad(units[RANK:], ((RANK, LANES - 2 * RANK), (0, 0)))
    shared = (jnp.arange(COLS) >= 2 * COLS - readout.shape[0]).astype(BF16)
    read = jnp.where(t == 0, readout[:COLS], readout[SKIP:] * shared).reshape(1, COLS)

    codes = tok[:, HALF].astype(jnp.int32).reshape(2, GROUP)
    pair_of = jnp.arange(LANES, dtype=jnp.int32)
    block_of = jnp.arange(GROUP, dtype=jnp.int32) // ROWS
    inside = (pair_of[:, None] // 2 == block_of[None, :])[None]
    chosen = inside & (codes[:, None, :] == 2 * (pair_of % 2)[None, :, None])
    rejected = inside & (codes[:, None, :] == 2 * (pair_of % 2)[None, :, None] + 1)
    signs = chosen.astype(BF16) - rejected.astype(BF16)
    valid = (jnp.any(chosen, axis=2) & jnp.any(rejected, axis=2)).astype(F32).reshape(2, 1, LANES)

    w_other, low, b_gate, b_up, read, signs, valid = lax.optimization_barrier(
        (w_other, low, b_gate, b_up, read, signs, valid)
    )
    count = jnp.sum((w_own[:, 2 * SLICE, 0] + w_other[:, 2 * SLICE, 0]).astype(F32))
    count_lanes = jnp.where(jnp.arange(LANES) == 64, count, 0.0).reshape(1, LANES)
    far = products(True, place, tok, w_other, acc)
    partner = lax.ppermute(far, "c", SWAP)
    near = products(False, place, tok, w_other, acc)
    message, low_t, k = kernel(
        score,
        [((4 * RANK, 4, LANES), F32), ((2 * RANK, GROUP), F32), ((4, GROUP, COLS), BF16)],
        (place, near, partner, low, b_gate, b_up, read, signs, count_lanes),
        8 * GROUP * COLS * LANES, 16,
        scratch=[pltpu.VMEM((4, GROUP, COLS), BF16), pltpu.SemaphoreType.DMA((4,))],
        out_hbm=1,
    )
    arrived = lax.all_to_all(message, ("c", "t", "z", "yl"), split_axis=0, concat_axis=0)
    outgoing, pair_total = kernel(
        close,
        [((2 * RANK, 6, LANES), F32), ((8, LANES), F32)],
        (place, arrived, signs, valid, low_t, k, tok),
        16 * GROUP * HALF * 2, 16,
        scratch=[
            pltpu.VMEM((4, GROUP, COLS), BF16),
            pltpu.VMEM((2 * GROUP, HALF + LANES), BF16),
            pltpu.SemaphoreType.DMA((2,)),
        ],
        in_hbm=2,
    )

    arrived = lax.all_to_all(outgoing, DP, split_axis=0, concat_axis=0)
    summed = jnp.sum(arrived.reshape(2, 2, 8, 6, LANES), axis=(0, 2))
    grad_b = jnp.pad(summed[0, :4], ((0, 3), (0, 0))) + jnp.pad(summed[1, :4], ((3, 0), (0, 0)))
    columns = summed[:, 4]
    log_total = summed[0, 5, 0]
    grad_a = lax.all_to_all(
        jnp.broadcast_to(columns[None], (16, 2, SLICE)), BLK, split_axis=0, concat_axis=0
    )
    grad_a = grad_a.transpose(2, 1, 0).reshape(SLICE, 2 * RANK)
    return -log_total / pair_total[0, 0], grad_a, grad_b.reshape(1, 7 * LANES)


def solution(mesh):
    fine = Mesh(mesh.devices.reshape(SIZES), AXES)
    in_specs = (
        P(AXES, None),
        P(AXES, None),
        P(AXES, None),
        P(None, DP, BLK),
        P(),
        P(None, BLK),
        P(BLK),
    )
    out_specs = (P(), P(DP, None), P(DP, BLK))
    return jax.shard_map(
        on_device, mesh=fine, in_specs=in_specs, out_specs=out_specs, check_vma=False
    )
```

```python
import functools

import jax
import jax.numpy as jnp
from jax import lax
from jax.experimental import pallas as pl
from jax.experimental.pallas import tpu as pltpu
from jax.sharding import Mesh, PartitionSpec as P

SEQS = 4
ROWS = 12
RANK = 16
WIDTH = 4096
DPO_BETA = 0.1
LOSS_SCALE = 1024.0
F32 = jnp.float32
BF16 = jnp.bfloat16

AXES = ("yh", "x", "c", "z", "yl")
SIZES = (4, 4, 2, 8, 2)
DP = ("yh", "x", "c")
BLK = ("z", "yl")
SWAP = [(0, 1), (1, 0)]

SLICE = 128
HALF = WIDTH // 2
LANES = 128
UNITS = 896
MAIN = 640
SIDE = UNITS - MAIN
PIECE = SLICE + 16
GROUP = 192
BLOCKS = GROUP // ROWS
CONTRACT_LAST = (((1,), (1,)), ((), ()))


def swapped(value, axis, index):
    far = lax.ppermute(value, axis, SWAP)
    return jnp.where(index == 0, jnp.stack([value, far]), jnp.stack([far, value]))


def split(value, terms):
    parts = []
    for _ in range(terms):
        parts.append(value.astype(BF16))
        value = value - parts[-1].astype(F32)
    return parts


def dot(a, b, dims=(((1,), (0,)), ((), ()))):
    return lax.dot_general(a, b, dims, preferred_element_type=F32)


def early_products(place, down, p0, r1, l1, r2, l2, r3, l3, far_z, s0, s1, s2, s3, out, tok_out, tok, w, sems):
    z, yh, x = place[1], place[2], place[3]
    block = 4 * ROWS
    moves = ((0, p0), (-1, r1), (1, l1), (-2, r2), (2, l2), (-3, r3), (3, l3), (4, far_z))
    copies = []
    for n, (k, ref) in enumerate(moves):
        rows = pl.ds(pl.multiple_of(lax.rem(z + 8 + k, 8) * block, block), block)
        copies.append(pltpu.make_async_copy(ref, tok.at[rows, :], sems.at[n]))
    for j, ref in enumerate((s0, s1, s2, s3)):
        for k in range(4):
            source = lax.rem(yh + k, 4) * 4 + lax.rem(x + j, 4)
            rows = pl.ds(pl.multiple_of(source * SLICE, SLICE), SLICE)
            copies.append(
                pltpu.make_async_copy(ref.at[pl.ds(k * PIECE, SLICE), :], w.at[rows, :], sems.at[8 + 4 * j + k])
            )
    for copy in copies:
        copy.start()
    for copy in copies:
        copy.wait()
    tok_copy = pltpu.make_async_copy(tok, tok_out, sems.at[24])
    tok_copy.start()
    for n in range(2):
        part = slice(n * SIDE, (n + 1) * SIDE)
        out[:, part] = dot(tok[:, 0:HALF], w[:, part])
    out[:, 2 * SIDE :] = dot(tok[:, 0:HALF], down[...])
    tok_copy.wait()


def main_products(far, place, tok, w_in, out, rows, w, sems):
    half = 1 - place[0] if far else place[0]
    mine = pl.ds(pl.multiple_of(half * GROUP, GROUP), GROUP)
    parts = [pl.ds(n * 256, 256) for n in range(2 * MAIN // 256)]
    rows_copy = pltpu.make_async_copy(tok.at[mine, pl.ds(0, HALF)], rows, sems.at[0])
    rows_copy.start()
    copies = [
        pltpu.make_async_copy(w_in.at[:, part], w.at[:, part], sems.at[1 + n]) for n, part in enumerate(parts)
    ]
    for copy in copies:
        copy.start()
    rows_copy.wait()
    for part, copy in zip(parts, copies):
        copy.wait()
        out[:, part] = dot(rows[...], w[:, part])


def products(far, place, tok, w):
    return kernel(
        functools.partial(main_products, far),
        [((GROUP, 2 * MAIN), F32)],
        (place, tok, w),
        2 * GROUP * HALF * 2 * MAIN, 56,
        scratch=[
            pltpu.VMEM((GROUP, HALF), BF16),
            pltpu.VMEM((HALF, 2 * MAIN), BF16),
            pltpu.SemaphoreType.DMA((6,)),
        ],
        in_hbm=2,
    )[0]


def score(place, near, partner, side, b_gate, b_up, readout, signs, count, message, low_t, k_out, k, sems):
    low_b = side[:, 2 * SIDE :].astype(BF16)
    main = near[...] + partner[...]
    gate_ref = jnp.concatenate([main[:, 0:MAIN], side[:, 0:SIDE]], axis=1)
    up_ref = jnp.concatenate([main[:, MAIN:], side[:, SIDE : 2 * SIDE]], axis=1)
    gate_pol = gate_ref + dot(low_b, b_gate[...])
    up_pol = up_ref + dot(low_b, b_up[...])
    sig_ref = jax.nn.sigmoid(gate_ref)
    sig_pol = jax.nn.sigmoid(gate_pol)
    act_pol = gate_pol * sig_pol
    read = readout[...].astype(F32)
    change = act_pol * up_pol - gate_ref * sig_ref * up_ref
    k_gate = read * sig_pol * (1.0 + gate_pol * (1.0 - sig_pol)) * up_pol
    k_up = read * act_pol
    read_b = jnp.broadcast_to(readout[...], (8, UNITS))
    change_row = sum(dot(read_b, part, CONTRACT_LAST) for part in split(change, 3))
    sign = signs[place[0]]
    gaps = sum(dot(part, sign, CONTRACT_LAST) for part in split(change_row, 3))
    tail = jnp.broadcast_to(gaps[0:1, :] + count[...], (RANK, LANES))
    high, rest = split(k_gate, 2)
    k[0], k[1] = high, rest
    copies = [pltpu.make_async_copy(k.at[i], k_out.at[i], sems.at[i]) for i in range(4)]
    copies[0].start()
    copies[1].start()
    mixed = dot(b_gate[0:RANK, :], high, CONTRACT_LAST) + dot(b_gate[0:RANK, :], rest, CONTRACT_LAST)
    high, rest = split(k_up, 2)
    k[2], k[3] = high, rest
    copies[2].start()
    copies[3].start()
    mixed_up = dot(b_up[RANK : 2 * RANK, :], high, CONTRACT_LAST) + dot(b_up[RANK : 2 * RANK, :], rest, CONTRACT_LAST)
    for core in range(2):
        lines = slice(RANK * core, RANK * (core + 1))
        for i, value in enumerate((mixed, mixed_up)):
            message[lines, 2 * i, :] = value[:, 0:LANES]
            message[lines, 2 * i + 1, :] = jnp.concatenate(
                [value[:, LANES:], jnp.zeros((RANK, 2 * LANES - GROUP), F32)], axis=1
            )
        message[lines, 4, :] = tail
    low_t[...] = low_b.astype(F32).T[0 : 2 * RANK, :]
    for copy in copies:
        copy.wait()


def close(place, arrived, signs, valid, low_t, k_in, tok_in, out, total_out, k, tok, sems):
    tok_copy = pltpu.make_async_copy(tok_in, tok, sems.at[0])
    k_copy = pltpu.make_async_copy(k_in, k, sems.at[1])
    tok_copy.start()
    k_copy.start()
    core = place[0]
    sums = [jnp.sum(arrived[RANK * h : RANK * (h + 1)], axis=0) for h in range(2)]
    tails = [total[4:5, :] for total in sums]
    line = lax.broadcasted_iota(jnp.int32, (8, GROUP), 0)
    pair_total = jnp.maximum(tails[0][:, 64:65] + tails[1][:, 64:65], 1.0)
    logs, cotangents, terms = 0.0, [], []
    for h in range(2):
        logit = DPO_BETA * tails[h]
        logs = logs + jnp.sum(
            valid[h] * (jnp.minimum(logit, 0.0) - jnp.log1p(jnp.exp(-jnp.abs(logit)))), axis=1, keepdims=True
        )
        scaled = -LOSS_SCALE * DPO_BETA * valid[h] * jax.nn.sigmoid(-logit) / pair_total
        scaled = jnp.broadcast_to(scaled, (8, LANES))
        cotangent = sum(dot(part, signs[h]) for part in split(scaled, 3))
        cotangents.append(cotangent[0:1, :])
        gate, up = (
            jnp.concatenate([sums[h][i : i + 1, :], sums[h][i + 1 : i + 2, 0 : GROUP - LANES]], axis=1) for i in (0, 2)
        )
        projected = jnp.where(line == 0, gate, jnp.where(line == 1, up, 0.0)) * cotangent
        if h == 0:
            tok_copy.wait()
        terms.append(dot(projected.astype(BF16), tok[h * GROUP : (h + 1) * GROUP, 0:HALF]))
    grad_a = terms[0] + terms[1]
    own = jnp.where(core == 0, cotangents[0], cotangents[1])
    high, rest = split(low_t[...] * own, 2)
    k_copy.wait()
    gate = dot(high[0:RANK], k[0]) + dot(high[0:RANK], k[1]) + dot(rest[0:RANK], k[0])
    up = dot(high[RANK:], k[2]) + dot(high[RANK:], k[3]) + dot(rest[RANK:], k[2])
    for i in range(UNITS // LANES):
        out[0:RANK, i, :] = gate[:, i * LANES : (i + 1) * LANES]
        out[RANK : 2 * RANK, i, :] = up[:, i * LANES : (i + 1) * LANES]
    line = lax.broadcasted_iota(jnp.int32, (2 * RANK, SLICE), 0)
    for column in range(2):
        slices = jnp.zeros((2 * RANK, SLICE), F32)
        for i in range(RANK):
            here = jnp.broadcast_to(
                grad_a[column : column + 1, i * SLICE : (i + 1) * SLICE], (2 * RANK, SLICE)
            )
            slices = jnp.where(line == 2 * i + core, here, slices)
        out[:, 7 + column, :] = slices
    out[:, 9, :] = jnp.broadcast_to(0.5 * logs, (2 * RANK, LANES))
    total_out[...] = jnp.broadcast_to(pair_total, (8, LANES))


def kernel(function, shapes, arguments, flops, grant, scratch=(), in_hbm=0, out_hbm=0):
    vmem = pl.BlockSpec(memory_space=pltpu.VMEM)
    smem = pl.BlockSpec(memory_space=pltpu.SMEM)
    hbm = pl.BlockSpec(memory_space=pltpu.HBM)
    return pl.pallas_call(
        function,
        out_shape=tuple(jax.ShapeDtypeStruct(*s) for s in shapes),
        in_specs=[smem] + [vmem] * (len(arguments) - 1 - in_hbm) + [hbm] * in_hbm,
        out_specs=(vmem,) * (len(shapes) - out_hbm) + (hbm,) * out_hbm,
        scratch_shapes=list(scratch),
        compiler_params=pltpu.CompilerParams(vmem_limit_bytes=grant * 1024 * 1024),
        cost_estimate=pl.CostEstimate(flops=flops, bytes_accessed=10_000_000, transcendentals=0),
    )(*arguments)


def along(value, axis, k):
    n = lax.axis_size(axis)
    return lax.ppermute(value, axis, [(i, (i + k) % n) for i in range(n)])


def fetch(value, axis, k):
    n = lax.axis_size(axis)
    return lax.ppermute(value, axis, [((i + k) % n, i) for i in range(n)])


def on_device(tokens, sequence_labels, response_mask, frozen, down, up, readout):
    yh, x, core, z, yl = (lax.axis_index(a) for a in AXES)
    place = jnp.stack([core, z, yh, x]).astype(jnp.int32)
    code = jnp.where(response_mask > 0, sequence_labels, SEQS)

    main = jnp.concatenate([frozen[0, :, :MAIN], frozen[1, :, :MAIN]], axis=1)
    w_main = lax.all_gather(main, ("yh", "x"), axis=0, tiled=True)

    by_core = tokens.reshape(ROWS, 16, 2, SLICE).transpose(2, 0, 1, 3).reshape(2, ROWS, HALF)
    code_lanes = jnp.pad(code.reshape(ROWS, 1).astype(BF16), ((0, 0), (0, LANES - 1)))
    keep = jnp.concatenate([jnp.where(core == 0, by_core[0], by_core[1]), code_lanes], axis=1)
    give = jnp.concatenate([jnp.where(core == 0, by_core[1], by_core[0]), code_lanes], axis=1)
    take = lax.ppermute(give, "c", SWAP)
    pair = jnp.where(
        core == 0, jnp.concatenate([keep, take], axis=0), jnp.concatenate([take, keep], axis=0)
    )
    four = swapped(pair, "yl", yl).reshape(4 * ROWS, HALF + LANES)
    ring = [four, along(four, "z", 1), along(four, "z", -1)]

    has = [jnp.max((code == q).astype(F32)) for q in range(SEQS)]
    count_rows = jnp.broadcast_to((has[0] * has[1] + has[2] * has[3]).astype(BF16), (16, 2 * SIDE))
    piece = jnp.concatenate(
        [jnp.concatenate([frozen[0, :, MAIN:], frozen[1, :, MAIN:]], axis=1), count_rows], axis=0
    )
    pieces = [piece] + [fetch(piece, "yh", k) for k in (1, 2, 3)]
    ring[1], ring[2], *pieces = lax.optimization_barrier((ring[1], ring[2], *pieces))
    stack = jnp.concatenate(pieces, axis=0)
    stacks = [stack] + [fetch(stack, "x", j) for j in (1, 2, 3)]
    for step in range(2):
        ring += [along(ring[-2], "z", 1), along(ring[-1], "z", -1)]
    ring.append(along(ring[-2], "z", 1))
    count = sum(jnp.sum(p.reshape(4, PIECE, 2 * SIDE)[:, SLICE, 0].astype(F32)) for p in stacks)
    count_lanes = jnp.where(jnp.arange(LANES) == 64, count, 0.0).reshape(1, LANES)

    down_half = down.reshape(16, 2, SLICE, 2 * RANK)
    down_half = jnp.where(core == 0, down_half[:, 0], down_half[:, 1]).reshape(HALF, 2 * RANK)
    down_half = jnp.pad(down_half, ((0, 0), (0, LANES - 2 * RANK)))
    side, tok = kernel(
        early_products,
        [((2 * GROUP, 2 * SIDE + LANES), F32), ((2 * GROUP, HALF + LANES), BF16)],
        (place, down_half, *ring, *stacks),
        4 * GROUP * HALF * (2 * SIDE + LANES), 56,
        scratch=[
            pltpu.VMEM((2 * GROUP, HALF + LANES), BF16),
            pltpu.VMEM((HALF, 2 * SIDE), BF16),
            pltpu.SemaphoreType.DMA((25,)),
        ],
        in_hbm=12, out_hbm=1,
    )
    side = side.reshape(2, GROUP, 2 * SIDE + LANES)
    side_far = jnp.where(core == 0, side[1], side[0])
    side = jnp.where(core == 0, side[0], side[1]) + lax.ppermute(side_far, "c", SWAP)

    b_gate = jnp.pad(up[:RANK], ((0, LANES - RANK), (0, 0)))
    b_up = jnp.pad(up[RANK:], ((RANK, LANES - 2 * RANK), (0, 0)))
    read = readout.reshape(1, UNITS)

    codes = tok[:, HALF].astype(jnp.int32).reshape(2, GROUP)
    pair_of = jnp.arange(LANES, dtype=jnp.int32)
    block_of = jnp.arange(GROUP, dtype=jnp.int32) // ROWS
    inside = (pair_of[:, None] // 2 == block_of[None, :])[None]
    chosen = inside & (codes[:, None, :] == 2 * (pair_of % 2)[None, :, None])
    rejected = inside & (codes[:, None, :] == 2 * (pair_of % 2)[None, :, None] + 1)
    signs = chosen.astype(BF16) - rejected.astype(BF16)
    valid = (jnp.any(chosen, axis=2) & jnp.any(rejected, axis=2)).astype(F32).reshape(2, 1, LANES)

    w_main, side, b_gate, b_up, read, signs, valid, count_lanes = lax.optimization_barrier(
        (w_main, side, b_gate, b_up, read, signs, valid, count_lanes)
    )
    far = products(True, place, tok, w_main)
    partner = lax.ppermute(far, "c", SWAP)
    near = products(False, place, tok, w_main)
    message, low_t, k = kernel(
        score,
        [((2 * RANK, 5, LANES), F32), ((2 * RANK, GROUP), F32), ((4, GROUP, UNITS), BF16)],
        (place, near, partner, side, b_gate, b_up, read, signs, count_lanes),
        8 * GROUP * UNITS * LANES, 16,
        scratch=[pltpu.VMEM((4, GROUP, UNITS), BF16), pltpu.SemaphoreType.DMA((4,))],
        out_hbm=1,
    )
    arrived = lax.all_to_all(message, ("c", "z", "yl"), split_axis=0, concat_axis=0)
    outgoing, pair_total = kernel(
        close,
        [((2 * RANK, 10, LANES), F32), ((8, LANES), F32)],
        (place, arrived, signs, valid, low_t, k, tok),
        16 * GROUP * HALF * 2, 16,
        scratch=[
            pltpu.VMEM((4, GROUP, UNITS), BF16),
            pltpu.VMEM((2 * GROUP, HALF + LANES), BF16),
            pltpu.SemaphoreType.DMA((2,)),
        ],
        in_hbm=2,
    )

    summed = jnp.sum(lax.all_to_all(outgoing, DP, split_axis=0, concat_axis=0), axis=0)
    grad_a = lax.all_to_all(
        jnp.broadcast_to(summed[None, 7:9], (16, 2, SLICE)), BLK, split_axis=0, concat_axis=0
    )
    grad_a = grad_a.transpose(2, 1, 0).reshape(SLICE, 2 * RANK)
    return -summed[9, 0] / pair_total[0, 0], grad_a, summed[:7].reshape(1, UNITS)


def solution(mesh):
    fine = Mesh(mesh.devices.reshape(SIZES), AXES)
    in_specs = (
        P(AXES, None),
        P(AXES, None),
        P(AXES, None),
        P(None, DP, BLK),
        P(),
        P(None, BLK),
        P(BLK),
    )
    out_specs = (P(), P(DP, None), P(DP, BLK))
    return jax.shard_map(
        on_device, mesh=fine, in_specs=in_specs, out_specs=out_specs, check_vma=False
    )
```

```python
import functools

import jax
import jax.numpy as jnp
from jax import lax
from jax.experimental import pallas as pl
from jax.experimental.pallas import tpu as pltpu
from jax.sharding import Mesh, PartitionSpec as P

SEQS = 4
ROWS = 12
RANK = 16
WIDTH = 4096
DPO_BETA = 0.1
LOSS_SCALE = 1024.0
F32 = jnp.float32
BF16 = jnp.bfloat16

AXES = ("yh", "x", "c", "z", "yl")
SIZES = (4, 4, 2, 8, 2)
DP = ("yh", "x", "c")
BLK = ("z", "yl")
SWAP = [(0, 1), (1, 0)]

SLICE = 128
HALF = WIDTH // 2
LANES = 128
UNITS = 896
MAIN = 640
SIDE = UNITS - MAIN
PIECE = SLICE + 16
COLUMNS = 512
GROUP = 192
BLOCKS = GROUP // ROWS
CONTRACT_LAST = (((1,), (1,)), ((), ()))


def swapped(value, axis, index):
    far = lax.ppermute(value, axis, SWAP)
    return jnp.where(index == 0, jnp.stack([value, far]), jnp.stack([far, value]))


def split(value, terms):
    parts = []
    for _ in range(terms):
        parts.append(value.astype(BF16))
        value = value - parts[-1].astype(F32)
    return parts


def dot(a, b, dims=(((1,), (0,)), ((), ()))):
    return lax.dot_general(a, b, dims, preferred_element_type=F32)


def early_products(place, down, p0, r1, l1, r2, l2, r3, l3, far_z, s0, s1, s2, s3, out, tok_out, tok, w, sems):
    z, yh, x = place[1], place[2], place[3]
    block = 4 * ROWS
    moves = ((0, p0), (-1, r1), (1, l1), (-2, r2), (2, l2), (-3, r3), (3, l3), (4, far_z))
    copies = []
    for n, (k, ref) in enumerate(moves):
        rows = pl.ds(pl.multiple_of(lax.rem(z + 8 + k, 8) * block, block), block)
        copies.append(pltpu.make_async_copy(ref, tok.at[rows, :], sems.at[n]))
    for j, ref in enumerate((s0, s1, s2, s3)):
        for k in range(4):
            source = lax.rem(yh + k, 4) * 4 + lax.rem(x + j, 4)
            rows = pl.ds(pl.multiple_of(source * SLICE, SLICE), SLICE)
            copies.append(
                pltpu.make_async_copy(ref.at[pl.ds(k * PIECE, SLICE), :], w.at[rows, :], sems.at[8 + 4 * j + k])
            )
    for copy in copies:
        copy.start()
    for copy in copies:
        copy.wait()
    tok_copy = pltpu.make_async_copy(tok, tok_out, sems.at[24])
    tok_copy.start()
    for n in range(2):
        part = slice(n * SIDE, (n + 1) * SIDE)
        out[:, part] = dot(tok[:, 0:HALF], w[:, part])
    out[:, 2 * SIDE :] = dot(tok[:, 0:HALF], down[...])
    tok_copy.wait()


def main_products(place, tok, w_in, far, near, rows, w, sems):
    halves = [
        pl.ds(pl.multiple_of(half * GROUP, GROUP), GROUP) for half in (1 - place[0], place[0])
    ]
    chunks = [pl.ds(n * COLUMNS, COLUMNS) for n in range(HALF // COLUMNS)]
    row_copies = [
        pltpu.make_async_copy(tok.at[half, pl.ds(0, HALF)], rows.at[n], sems.at[n]) for n, half in enumerate(halves)
    ]
    copies = [
        pltpu.make_async_copy(w_in.at[chunk, :], w.at[chunk, :], sems.at[2 + n]) for n, chunk in enumerate(chunks)
    ]
    row_copies[0].start()
    copies[0].start()
    row_copies[1].start()
    for copy in copies[1:]:
        copy.start()
    for copy in row_copies:
        copy.wait()
    for n, (chunk, copy) in enumerate(zip(chunks, copies)):
        copy.wait()
        for at, out in enumerate((far, near)):
            term = dot(rows[at, :, chunk], w[chunk, :])
            out[...] = term if n == 0 else out[...] + term


def products(place, tok, w):
    return kernel(
        main_products,
        [((GROUP, 2 * MAIN), F32)] * 2,
        (place, tok, w),
        4 * GROUP * HALF * 2 * MAIN, 56,
        scratch=[
            pltpu.VMEM((2, GROUP, HALF), BF16),
            pltpu.VMEM((HALF, 2 * MAIN), BF16),
            pltpu.SemaphoreType.DMA((2 + HALF // COLUMNS,)),
        ],
        in_hbm=2,
    )


def score(place, near, partner, side, b_gate, b_up, readout, signs, count, message, low_t, k_out, k, sems):
    low_b = side[:, 2 * SIDE :].astype(BF16)
    main = near[...] + partner[...]
    gate_ref = jnp.concatenate([main[:, 0:MAIN], side[:, 0:SIDE]], axis=1)
    up_ref = jnp.concatenate([main[:, MAIN:], side[:, SIDE : 2 * SIDE]], axis=1)
    gate_pol = gate_ref + dot(low_b, b_gate[...])
    up_pol = up_ref + dot(low_b, b_up[...])
    sig_ref = jax.nn.sigmoid(gate_ref)
    sig_pol = jax.nn.sigmoid(gate_pol)
    act_pol = gate_pol * sig_pol
    read = readout[...].astype(F32)
    change = act_pol * up_pol - gate_ref * sig_ref * up_ref
    k_gate = read * sig_pol * (1.0 + gate_pol * (1.0 - sig_pol)) * up_pol
    k_up = read * act_pol
    read_b = jnp.broadcast_to(readout[...], (8, UNITS))
    change_row = sum(dot(read_b, part, CONTRACT_LAST) for part in split(change, 3))
    sign = signs[place[0]]
    gaps = sum(dot(part, sign, CONTRACT_LAST) for part in split(change_row, 3))
    tail = jnp.broadcast_to(gaps[0:1, :] + count[...], (RANK, LANES))
    high, rest = split(k_gate, 2)
    k[0], k[1] = high, rest
    copies = [pltpu.make_async_copy(k.at[i], k_out.at[i], sems.at[i]) for i in range(4)]
    copies[0].start()
    copies[1].start()
    mixed = dot(b_gate[0:RANK, :], high, CONTRACT_LAST) + dot(b_gate[0:RANK, :], rest, CONTRACT_LAST)
    high, rest = split(k_up, 2)
    k[2], k[3] = high, rest
    copies[2].start()
    copies[3].start()
    mixed_up = dot(b_up[RANK : 2 * RANK, :], high, CONTRACT_LAST) + dot(b_up[RANK : 2 * RANK, :], rest, CONTRACT_LAST)
    message[...] = jnp.zeros_like(message)
    for core in range(2):
        lines = slice(RANK * core, RANK * (core + 1))
        for i, value in enumerate((mixed, mixed_up)):
            message[lines, 0, 2 * i * LANES : 2 * i * LANES + GROUP] = value
        message[lines, 0, 4 * LANES :] = tail
    low_t[...] = low_b.astype(F32).T[0 : 2 * RANK, :]
    for copy in copies:
        copy.wait()


def close(place, arrived, signs, valid, low_t, k_in, tok_in, out, total_out, k, tok, sems):
    tok_copy = pltpu.make_async_copy(tok_in, tok, sems.at[0])
    k_copy = pltpu.make_async_copy(k_in, k, sems.at[1])
    tok_copy.start()
    k_copy.start()
    core = place[0]
    sums = [jnp.sum(arrived[RANK * h : RANK * (h + 1)], axis=0) for h in range(2)]
    tails = [total[:, 4 * LANES :] for total in sums]
    line = lax.broadcasted_iota(jnp.int32, (8, GROUP), 0)
    pair_total = jnp.maximum(tails[0][:, 64:65] + tails[1][:, 64:65], 1.0)
    logs, cotangents, terms = 0.0, [], []
    for h in range(2):
        logit = DPO_BETA * tails[h]
        logs = logs + jnp.sum(
            valid[h] * (jnp.minimum(logit, 0.0) - jnp.log1p(jnp.exp(-jnp.abs(logit)))), axis=1, keepdims=True
        )
        scaled = -LOSS_SCALE * DPO_BETA * valid[h] * jax.nn.sigmoid(-logit) / pair_total
        scaled = jnp.broadcast_to(scaled, (8, LANES))
        cotangent = sum(dot(part, signs[h]) for part in split(scaled, 3))
        cotangents.append(cotangent[0:1, :])
        gate, up = (sums[h][:, i * LANES : i * LANES + GROUP] for i in (0, 2))
        projected = jnp.where(line == 0, gate, jnp.where(line == 1, up, 0.0)) * cotangent
        if h == 0:
            tok_copy.wait()
        terms.append(dot(projected.astype(BF16), tok[h * GROUP : (h + 1) * GROUP, 0:HALF]))
    grad_a = terms[0] + terms[1]
    own = jnp.where(core == 0, cotangents[0], cotangents[1])
    high, rest = split(low_t[...] * own, 2)
    k_copy.wait()
    gate = dot(high[0:RANK], k[0]) + dot(high[0:RANK], k[1]) + dot(rest[0:RANK], k[0])
    up = dot(high[RANK:], k[2]) + dot(high[RANK:], k[3]) + dot(rest[RANK:], k[2])
    out[0:RANK, 0, 0:UNITS] = gate
    out[RANK : 2 * RANK, 0, 0:UNITS] = up
    line = lax.broadcasted_iota(jnp.int32, (2 * RANK, SLICE), 0)
    for column in range(2):
        slices = jnp.zeros((2 * RANK, SLICE), F32)
        for i in range(RANK):
            here = jnp.broadcast_to(
                grad_a[column : column + 1, i * SLICE : (i + 1) * SLICE], (2 * RANK, SLICE)
            )
            slices = jnp.where(line == 2 * i + core, here, slices)
        out[:, 0, UNITS + column * SLICE : UNITS + (column + 1) * SLICE] = slices
    out[:, 0, UNITS + 2 * SLICE :] = jnp.broadcast_to(0.5 * logs, (2 * RANK, LANES))
    total_out[...] = jnp.broadcast_to(pair_total, (8, LANES))


def kernel(function, shapes, arguments, flops, grant, scratch=(), in_hbm=0, out_hbm=0):
    vmem = pl.BlockSpec(memory_space=pltpu.VMEM)
    smem = pl.BlockSpec(memory_space=pltpu.SMEM)
    hbm = pl.BlockSpec(memory_space=pltpu.HBM)
    return pl.pallas_call(
        function,
        out_shape=tuple(jax.ShapeDtypeStruct(*s) for s in shapes),
        in_specs=[smem] + [vmem] * (len(arguments) - 1 - in_hbm) + [hbm] * in_hbm,
        out_specs=(vmem,) * (len(shapes) - out_hbm) + (hbm,) * out_hbm,
        scratch_shapes=list(scratch),
        compiler_params=pltpu.CompilerParams(vmem_limit_bytes=grant * 1024 * 1024),
        cost_estimate=pl.CostEstimate(flops=flops, bytes_accessed=10_000_000, transcendentals=0),
    )(*arguments)


def along(value, axis, k):
    n = lax.axis_size(axis)
    return lax.ppermute(value, axis, [(i, (i + k) % n) for i in range(n)])


def fetch(value, axis, k):
    n = lax.axis_size(axis)
    return lax.ppermute(value, axis, [((i + k) % n, i) for i in range(n)])


def on_device(tokens, sequence_labels, response_mask, frozen, down, up, readout):
    yh, x, core, z, yl = (lax.axis_index(a) for a in AXES)
    place = jnp.stack([core, z, yh, x]).astype(jnp.int32)
    code = jnp.where(response_mask > 0, sequence_labels, SEQS)

    main = jnp.concatenate([frozen[0, :, :MAIN], frozen[1, :, :MAIN]], axis=1)
    w_main = lax.all_gather(main, ("yh", "x"), axis=0, tiled=True)

    by_core = tokens.reshape(ROWS, 16, 2, SLICE).transpose(2, 0, 1, 3).reshape(2, ROWS, HALF)
    code_lanes = jnp.pad(code.reshape(ROWS, 1).astype(BF16), ((0, 0), (0, LANES - 1)))
    keep = jnp.concatenate([jnp.where(core == 0, by_core[0], by_core[1]), code_lanes], axis=1)
    give = jnp.concatenate([jnp.where(core == 0, by_core[1], by_core[0]), code_lanes], axis=1)
    take = lax.ppermute(give, "c", SWAP)
    pair = jnp.where(
        core == 0, jnp.concatenate([keep, take], axis=0), jnp.concatenate([take, keep], axis=0)
    )
    four = swapped(pair, "yl", yl).reshape(4 * ROWS, HALF + LANES)
    has = [jnp.max((code == q).astype(F32)) for q in range(SEQS)]
    count_rows = jnp.broadcast_to((has[0] * has[1] + has[2] * has[3]).astype(BF16), (16, 2 * SIDE))
    piece = jnp.concatenate(
        [jnp.concatenate([frozen[0, :, MAIN:], frozen[1, :, MAIN:]], axis=1), count_rows], axis=0
    )
    pieces = [piece] + [fetch(piece, "yh", k) for k in (1, 2, 3)]
    four, *pieces = lax.optimization_barrier((four, *pieces))
    ring = [four, along(four, "z", 1), along(four, "z", -1)]
    stack = jnp.concatenate(pieces, axis=0)
    stacks = [stack] + [fetch(stack, "x", j) for j in (1, 2, 3)]
    for step in range(2):
        ring += [along(ring[-2], "z", 1), along(ring[-1], "z", -1)]
    ring.append(along(four, "z", 4))
    count = sum(jnp.sum(p.reshape(4, PIECE, 2 * SIDE)[:, SLICE, 0].astype(F32)) for p in stacks)
    count_lanes = jnp.where(jnp.arange(LANES) == 64, count, 0.0).reshape(1, LANES)

    down_half = down.reshape(16, 2, SLICE, 2 * RANK)
    down_half = jnp.where(core == 0, down_half[:, 0], down_half[:, 1]).reshape(HALF, 2 * RANK)
    down_half = jnp.pad(down_half, ((0, 0), (0, LANES - 2 * RANK)))
    side, tok = kernel(
        early_products,
        [((2 * GROUP, 2 * SIDE + LANES), F32), ((2 * GROUP, HALF + LANES), BF16)],
        (place, down_half, *ring, *stacks),
        4 * GROUP * HALF * (2 * SIDE + LANES), 56,
        scratch=[
            pltpu.VMEM((2 * GROUP, HALF + LANES), BF16),
            pltpu.VMEM((HALF, 2 * SIDE), BF16),
            pltpu.SemaphoreType.DMA((25,)),
        ],
        in_hbm=12, out_hbm=1,
    )
    side = side.reshape(2, GROUP, 2 * SIDE + LANES)
    side_far = jnp.where(core == 0, side[1], side[0])
    side = jnp.where(core == 0, side[0], side[1]) + lax.ppermute(side_far, "c", SWAP)

    b_gate = jnp.pad(up[:RANK], ((0, LANES - RANK), (0, 0)))
    b_up = jnp.pad(up[RANK:], ((RANK, LANES - 2 * RANK), (0, 0)))
    read = readout.reshape(1, UNITS)

    codes = tok[:, HALF].astype(jnp.int32).reshape(2, GROUP)
    pair_of = jnp.arange(LANES, dtype=jnp.int32)
    block_of = jnp.arange(GROUP, dtype=jnp.int32) // ROWS
    inside = (pair_of[:, None] // 2 == block_of[None, :])[None]
    chosen = inside & (codes[:, None, :] == 2 * (pair_of % 2)[None, :, None])
    rejected = inside & (codes[:, None, :] == 2 * (pair_of % 2)[None, :, None] + 1)
    signs = chosen.astype(BF16) - rejected.astype(BF16)
    valid = (jnp.any(chosen, axis=2) & jnp.any(rejected, axis=2)).astype(F32).reshape(2, 1, LANES)

    w_main, side, b_gate, b_up, read, signs, valid, count_lanes = lax.optimization_barrier(
        (w_main, side, b_gate, b_up, read, signs, valid, count_lanes)
    )
    far, near = products(place, tok, w_main)
    partner = lax.ppermute(far, "c", SWAP)
    message, low_t, k = kernel(
        score,
        [((2 * RANK, 1, 5 * LANES), F32), ((2 * RANK, GROUP), F32), ((4, GROUP, UNITS), BF16)],
        (place, near, partner, side, b_gate, b_up, read, signs, count_lanes),
        8 * GROUP * UNITS * LANES, 16,
        scratch=[pltpu.VMEM((4, GROUP, UNITS), BF16), pltpu.SemaphoreType.DMA((4,))],
        out_hbm=1,
    )
    arrived = lax.all_to_all(message, ("c", "z", "yl"), split_axis=0, concat_axis=0)
    outgoing, pair_total = kernel(
        close,
        [((2 * RANK, 1, UNITS + 2 * SLICE + LANES), F32), ((8, LANES), F32)],
        (place, arrived, signs, valid, low_t, k, tok),
        16 * GROUP * HALF * 2, 16,
        scratch=[
            pltpu.VMEM((4, GROUP, UNITS), BF16),
            pltpu.VMEM((2 * GROUP, HALF + LANES), BF16),
            pltpu.SemaphoreType.DMA((2,)),
        ],
        in_hbm=2,
    )

    summed = jnp.sum(lax.all_to_all(outgoing, DP, split_axis=0, concat_axis=0), axis=0)
    columns = summed[:, UNITS : UNITS + 2 * SLICE].reshape(1, 2, SLICE)
    grad_a = lax.all_to_all(
        jnp.broadcast_to(columns, (16, 2, SLICE)), BLK, split_axis=0, concat_axis=0
    )
    grad_a = grad_a.transpose(2, 1, 0).reshape(SLICE, 2 * RANK)
    return -summed[0, UNITS + 2 * SLICE] / pair_total[0, 0], grad_a, summed[:, :UNITS]


def solution(mesh):
    fine = Mesh(mesh.devices.reshape(SIZES), AXES)
    in_specs = (
        P(AXES, None),
        P(AXES, None),
        P(AXES, None),
        P(None, DP, BLK),
        P(),
        P(None, BLK),
        P(BLK),
    )
    out_specs = (P(), P(DP, None), P(DP, BLK))
    return jax.shard_map(
        on_device, mesh=fine, in_specs=in_specs, out_specs=out_specs, check_vma=False
    )
```

```python
import functools

import jax
import jax.numpy as jnp
from jax import lax
from jax.experimental import pallas as pl
from jax.experimental.pallas import tpu as pltpu
from jax.sharding import Mesh, PartitionSpec as P

SEQS = 4
ROWS = 12
RANK = 16
WIDTH = 4096
DPO_BETA = 0.1
LOSS_SCALE = 1024.0
F32 = jnp.float32
BF16 = jnp.bfloat16

AXES = ("yh", "x", "c", "z", "yl")
SIZES = (4, 4, 2, 8, 2)
DP = ("yh", "x", "c")
BLK = ("z", "yl")
SWAP = [(0, 1), (1, 0)]

SLICE = 128
HALF = WIDTH // 2
LANES = 128
UNITS = 896
MAIN = 640
SIDE = UNITS - MAIN
PIECE = SLICE + 16
COLUMNS = 512
GROUP = 192
BLOCKS = GROUP // ROWS
CONTRACT_LAST = (((1,), (1,)), ((), ()))


def swapped(value, axis, index):
    far = lax.ppermute(value, axis, SWAP)
    return jnp.where(index == 0, jnp.stack([value, far]), jnp.stack([far, value]))


def split(value, terms):
    parts = []
    for _ in range(terms):
        parts.append(value.astype(BF16))
        value = value - parts[-1].astype(F32)
    return parts


def dot(a, b, dims=(((1,), (0,)), ((), ()))):
    return lax.dot_general(a, b, dims, preferred_element_type=F32)


def early_products(place, down, p0, r1, l1, r2, l2, r3, l3, far_z, s0, s1, s2, s3, far, near, tok_out, tok, w, sems):
    z, yh, x = place[1], place[2], place[3]
    block = 4 * ROWS
    moves = ((0, p0), (-1, r1), (1, l1), (-2, r2), (2, l2), (-3, r3), (3, l3), (4, far_z))
    copies = []
    for n, (k, ref) in enumerate(moves):
        rows = pl.ds(pl.multiple_of(lax.rem(z + 8 + k, 8) * block, block), block)
        copies.append(pltpu.make_async_copy(ref, tok.at[rows, :], sems.at[n]))
    for j, ref in enumerate((s0, s1, s2, s3)):
        for k in range(4):
            source = lax.rem(yh + k, 4) * 4 + lax.rem(x + j, 4)
            rows = pl.ds(pl.multiple_of(source * SLICE, SLICE), SLICE)
            copies.append(
                pltpu.make_async_copy(ref.at[pl.ds(k * PIECE, SLICE), :], w.at[rows, :], sems.at[8 + 4 * j + k])
            )
    for copy in copies:
        copy.start()
    for copy in copies:
        copy.wait()
    tok_copy = pltpu.make_async_copy(tok, tok_out, sems.at[24])
    tok_copy.start()
    for half, out in ((1 - place[0], far), (place[0], near)):
        rows = pl.ds(pl.multiple_of(half * GROUP, GROUP), GROUP)
        for n in range(2):
            part = slice(n * SIDE, (n + 1) * SIDE)
            out[:, part] = dot(tok[rows, 0:HALF], w[:, part])
        out[:, 2 * SIDE :] = dot(tok[rows, 0:HALF], down[...])
    tok_copy.wait()


def main_products(place, tok, w_in, far, near, rows, w, sems):
    halves = [
        pl.ds(pl.multiple_of(half * GROUP, GROUP), GROUP) for half in (1 - place[0], place[0])
    ]
    chunks = [pl.ds(n * COLUMNS, COLUMNS) for n in range(HALF // COLUMNS)]
    row_copies = [
        pltpu.make_async_copy(tok.at[half, pl.ds(0, HALF)], rows.at[n], sems.at[n]) for n, half in enumerate(halves)
    ]
    copies = [
        pltpu.make_async_copy(w_in.at[chunk, :], w.at[chunk, :], sems.at[2 + n]) for n, chunk in enumerate(chunks)
    ]
    row_copies[0].start()
    copies[0].start()
    row_copies[1].start()
    for copy in copies[1:]:
        copy.start()
    for copy in row_copies:
        copy.wait()
    for n, (chunk, copy) in enumerate(zip(chunks, copies)):
        copy.wait()
        for at, out in enumerate((far, near)):
            term = dot(rows[at, :, chunk], w[chunk, :])
            out[...] = term if n == 0 else out[...] + term


def products(place, tok, w):
    return kernel(
        main_products,
        [((GROUP, 2 * MAIN), F32)] * 2,
        (place, tok, w),
        4 * GROUP * HALF * 2 * MAIN, 56,
        scratch=[
            pltpu.VMEM((2, GROUP, HALF), BF16),
            pltpu.VMEM((HALF, 2 * MAIN), BF16),
            pltpu.SemaphoreType.DMA((2 + HALF // COLUMNS,)),
        ],
        in_hbm=2,
    )


def score(place, partner, side_near, side_partner, b_gate, b_up, readout, signs, count, near_in, message, low_t, k_out, k,
          near, sems):
    near_copy = pltpu.make_async_copy(near_in, near, sems.at[4])
    near_copy.start()
    side = side_near[...] + side_partner[...]
    low_b = side[:, 2 * SIDE :].astype(BF16)
    near_copy.wait()
    main = near[...] + partner[...]
    gate_ref = jnp.concatenate([main[:, 0:MAIN], side[:, 0:SIDE]], axis=1)
    up_ref = jnp.concatenate([main[:, MAIN:], side[:, SIDE : 2 * SIDE]], axis=1)
    gate_pol = gate_ref + dot(low_b, b_gate[...])
    up_pol = up_ref + dot(low_b, b_up[...])
    sig_ref = jax.nn.sigmoid(gate_ref)
    sig_pol = jax.nn.sigmoid(gate_pol)
    act_pol = gate_pol * sig_pol
    read = readout[...].astype(F32)
    change = act_pol * up_pol - gate_ref * sig_ref * up_ref
    k_gate = read * sig_pol * (1.0 + gate_pol * (1.0 - sig_pol)) * up_pol
    k_up = read * act_pol
    read_b = jnp.broadcast_to(readout[...], (8, UNITS))
    change_row = sum(dot(read_b, part, CONTRACT_LAST) for part in split(change, 3))
    sign = signs[place[0]]
    gaps = sum(dot(part, sign, CONTRACT_LAST) for part in split(change_row, 3))
    tail = jnp.broadcast_to(gaps[0:1, :] + count[...], (RANK, LANES))
    high, rest = split(k_gate, 2)
    k[0], k[1] = high, rest
    copies = [pltpu.make_async_copy(k.at[i], k_out.at[i], sems.at[i]) for i in range(4)]
    copies[0].start()
    copies[1].start()
    mixed = dot(b_gate[0:RANK, :], high, CONTRACT_LAST) + dot(b_gate[0:RANK, :], rest, CONTRACT_LAST)
    high, rest = split(k_up, 2)
    k[2], k[3] = high, rest
    copies[2].start()
    copies[3].start()
    mixed_up = dot(b_up[RANK : 2 * RANK, :], high, CONTRACT_LAST) + dot(b_up[RANK : 2 * RANK, :], rest, CONTRACT_LAST)
    message[...] = jnp.zeros_like(message)
    for core in range(2):
        lines = slice(RANK * core, RANK * (core + 1))
        for i, value in enumerate((mixed, mixed_up)):
            message[lines, 0, 2 * i * LANES : 2 * i * LANES + GROUP] = value
        message[lines, 0, 4 * LANES :] = tail
    low_t[...] = low_b.astype(F32).T[0 : 2 * RANK, :]
    for copy in copies:
        copy.wait()


def close(place, arrived, signs, valid, low_t, k_in, tok_in, out, total_out, k, tok, sems):
    tok_copy = pltpu.make_async_copy(tok_in, tok, sems.at[0])
    k_copy = pltpu.make_async_copy(k_in, k, sems.at[1])
    tok_copy.start()
    k_copy.start()
    core = place[0]
    sums = [jnp.sum(arrived[RANK * h : RANK * (h + 1)], axis=0) for h in range(2)]
    tails = [total[:, 4 * LANES :] for total in sums]
    line = lax.broadcasted_iota(jnp.int32, (8, GROUP), 0)
    pair_total = jnp.maximum(tails[0][:, 64:65] + tails[1][:, 64:65], 1.0)
    logs, cotangents, terms = 0.0, [], []
    for h in range(2):
        logit = DPO_BETA * tails[h]
        logs = logs + jnp.sum(
            valid[h] * (jnp.minimum(logit, 0.0) - jnp.log1p(jnp.exp(-jnp.abs(logit)))), axis=1, keepdims=True
        )
        scaled = -LOSS_SCALE * DPO_BETA * valid[h] * jax.nn.sigmoid(-logit) / pair_total
        scaled = jnp.broadcast_to(scaled, (8, LANES))
        cotangent = sum(dot(part, signs[h]) for part in split(scaled, 3))
        cotangents.append(cotangent[0:1, :])
        gate, up = (sums[h][:, i * LANES : i * LANES + GROUP] for i in (0, 2))
        projected = jnp.where(line == 0, gate, jnp.where(line == 1, up, 0.0)) * cotangent
        if h == 0:
            tok_copy.wait()
        terms.append(dot(projected.astype(BF16), tok[h * GROUP : (h + 1) * GROUP, 0:HALF]))
    grad_a = terms[0] + terms[1]
    own = jnp.where(core == 0, cotangents[0], cotangents[1])
    high, rest = split(low_t[...] * own, 2)
    k_copy.wait()
    gate = dot(high[0:RANK], k[0]) + dot(high[0:RANK], k[1]) + dot(rest[0:RANK], k[0])
    up = dot(high[RANK:], k[2]) + dot(high[RANK:], k[3]) + dot(rest[RANK:], k[2])
    out[0:RANK, 0, 0:UNITS] = gate
    out[RANK : 2 * RANK, 0, 0:UNITS] = up
    line = lax.broadcasted_iota(jnp.int32, (2 * RANK, SLICE), 0)
    for column in range(2):
        slices = jnp.zeros((2 * RANK, SLICE), F32)
        for i in range(RANK):
            here = jnp.broadcast_to(
                grad_a[column : column + 1, i * SLICE : (i + 1) * SLICE], (2 * RANK, SLICE)
            )
            slices = jnp.where(line == 2 * i + core, here, slices)
        out[:, 0, UNITS + column * SLICE : UNITS + (column + 1) * SLICE] = slices
    out[:, 0, UNITS + 2 * SLICE :] = jnp.broadcast_to(0.5 * logs, (2 * RANK, LANES))
    total_out[...] = jnp.broadcast_to(pair_total, (8, LANES))


def kernel(function, shapes, arguments, flops, grant, scratch=(), in_hbm=0, out_hbm=0):
    vmem = pl.BlockSpec(memory_space=pltpu.VMEM)
    smem = pl.BlockSpec(memory_space=pltpu.SMEM)
    hbm = pl.BlockSpec(memory_space=pltpu.HBM)
    return pl.pallas_call(
        function,
        out_shape=tuple(jax.ShapeDtypeStruct(*s) for s in shapes),
        in_specs=[smem] + [vmem] * (len(arguments) - 1 - in_hbm) + [hbm] * in_hbm,
        out_specs=(vmem,) * (len(shapes) - out_hbm) + (hbm,) * out_hbm,
        scratch_shapes=list(scratch),
        compiler_params=pltpu.CompilerParams(vmem_limit_bytes=grant * 1024 * 1024),
        cost_estimate=pl.CostEstimate(flops=flops, bytes_accessed=10_000_000, transcendentals=0),
    )(*arguments)


def along(value, axis, k):
    n = lax.axis_size(axis)
    return lax.ppermute(value, axis, [(i, (i + k) % n) for i in range(n)])


def fetch(value, axis, k):
    n = lax.axis_size(axis)
    return lax.ppermute(value, axis, [((i + k) % n, i) for i in range(n)])


def on_device(tokens, sequence_labels, response_mask, frozen, down, up, readout):
    yh, x, core, z, yl = (lax.axis_index(a) for a in AXES)
    place = jnp.stack([core, z, yh, x]).astype(jnp.int32)
    code = jnp.where(response_mask > 0, sequence_labels, SEQS)

    main = jnp.concatenate([frozen[0, :, :MAIN], frozen[1, :, :MAIN]], axis=1)
    main, tokens, frozen = lax.optimization_barrier((main, tokens, frozen))
    w_main = lax.all_gather(main, ("yh", "x"), axis=0, tiled=True)

    by_core = tokens.reshape(ROWS, 16, 2, SLICE).transpose(2, 0, 1, 3).reshape(2, ROWS, HALF)
    code_lanes = jnp.pad(code.reshape(ROWS, 1).astype(BF16), ((0, 0), (0, LANES - 1)))
    keep = jnp.concatenate([jnp.where(core == 0, by_core[0], by_core[1]), code_lanes], axis=1)
    give = jnp.concatenate([jnp.where(core == 0, by_core[1], by_core[0]), code_lanes], axis=1)
    take = lax.ppermute(give, "c", SWAP)
    pair = jnp.where(
        core == 0, jnp.concatenate([keep, take], axis=0), jnp.concatenate([take, keep], axis=0)
    )
    four = swapped(pair, "yl", yl).reshape(4 * ROWS, HALF + LANES)
    has = [jnp.max((code == q).astype(F32)) for q in range(SEQS)]
    count_rows = jnp.broadcast_to((has[0] * has[1] + has[2] * has[3]).astype(BF16), (16, 2 * SIDE))
    piece = jnp.concatenate(
        [jnp.concatenate([frozen[0, :, MAIN:], frozen[1, :, MAIN:]], axis=1), count_rows], axis=0
    )
    pieces = [piece] + [fetch(piece, "yh", k) for k in (1, 2, 3)]
    ring = [four, along(four, "z", 1), along(four, "z", -1)]
    stack = jnp.concatenate(pieces, axis=0)
    stacks = [stack] + [fetch(stack, "x", j) for j in (1, 2, 3)]
    for step in range(2):
        ring += [along(ring[-2], "z", 1), along(ring[-1], "z", -1)]
    ring.append(along(four, "z", 4))
    ring[5], ring[6], stacks[1] = lax.optimization_barrier((ring[5], ring[6], stacks[1]))
    count = sum(jnp.sum(p.reshape(4, PIECE, 2 * SIDE)[:, SLICE, 0].astype(F32)) for p in stacks)
    count_lanes = jnp.where(jnp.arange(LANES) == 64, count, 0.0).reshape(1, LANES)

    down_half = down.reshape(16, 2, SLICE, 2 * RANK)
    down_half = jnp.where(core == 0, down_half[:, 0], down_half[:, 1]).reshape(HALF, 2 * RANK)
    down_half = jnp.pad(down_half, ((0, 0), (0, LANES - 2 * RANK)))
    side_far, side, tok = kernel(
        early_products,
        [((GROUP, 2 * SIDE + LANES), F32)] * 2 + [((2 * GROUP, HALF + LANES), BF16)],
        (place, down_half, *ring, *stacks),
        4 * GROUP * HALF * (2 * SIDE + LANES), 56,
        scratch=[
            pltpu.VMEM((2 * GROUP, HALF + LANES), BF16),
            pltpu.VMEM((HALF, 2 * SIDE), BF16),
            pltpu.SemaphoreType.DMA((25,)),
        ],
        in_hbm=12, out_hbm=1,
    )
    side_partner = lax.ppermute(side_far, "c", SWAP)

    b_gate = jnp.pad(up[:RANK], ((0, LANES - RANK), (0, 0)))
    b_up = jnp.pad(up[RANK:], ((RANK, LANES - 2 * RANK), (0, 0)))
    read = readout.reshape(1, UNITS)

    codes = tok[:, HALF].astype(jnp.int32).reshape(2, GROUP)
    pair_of = jnp.arange(LANES, dtype=jnp.int32)
    block_of = jnp.arange(GROUP, dtype=jnp.int32) // ROWS
    inside = (pair_of[:, None] // 2 == block_of[None, :])[None]
    chosen = inside & (codes[:, None, :] == 2 * (pair_of % 2)[None, :, None])
    rejected = inside & (codes[:, None, :] == 2 * (pair_of % 2)[None, :, None] + 1)
    signs = chosen.astype(BF16) - rejected.astype(BF16)
    valid = (jnp.any(chosen, axis=2) & jnp.any(rejected, axis=2)).astype(F32).reshape(2, 1, LANES)

    w_main, b_gate, b_up, read, count_lanes = lax.optimization_barrier(
        (w_main, b_gate, b_up, read, count_lanes)
    )
    far, near = products(place, tok, w_main)
    partner = lax.ppermute(far, "c", SWAP)
    message, low_t, k = kernel(
        score,
        [((2 * RANK, 1, 5 * LANES), F32), ((2 * RANK, GROUP), F32), ((4, GROUP, UNITS), BF16)],
        (place, partner, side, side_partner, b_gate, b_up, read, signs, count_lanes, near),
        8 * GROUP * UNITS * LANES, 16,
        scratch=[
            pltpu.VMEM((4, GROUP, UNITS), BF16),
            pltpu.VMEM((GROUP, 2 * MAIN), F32),
            pltpu.SemaphoreType.DMA((5,)),
        ],
        in_hbm=1, out_hbm=1,
    )
    arrived = lax.all_to_all(message, ("c", "z", "yl"), split_axis=0, concat_axis=0)
    outgoing, pair_total = kernel(
        close,
        [((2 * RANK, 1, UNITS + 2 * SLICE + LANES), F32), ((8, LANES), F32)],
        (place, arrived, signs, valid, low_t, k, tok),
        16 * GROUP * HALF * 2, 16,
        scratch=[
            pltpu.VMEM((4, GROUP, UNITS), BF16),
            pltpu.VMEM((2 * GROUP, HALF + LANES), BF16),
            pltpu.SemaphoreType.DMA((2,)),
        ],
        in_hbm=2,
    )

    summed = jnp.sum(lax.all_to_all(outgoing, DP, split_axis=0, concat_axis=0), axis=0)
    columns = summed[:, UNITS : UNITS + 2 * SLICE].reshape(1, 2, SLICE)
    grad_a = lax.all_to_all(
        jnp.broadcast_to(columns, (16, 2, SLICE)), BLK, split_axis=0, concat_axis=0
    )
    grad_a = grad_a.transpose(2, 1, 0).reshape(SLICE, 2 * RANK)
    return -summed[0, UNITS + 2 * SLICE] / pair_total[0, 0], grad_a, summed[:, :UNITS]


def solution(mesh):
    fine = Mesh(mesh.devices.reshape(SIZES), AXES)
    in_specs = (
        P(AXES, None),
        P(AXES, None),
        P(AXES, None),
        P(None, DP, BLK),
        P(),
        P(None, BLK),
        P(BLK),
    )
    out_specs = (P(), P(DP, None), P(DP, BLK))
    return jax.shard_map(
        on_device, mesh=fine, in_specs=in_specs, out_specs=out_specs, check_vma=False
    )
```

```python
import functools

import jax
import jax.numpy as jnp
from jax import lax
from jax.experimental import pallas as pl
from jax.experimental.pallas import tpu as pltpu
from jax.sharding import Mesh, PartitionSpec as P

SEQS = 4
ROWS = 12
RANK = 16
WIDTH = 4096
DPO_BETA = 0.1
LOSS_SCALE = 1024.0
F32 = jnp.float32
BF16 = jnp.bfloat16

AXES = ("yh", "x", "c", "z", "yl")
SIZES = (4, 4, 2, 8, 2)
DP = ("yh", "x", "c")
BLK = ("z", "yl")
SWAP = [(0, 1), (1, 0)]

SLICE = 128
HALF = WIDTH // 2
LANES = 128
UNITS = 896
MAIN = 640
SIDE = UNITS - MAIN
PIECE = SLICE + 16
COLUMNS = 512
GROUP = 192
BLOCKS = GROUP // ROWS
CONTRACT_LAST = (((1,), (1,)), ((), ()))


def swapped(value, axis, index):
    far = lax.ppermute(value, axis, SWAP)
    return jnp.where(index == 0, jnp.stack([value, far]), jnp.stack([far, value]))


def split(value, terms):
    parts = []
    for _ in range(terms):
        parts.append(value.astype(BF16))
        value = value - parts[-1].astype(F32)
    return parts


def dot(a, b, dims=(((1,), (0,)), ((), ()))):
    return lax.dot_general(a, b, dims, preferred_element_type=F32)


def early_products(place, down, p0, r1, l1, r2, l2, r3, l3, far_z, s0, s1, s2, s3, far, near, tok_out, tok, w, sems):
    z, yh, x = place[1], place[2], place[3]
    block = 4 * ROWS
    moves = ((0, p0), (-1, r1), (1, l1), (-2, r2), (2, l2), (-3, r3), (3, l3), (4, far_z))
    copies = []
    for n, (k, ref) in enumerate(moves):
        rows = pl.ds(pl.multiple_of(lax.rem(z + 8 + k, 8) * block, block), block)
        copies.append(pltpu.make_async_copy(ref, tok.at[rows, :], sems.at[n]))
    for j, ref in enumerate((s0, s1, s2, s3)):
        for k in range(4):
            source = lax.rem(yh + k, 4) * 4 + lax.rem(x + j, 4)
            rows = pl.ds(pl.multiple_of(source * SLICE, SLICE), SLICE)
            copies.append(
                pltpu.make_async_copy(ref.at[pl.ds(k * PIECE, SLICE), :], w.at[rows, :], sems.at[8 + 4 * j + k])
            )
    for copy in copies:
        copy.start()
    for copy in copies:
        copy.wait()
    tok_copy = pltpu.make_async_copy(tok, tok_out, sems.at[24])
    tok_copy.start()
    for half, out in ((1 - place[0], far), (place[0], near)):
        rows = pl.ds(pl.multiple_of(half * GROUP, GROUP), GROUP)
        for n in range(2):
            part = slice(n * SIDE, (n + 1) * SIDE)
            out[:, part] = dot(tok[rows, 0:HALF], w[:, part])
        out[:, 2 * SIDE :] = dot(tok[rows, 0:HALF], down[...])
    tok_copy.wait()


def main_products(place, tok, w_in, far, near, rows, w, sems):
    halves = [
        pl.ds(pl.multiple_of(half * GROUP, GROUP), GROUP) for half in (1 - place[0], place[0])
    ]
    chunks = [pl.ds(n * COLUMNS, COLUMNS) for n in range(HALF // COLUMNS)]
    row_copies = [
        pltpu.make_async_copy(tok.at[half, pl.ds(0, HALF)], rows.at[n], sems.at[n]) for n, half in enumerate(halves)
    ]
    copies = [
        pltpu.make_async_copy(w_in.at[chunk, :], w.at[chunk, :], sems.at[2 + n]) for n, chunk in enumerate(chunks)
    ]
    row_copies[0].start()
    copies[0].start()
    row_copies[1].start()
    for copy in copies[1:]:
        copy.start()
    for copy in row_copies:
        copy.wait()
    for n, (chunk, copy) in enumerate(zip(chunks, copies)):
        copy.wait()
        for at, out in enumerate((far, near)):
            term = dot(rows[at, :, chunk], w[chunk, :])
            out[...] = term if n == 0 else out[...] + term


def products(place, tok, w):
    return kernel(
        main_products,
        [((GROUP, 2 * MAIN), F32)] * 2,
        (place, tok, w),
        4 * GROUP * HALF * 2 * MAIN, 56,
        scratch=[
            pltpu.VMEM((2, GROUP, HALF), BF16),
            pltpu.VMEM((HALF, 2 * MAIN), BF16),
            pltpu.SemaphoreType.DMA((2 + HALF // COLUMNS,)),
        ],
        in_hbm=2,
    )


def score(place, partner, readout, count, near_in, side_in, side_partner_in, gate_in, up_in, signs_in, message, low_t,
          k_out, k, near, side_near, side_partner, b_gate, b_up, signs, sems):
    fetches = [
        pltpu.make_async_copy(source, target, sems.at[4 + n])
        for n, (source, target) in enumerate(
            (
                (side_in, side_near), (side_partner_in, side_partner), (near_in, near),
                (gate_in, b_gate), (up_in, b_up), (signs_in, signs),
            )
        )
    ]
    for copy in fetches:
        copy.start()
    for copy in fetches:
        copy.wait()
    side = side_near[...] + side_partner[...]
    low_b = side[:, 2 * SIDE :].astype(BF16)
    main = near[...] + partner[...]
    gate_ref = jnp.concatenate([main[:, 0:MAIN], side[:, 0:SIDE]], axis=1)
    up_ref = jnp.concatenate([main[:, MAIN:], side[:, SIDE : 2 * SIDE]], axis=1)
    gate_pol = gate_ref + dot(low_b, b_gate[...])
    up_pol = up_ref + dot(low_b, b_up[...])
    sig_ref = jax.nn.sigmoid(gate_ref)
    sig_pol = jax.nn.sigmoid(gate_pol)
    act_pol = gate_pol * sig_pol
    read = readout[...].astype(F32)
    change = act_pol * up_pol - gate_ref * sig_ref * up_ref
    k_gate = read * sig_pol * (1.0 + gate_pol * (1.0 - sig_pol)) * up_pol
    k_up = read * act_pol
    read_b = jnp.broadcast_to(readout[...], (8, UNITS))
    change_row = sum(dot(read_b, part, CONTRACT_LAST) for part in split(change, 3))
    sign = signs[place[0]]
    gaps = sum(dot(part, sign, CONTRACT_LAST) for part in split(change_row, 3))
    tail = jnp.broadcast_to(gaps[0:1, :] + count[...], (RANK, LANES))
    high, rest = split(k_gate, 2)
    k[0], k[1] = high, rest
    copies = [pltpu.make_async_copy(k.at[i], k_out.at[i], sems.at[i]) for i in range(4)]
    copies[0].start()
    copies[1].start()
    mixed = dot(b_gate[0:RANK, :], high, CONTRACT_LAST) + dot(b_gate[0:RANK, :], rest, CONTRACT_LAST)
    high, rest = split(k_up, 2)
    k[2], k[3] = high, rest
    copies[2].start()
    copies[3].start()
    mixed_up = dot(b_up[RANK : 2 * RANK, :], high, CONTRACT_LAST) + dot(b_up[RANK : 2 * RANK, :], rest, CONTRACT_LAST)
    message[...] = jnp.zeros_like(message)
    for core in range(2):
        lines = slice(RANK * core, RANK * (core + 1))
        for i, value in enumerate((mixed, mixed_up)):
            message[lines, 0, 2 * i * LANES : 2 * i * LANES + GROUP] = value
        message[lines, 0, 4 * LANES :] = tail
    low_t[...] = low_b.astype(F32).T[0 : 2 * RANK, :]
    for copy in copies:
        copy.wait()


def close(place, arrived, signs, valid, low_t, k_in, tok_in, out, total_out, k, tok, sems):
    tok_copy = pltpu.make_async_copy(tok_in, tok, sems.at[0])
    k_copy = pltpu.make_async_copy(k_in, k, sems.at[1])
    tok_copy.start()
    k_copy.start()
    core = place[0]
    sums = [jnp.sum(arrived[RANK * h : RANK * (h + 1)], axis=0) for h in range(2)]
    tails = [total[:, 4 * LANES :] for total in sums]
    line = lax.broadcasted_iota(jnp.int32, (8, GROUP), 0)
    pair_total = jnp.maximum(tails[0][:, 64:65] + tails[1][:, 64:65], 1.0)
    logs, cotangents, terms = 0.0, [], []
    for h in range(2):
        logit = DPO_BETA * tails[h]
        logs = logs + jnp.sum(
            valid[h] * (jnp.minimum(logit, 0.0) - jnp.log1p(jnp.exp(-jnp.abs(logit)))), axis=1, keepdims=True
        )
        scaled = -LOSS_SCALE * DPO_BETA * valid[h] * jax.nn.sigmoid(-logit) / pair_total
        scaled = jnp.broadcast_to(scaled, (8, LANES))
        cotangent = sum(dot(part, signs[h]) for part in split(scaled, 3))
        cotangents.append(cotangent[0:1, :])
        gate, up = (sums[h][:, i * LANES : i * LANES + GROUP] for i in (0, 2))
        projected = jnp.where(line == 0, gate, jnp.where(line == 1, up, 0.0)) * cotangent
        if h == 0:
            tok_copy.wait()
        terms.append(dot(projected.astype(BF16), tok[h * GROUP : (h + 1) * GROUP, 0:HALF]))
    grad_a = terms[0] + terms[1]
    own = jnp.where(core == 0, cotangents[0], cotangents[1])
    high, rest = split(low_t[...] * own, 2)
    k_copy.wait()
    gate = dot(high[0:RANK], k[0]) + dot(high[0:RANK], k[1]) + dot(rest[0:RANK], k[0])
    up = dot(high[RANK:], k[2]) + dot(high[RANK:], k[3]) + dot(rest[RANK:], k[2])
    out[0:RANK, 0, 0:UNITS] = gate
    out[RANK : 2 * RANK, 0, 0:UNITS] = up
    line = lax.broadcasted_iota(jnp.int32, (2 * RANK, SLICE), 0)
    for column in range(2):
        slices = jnp.zeros((2 * RANK, SLICE), F32)
        for i in range(RANK):
            here = jnp.broadcast_to(
                grad_a[column : column + 1, i * SLICE : (i + 1) * SLICE], (2 * RANK, SLICE)
            )
            slices = jnp.where(line == 2 * i + core, here, slices)
        out[:, 0, UNITS + column * SLICE : UNITS + (column + 1) * SLICE] = slices
    out[:, 0, UNITS + 2 * SLICE :] = jnp.broadcast_to(0.5 * logs, (2 * RANK, LANES))
    total_out[...] = jnp.broadcast_to(pair_total, (8, LANES))


def kernel(function, shapes, arguments, flops, grant, scratch=(), in_hbm=0, out_hbm=0):
    vmem = pl.BlockSpec(memory_space=pltpu.VMEM)
    smem = pl.BlockSpec(memory_space=pltpu.SMEM)
    hbm = pl.BlockSpec(memory_space=pltpu.HBM)
    return pl.pallas_call(
        function,
        out_shape=tuple(jax.ShapeDtypeStruct(*s) for s in shapes),
        in_specs=[smem] + [vmem] * (len(arguments) - 1 - in_hbm) + [hbm] * in_hbm,
        out_specs=(vmem,) * (len(shapes) - out_hbm) + (hbm,) * out_hbm,
        scratch_shapes=list(scratch),
        compiler_params=pltpu.CompilerParams(vmem_limit_bytes=grant * 1024 * 1024),
        cost_estimate=pl.CostEstimate(flops=flops, bytes_accessed=10_000_000, transcendentals=0),
    )(*arguments)


def along(value, axis, k):
    n = lax.axis_size(axis)
    return lax.ppermute(value, axis, [(i, (i + k) % n) for i in range(n)])


def fetch(value, axis, k):
    n = lax.axis_size(axis)
    return lax.ppermute(value, axis, [((i + k) % n, i) for i in range(n)])


def on_device(tokens, sequence_labels, response_mask, frozen, down, up, readout):
    yh, x, core, z, yl = (lax.axis_index(a) for a in AXES)
    place = jnp.stack([core, z, yh, x]).astype(jnp.int32)
    code = jnp.where(response_mask > 0, sequence_labels, SEQS)

    main = jnp.concatenate([frozen[0, :, :MAIN], frozen[1, :, :MAIN]], axis=1)
    main, tokens, frozen = lax.optimization_barrier((main, tokens, frozen))
    w_main = lax.all_gather(main, ("yh", "x"), axis=0, tiled=True)

    by_core = tokens.reshape(ROWS, 16, 2, SLICE).transpose(2, 0, 1, 3).reshape(2, ROWS, HALF)
    code_lanes = jnp.pad(code.reshape(ROWS, 1).astype(BF16), ((0, 0), (0, LANES - 1)))
    keep = jnp.concatenate([jnp.where(core == 0, by_core[0], by_core[1]), code_lanes], axis=1)
    give = jnp.concatenate([jnp.where(core == 0, by_core[1], by_core[0]), code_lanes], axis=1)
    take = lax.ppermute(give, "c", SWAP)
    pair = jnp.where(
        core == 0, jnp.concatenate([keep, take], axis=0), jnp.concatenate([take, keep], axis=0)
    )
    four = swapped(pair, "yl", yl).reshape(4 * ROWS, HALF + LANES)
    has = [jnp.max((code == q).astype(F32)) for q in range(SEQS)]
    count_rows = jnp.broadcast_to((has[0] * has[1] + has[2] * has[3]).astype(BF16), (16, 2 * SIDE))
    piece = jnp.concatenate(
        [jnp.concatenate([frozen[0, :, MAIN:], frozen[1, :, MAIN:]], axis=1), count_rows], axis=0
    )
    pieces = [piece] + [fetch(piece, "yh", k) for k in (1, 2, 3)]
    ring = [four, along(four, "z", 1), along(four, "z", -1)]
    stack = jnp.concatenate(pieces, axis=0)
    stacks = [stack] + [fetch(stack, "x", j) for j in (1, 2, 3)]
    for step in range(2):
        ring += [along(ring[-2], "z", 1), along(ring[-1], "z", -1)]
    ring.append(along(ring[-2], "z", 1))
    ring[7], *stacks[1:] = lax.optimization_barrier((ring[7], *stacks[1:]))
    count = sum(jnp.sum(p.reshape(4, PIECE, 2 * SIDE)[:, SLICE, 0].astype(F32)) for p in stacks)
    count_lanes = jnp.where(jnp.arange(LANES) == 64, count, 0.0).reshape(1, LANES)

    down_half = down.reshape(16, 2, SLICE, 2 * RANK)
    down_half = jnp.where(core == 0, down_half[:, 0], down_half[:, 1]).reshape(HALF, 2 * RANK)
    down_half = jnp.pad(down_half, ((0, 0), (0, LANES - 2 * RANK)))
    side_far, side, tok = kernel(
        early_products,
        [((GROUP, 2 * SIDE + LANES), F32)] * 2 + [((2 * GROUP, HALF + LANES), BF16)],
        (place, down_half, *ring, *stacks),
        4 * GROUP * HALF * (2 * SIDE + LANES), 56,
        scratch=[
            pltpu.VMEM((2 * GROUP, HALF + LANES), BF16),
            pltpu.VMEM((HALF, 2 * SIDE), BF16),
            pltpu.SemaphoreType.DMA((25,)),
        ],
        in_hbm=12, out_hbm=1,
    )
    side_partner = lax.ppermute(side_far, "c", SWAP)

    b_gate = jnp.pad(up[:RANK], ((0, LANES - RANK), (0, 0)))
    b_up = jnp.pad(up[RANK:], ((RANK, LANES - 2 * RANK), (0, 0)))
    read = readout.reshape(1, UNITS)

    codes = tok[:, HALF].astype(jnp.int32).reshape(2, GROUP)
    pair_of = jnp.arange(LANES, dtype=jnp.int32)
    block_of = jnp.arange(GROUP, dtype=jnp.int32) // ROWS
    inside = (pair_of[:, None] // 2 == block_of[None, :])[None]
    chosen = inside & (codes[:, None, :] == 2 * (pair_of % 2)[None, :, None])
    rejected = inside & (codes[:, None, :] == 2 * (pair_of % 2)[None, :, None] + 1)
    signs = chosen.astype(BF16) - rejected.astype(BF16)
    valid = (jnp.any(chosen, axis=2) & jnp.any(rejected, axis=2)).astype(F32).reshape(2, 1, LANES)

    w_main, side, side_partner, b_gate, b_up, read, signs, valid, count_lanes = lax.optimization_barrier(
        (w_main, side, side_partner, b_gate, b_up, read, signs, valid, count_lanes)
    )
    far, near = products(place, tok, w_main)
    partner = lax.ppermute(far, "c", SWAP)
    message, low_t, k = kernel(
        score,
        [((2 * RANK, 1, 5 * LANES), F32), ((2 * RANK, GROUP), F32), ((4, GROUP, UNITS), BF16)],
        (place, partner, read, count_lanes, near, side, side_partner, b_gate, b_up, signs),
        8 * GROUP * UNITS * LANES, 56,
        scratch=[
            pltpu.VMEM((4, GROUP, UNITS), BF16),
            pltpu.VMEM((GROUP, 2 * MAIN), F32),
            pltpu.VMEM((GROUP, 2 * SIDE + LANES), F32),
            pltpu.VMEM((GROUP, 2 * SIDE + LANES), F32),
            pltpu.VMEM((LANES, UNITS), BF16),
            pltpu.VMEM((LANES, UNITS), BF16),
            pltpu.VMEM((2, LANES, GROUP), BF16),
            pltpu.SemaphoreType.DMA((10,)),
        ],
        in_hbm=6, out_hbm=1,
    )
    arrived = lax.all_to_all(message, ("c", "z", "yl"), split_axis=0, concat_axis=0)
    outgoing, pair_total = kernel(
        close,
        [((2 * RANK, 1, UNITS + 2 * SLICE + LANES), F32), ((8, LANES), F32)],
        (place, arrived, signs, valid, low_t, k, tok),
        16 * GROUP * HALF * 2, 16,
        scratch=[
            pltpu.VMEM((4, GROUP, UNITS), BF16),
            pltpu.VMEM((2 * GROUP, HALF + LANES), BF16),
            pltpu.SemaphoreType.DMA((2,)),
        ],
        in_hbm=2,
    )

    summed = jnp.sum(lax.all_to_all(outgoing, DP, split_axis=0, concat_axis=0), axis=0)
    columns = summed[:, UNITS : UNITS + 2 * SLICE].reshape(1, 2, SLICE)
    grad_a = lax.all_to_all(
        jnp.broadcast_to(columns, (16, 2, SLICE)), BLK, split_axis=0, concat_axis=0
    )
    grad_a = grad_a.transpose(2, 1, 0).reshape(SLICE, 2 * RANK)
    return -summed[0, UNITS + 2 * SLICE] / pair_total[0, 0], grad_a, summed[:, :UNITS]


def solution(mesh):
    fine = Mesh(mesh.devices.reshape(SIZES), AXES)
    in_specs = (
        P(AXES, None),
        P(AXES, None),
        P(AXES, None),
        P(None, DP, BLK),
        P(),
        P(None, BLK),
        P(BLK),
    )
    out_specs = (P(), P(DP, None), P(DP, BLK))
    return jax.shard_map(
        on_device, mesh=fine, in_specs=in_specs, out_specs=out_specs, check_vma=False
    )
```

```python
import functools

import jax
import jax.numpy as jnp
from jax import lax
from jax.experimental import pallas as pl
from jax.experimental.pallas import tpu as pltpu
from jax.sharding import Mesh, PartitionSpec as P

SEQS = 4
ROWS = 12
RANK = 16
WIDTH = 4096
DPO_BETA = 0.1
LOSS_SCALE = 1024.0
F32 = jnp.float32
BF16 = jnp.bfloat16

AXES = ("yh", "x", "c", "z", "yl")
SIZES = (4, 4, 2, 8, 2)
DP = ("yh", "x", "c")
BLK = ("z", "yl")
SWAP = [(0, 1), (1, 0)]

SLICE = 128
HALF = WIDTH // 2
LANES = 128
UNITS = 896
MAIN = 640
SIDE = UNITS - MAIN
PIECE = SLICE + 16
COLUMNS = 512
GROUP = 192
BLOCKS = GROUP // ROWS
CONTRACT_LAST = (((1,), (1,)), ((), ()))


def swapped(value, axis, index):
    far = lax.ppermute(value, axis, SWAP)
    return jnp.where(index == 0, jnp.stack([value, far]), jnp.stack([far, value]))


def split(value, terms):
    parts = []
    for _ in range(terms):
        parts.append(value.astype(BF16))
        value = value - parts[-1].astype(F32)
    return parts


def dot(a, b, dims=(((1,), (0,)), ((), ()))):
    return lax.dot_general(a, b, dims, preferred_element_type=F32)


def early_products(place, down, p0, r1, l1, r2, l2, r3, l3, far_z, s0, s1, s2, s3, far, near, count,
                   tok_out, tok, w, counts, sems):
    z, yh, x = place[1], place[2], place[3]
    block = 4 * ROWS
    moves = ((0, p0), (-1, r1), (1, l1), (-2, r2), (2, l2), (-3, r3), (3, l3), (4, far_z))
    copies = []
    for n, (k, ref) in enumerate(moves):
        rows = pl.ds(pl.multiple_of(lax.rem(z + 8 + k, 8) * block, block), block)
        copies.append(pltpu.make_async_copy(ref, tok.at[rows, :], sems.at[n]))
    for j, ref in enumerate((s0, s1, s2, s3)):
        for k in range(4):
            source = lax.rem(yh + k, 4) * 4 + lax.rem(x + j, 4)
            rows = pl.ds(pl.multiple_of(source * SLICE, SLICE), SLICE)
            at = 4 * j + k
            copies.append(pltpu.make_async_copy(ref.at[pl.ds(k * PIECE, SLICE), :], w.at[rows, :], sems.at[8 + at]))
            spare = ref.at[pl.ds(k * PIECE + SLICE, PIECE - SLICE), pl.ds(0, LANES)]
            copies.append(pltpu.make_async_copy(spare, counts.at[at], sems.at[25 + at]))
    for copy in copies:
        copy.start()
    for copy in copies:
        copy.wait()
    tok_copy = pltpu.make_async_copy(tok, tok_out, sems.at[24])
    tok_copy.start()
    total = jnp.sum(counts[...].astype(F32), axis=0)[0:1, :]
    count[...] = jnp.where(lax.broadcasted_iota(jnp.int32, (1, LANES), 1) == 64, total, 0.0)
    for half, out in ((1 - place[0], far), (place[0], near)):
        rows = pl.ds(pl.multiple_of(half * GROUP, GROUP), GROUP)
        for n in range(2):
            part = slice(n * SIDE, (n + 1) * SIDE)
            out[:, part] = dot(tok[rows, 0:HALF], w[:, part])
        out[:, 2 * SIDE :] = dot(tok[rows, 0:HALF], down[...])
    tok_copy.wait()


def main_products(place, tok, w_in, far, near, rows, w, sems):
    halves = [
        pl.ds(pl.multiple_of(half * GROUP, GROUP), GROUP) for half in (1 - place[0], place[0])
    ]
    chunks = [pl.ds(n * COLUMNS, COLUMNS) for n in range(HALF // COLUMNS)]
    row_copies = [
        pltpu.make_async_copy(tok.at[half, pl.ds(0, HALF)], rows.at[n], sems.at[n]) for n, half in enumerate(halves)
    ]
    copies = [
        pltpu.make_async_copy(w_in.at[chunk, :], w.at[chunk, :], sems.at[2 + n]) for n, chunk in enumerate(chunks)
    ]
    row_copies[0].start()
    copies[0].start()
    row_copies[1].start()
    for copy in copies[1:]:
        copy.start()
    for copy in row_copies:
        copy.wait()
    for n, (chunk, copy) in enumerate(zip(chunks, copies)):
        copy.wait()
        for at, out in enumerate((far, near)):
            term = dot(rows[at, :, chunk], w[chunk, :])
            out[...] = term if n == 0 else out[...] + term


def products(place, tok, w):
    return kernel(
        main_products,
        [((GROUP, 2 * MAIN), F32)] * 2,
        (place, tok, w),
        4 * GROUP * HALF * 2 * MAIN, 56,
        scratch=[
            pltpu.VMEM((2, GROUP, HALF), BF16),
            pltpu.VMEM((HALF, 2 * MAIN), BF16),
            pltpu.SemaphoreType.DMA((2 + HALF // COLUMNS,)),
        ],
        in_hbm=2,
    )


def score(place, near, partner, side, b_gate, b_up, readout, signs, count, message, low_t, k_out, k, sems):
    low_b = side[:, 2 * SIDE :].astype(BF16)
    main = near[...] + partner[...]
    gate_ref = jnp.concatenate([main[:, 0:MAIN], side[:, 0:SIDE]], axis=1)
    up_ref = jnp.concatenate([main[:, MAIN:], side[:, SIDE : 2 * SIDE]], axis=1)
    gate_pol = gate_ref + dot(low_b, b_gate[...])
    up_pol = up_ref + dot(low_b, b_up[...])
    sig_ref = jax.nn.sigmoid(gate_ref)
    sig_pol = jax.nn.sigmoid(gate_pol)
    act_pol = gate_pol * sig_pol
    read = readout[...].astype(F32)
    change = act_pol * up_pol - gate_ref * sig_ref * up_ref
    k_gate = read * sig_pol * (1.0 + gate_pol * (1.0 - sig_pol)) * up_pol
    k_up = read * act_pol
    read_b = jnp.broadcast_to(readout[...], (8, UNITS))
    change_row = sum(dot(read_b, part, CONTRACT_LAST) for part in split(change, 3))
    sign = signs[place[0]]
    gaps = sum(dot(part, sign, CONTRACT_LAST) for part in split(change_row, 3))
    tail = jnp.broadcast_to(gaps[0:1, :] + count[...], (RANK, LANES))
    high, rest = split(k_gate, 2)
    k[0], k[1] = high, rest
    copies = [pltpu.make_async_copy(k.at[i], k_out.at[i], sems.at[i]) for i in range(4)]
    copies[0].start()
    copies[1].start()
    mixed = dot(b_gate[0:RANK, :], high, CONTRACT_LAST) + dot(b_gate[0:RANK, :], rest, CONTRACT_LAST)
    high, rest = split(k_up, 2)
    k[2], k[3] = high, rest
    copies[2].start()
    copies[3].start()
    mixed_up = dot(b_up[RANK : 2 * RANK, :], high, CONTRACT_LAST) + dot(b_up[RANK : 2 * RANK, :], rest, CONTRACT_LAST)
    message[...] = jnp.zeros_like(message)
    for core in range(2):
        lines = slice(RANK * core, RANK * (core + 1))
        for i, value in enumerate((mixed, mixed_up)):
            message[lines, 0, 2 * i * LANES : 2 * i * LANES + GROUP] = value
        message[lines, 0, 4 * LANES :] = tail
    low_t[...] = low_b.astype(F32).T[0 : 2 * RANK, :]
    for copy in copies:
        copy.wait()


def close(place, arrived, signs, valid, low_t, k_in, tok_in, out, total_out, k, tok, sems):
    tok_copy = pltpu.make_async_copy(tok_in, tok, sems.at[0])
    k_copy = pltpu.make_async_copy(k_in, k, sems.at[1])
    tok_copy.start()
    k_copy.start()
    core = place[0]
    sums = [jnp.sum(arrived[RANK * h : RANK * (h + 1)], axis=0) for h in range(2)]
    tails = [total[:, 4 * LANES :] for total in sums]
    line = lax.broadcasted_iota(jnp.int32, (8, GROUP), 0)
    pair_total = jnp.maximum(tails[0][:, 64:65] + tails[1][:, 64:65], 1.0)
    logs, cotangents, terms = 0.0, [], []
    for h in range(2):
        logit = DPO_BETA * tails[h]
        logs = logs + jnp.sum(
            valid[h] * (jnp.minimum(logit, 0.0) - jnp.log1p(jnp.exp(-jnp.abs(logit)))), axis=1, keepdims=True
        )
        scaled = -LOSS_SCALE * DPO_BETA * valid[h] * jax.nn.sigmoid(-logit) / pair_total
        scaled = jnp.broadcast_to(scaled, (8, LANES))
        cotangent = sum(dot(part, signs[h]) for part in split(scaled, 3))
        cotangents.append(cotangent[0:1, :])
        gate, up = (sums[h][:, i * LANES : i * LANES + GROUP] for i in (0, 2))
        projected = jnp.where(line == 0, gate, jnp.where(line == 1, up, 0.0)) * cotangent
        if h == 0:
            tok_copy.wait()
        terms.append(dot(projected.astype(BF16), tok[h * GROUP : (h + 1) * GROUP, 0:HALF]))
    grad_a = terms[0] + terms[1]
    own = jnp.where(core == 0, cotangents[0], cotangents[1])
    high, rest = split(low_t[...] * own, 2)
    k_copy.wait()
    gate = dot(high[0:RANK], k[0]) + dot(high[0:RANK], k[1]) + dot(rest[0:RANK], k[0])
    up = dot(high[RANK:], k[2]) + dot(high[RANK:], k[3]) + dot(rest[RANK:], k[2])
    out[0:RANK, 0, 0:UNITS] = gate
    out[RANK : 2 * RANK, 0, 0:UNITS] = up
    line = lax.broadcasted_iota(jnp.int32, (2 * RANK, SLICE), 0)
    for column in range(2):
        slices = jnp.zeros((2 * RANK, SLICE), F32)
        for i in range(RANK):
            here = jnp.broadcast_to(
                grad_a[column : column + 1, i * SLICE : (i + 1) * SLICE], (2 * RANK, SLICE)
            )
            slices = jnp.where(line == 2 * i + core, here, slices)
        out[:, 0, UNITS + column * SLICE : UNITS + (column + 1) * SLICE] = slices
    out[:, 0, UNITS + 2 * SLICE :] = jnp.broadcast_to(0.5 * logs, (2 * RANK, LANES))
    total_out[...] = jnp.broadcast_to(pair_total, (8, LANES))


def kernel(function, shapes, arguments, flops, grant, scratch=(), in_hbm=0, out_hbm=0):
    vmem = pl.BlockSpec(memory_space=pltpu.VMEM)
    smem = pl.BlockSpec(memory_space=pltpu.SMEM)
    hbm = pl.BlockSpec(memory_space=pltpu.HBM)
    return pl.pallas_call(
        function,
        out_shape=tuple(jax.ShapeDtypeStruct(*s) for s in shapes),
        in_specs=[smem] + [vmem] * (len(arguments) - 1 - in_hbm) + [hbm] * in_hbm,
        out_specs=(vmem,) * (len(shapes) - out_hbm) + (hbm,) * out_hbm,
        scratch_shapes=list(scratch),
        compiler_params=pltpu.CompilerParams(vmem_limit_bytes=grant * 1024 * 1024),
        cost_estimate=pl.CostEstimate(flops=flops, bytes_accessed=10_000_000, transcendentals=0),
    )(*arguments)


def along(value, axis, k):
    n = lax.axis_size(axis)
    return lax.ppermute(value, axis, [(i, (i + k) % n) for i in range(n)])


def fetch(value, axis, k):
    n = lax.axis_size(axis)
    return lax.ppermute(value, axis, [((i + k) % n, i) for i in range(n)])


def on_device(tokens, sequence_labels, response_mask, frozen, down, up, readout):
    yh, x, core, z, yl = (lax.axis_index(a) for a in AXES)
    place = jnp.stack([core, z, yh, x]).astype(jnp.int32)
    code = jnp.where(response_mask > 0, sequence_labels, SEQS)

    main = jnp.concatenate([frozen[0, :, :MAIN], frozen[1, :, :MAIN]], axis=1)
    w_main = lax.all_gather(main, ("yh", "x"), axis=0, tiled=True)

    by_core = tokens.reshape(ROWS, 16, 2, SLICE).transpose(2, 0, 1, 3).reshape(2, ROWS, HALF)
    code_lanes = jnp.pad(code.reshape(ROWS, 1).astype(BF16), ((0, 0), (0, LANES - 1)))
    keep = jnp.concatenate([jnp.where(core == 0, by_core[0], by_core[1]), code_lanes], axis=1)
    give = jnp.concatenate([jnp.where(core == 0, by_core[1], by_core[0]), code_lanes], axis=1)
    take = lax.ppermute(give, "c", SWAP)
    pair = jnp.where(
        core == 0, jnp.concatenate([keep, take], axis=0), jnp.concatenate([take, keep], axis=0)
    )
    four = swapped(pair, "yl", yl).reshape(4 * ROWS, HALF + LANES)
    has = [jnp.max((code == q).astype(F32)) for q in range(SEQS)]
    count_rows = jnp.broadcast_to((has[0] * has[1] + has[2] * has[3]).astype(BF16), (16, 2 * SIDE))
    piece = jnp.concatenate(
        [jnp.concatenate([frozen[0, :, MAIN:], frozen[1, :, MAIN:]], axis=1), count_rows], axis=0
    )
    pieces = [piece] + [fetch(piece, "yh", k) for k in (1, 2, 3)]
    four, *pieces = lax.optimization_barrier((four, *pieces))
    ring = [four, along(four, "z", 1), along(four, "z", -1)]
    stack = jnp.concatenate(pieces, axis=0)
    stacks = [stack] + [fetch(stack, "x", j) for j in (1, 2, 3)]
    for step in range(2):
        ring += [along(ring[-2], "z", 1), along(ring[-1], "z", -1)]
    ring.append(along(ring[-2], "z", 1))

    down_half = down.reshape(16, 2, SLICE, 2 * RANK)
    down_half = jnp.where(core == 0, down_half[:, 0], down_half[:, 1]).reshape(HALF, 2 * RANK)
    down_half = jnp.pad(down_half, ((0, 0), (0, LANES - 2 * RANK)))
    side_far, side, count_lanes, tok = kernel(
        early_products,
        [((GROUP, 2 * SIDE + LANES), F32)] * 2 + [((1, LANES), F32), ((2 * GROUP, HALF + LANES), BF16)],
        (place, down_half, *ring, *stacks),
        4 * GROUP * HALF * (2 * SIDE + LANES), 56,
        scratch=[
            pltpu.VMEM((2 * GROUP, HALF + LANES), BF16),
            pltpu.VMEM((HALF, 2 * SIDE), BF16),
            pltpu.VMEM((16, PIECE - SLICE, LANES), BF16),
            pltpu.SemaphoreType.DMA((41,)),
        ],
        in_hbm=12, out_hbm=1,
    )
    side = side + lax.ppermute(side_far, "c", SWAP)

    b_gate = jnp.pad(up[:RANK], ((0, LANES - RANK), (0, 0)))
    b_up = jnp.pad(up[RANK:], ((RANK, LANES - 2 * RANK), (0, 0)))
    read = readout.reshape(1, UNITS)

    codes = tok[:, HALF].astype(jnp.int32).reshape(2, GROUP)
    pair_of = jnp.arange(LANES, dtype=jnp.int32)
    block_of = jnp.arange(GROUP, dtype=jnp.int32) // ROWS
    inside = (pair_of[:, None] // 2 == block_of[None, :])[None]
    chosen = inside & (codes[:, None, :] == 2 * (pair_of % 2)[None, :, None])
    rejected = inside & (codes[:, None, :] == 2 * (pair_of % 2)[None, :, None] + 1)
    signs = chosen.astype(BF16) - rejected.astype(BF16)
    valid = (jnp.any(chosen, axis=2) & jnp.any(rejected, axis=2)).astype(F32).reshape(2, 1, LANES)

    w_main, side, b_gate, b_up, read, signs, valid, count_lanes = lax.optimization_barrier(
        (w_main, side, b_gate, b_up, read, signs, valid, count_lanes)
    )
    far, near = products(place, tok, w_main)
    partner = lax.ppermute(far, "c", SWAP)
    message, low_t, k = kernel(
        score,
        [((2 * RANK, 1, 5 * LANES), F32), ((2 * RANK, GROUP), F32), ((4, GROUP, UNITS), BF16)],
        (place, near, partner, side, b_gate, b_up, read, signs, count_lanes),
        8 * GROUP * UNITS * LANES, 16,
        scratch=[pltpu.VMEM((4, GROUP, UNITS), BF16), pltpu.SemaphoreType.DMA((4,))],
        out_hbm=1,
    )
    arrived = lax.all_to_all(message, ("c", "z", "yl"), split_axis=0, concat_axis=0)
    outgoing, pair_total = kernel(
        close,
        [((2 * RANK, 1, UNITS + 2 * SLICE + LANES), F32), ((8, LANES), F32)],
        (place, arrived, signs, valid, low_t, k, tok),
        16 * GROUP * HALF * 2, 16,
        scratch=[
            pltpu.VMEM((4, GROUP, UNITS), BF16),
            pltpu.VMEM((2 * GROUP, HALF + LANES), BF16),
            pltpu.SemaphoreType.DMA((2,)),
        ],
        in_hbm=2,
    )

    summed = jnp.sum(lax.all_to_all(outgoing, DP, split_axis=0, concat_axis=0), axis=0)
    columns = summed[:, UNITS : UNITS + 2 * SLICE].reshape(1, 2, SLICE)
    grad_a = lax.all_to_all(
        jnp.broadcast_to(columns, (16, 2, SLICE)), BLK, split_axis=0, concat_axis=0
    )
    grad_a = grad_a.transpose(2, 1, 0).reshape(SLICE, 2 * RANK)
    return -summed[0, UNITS + 2 * SLICE] / pair_total[0, 0], grad_a, summed[:, :UNITS]


def solution(mesh):
    fine = Mesh(mesh.devices.reshape(SIZES), AXES)
    in_specs = (
        P(AXES, None),
        P(AXES, None),
        P(AXES, None),
        P(None, DP, BLK),
        P(),
        P(None, BLK),
        P(BLK),
    )
    out_specs = (P(), P(DP, None), P(DP, BLK))
    return jax.shard_map(
        on_device, mesh=fine, in_specs=in_specs, out_specs=out_specs, check_vma=False
    )
```

```python
import functools

import jax
import jax.numpy as jnp
from jax import lax
from jax.experimental import pallas as pl
from jax.experimental.pallas import tpu as pltpu
from jax.sharding import Mesh, PartitionSpec as P

SEQS = 4
ROWS = 12
RANK = 16
WIDTH = 4096
DPO_BETA = 0.1
LOSS_SCALE = 1024.0
F32 = jnp.float32
BF16 = jnp.bfloat16

AXES = ("yh", "x", "c", "z", "yl")
SIZES = (4, 4, 2, 8, 2)
DP = ("yh", "x", "c")
BLK = ("z", "yl")
SWAP = [(0, 1), (1, 0)]

SLICE = 128
HALF = WIDTH // 2
LANES = 128
UNITS = 896
MAIN = 640
SIDE = UNITS - MAIN
EXTRA = 2 * SIDE + LANES
PIECE = SLICE + 16
COLUMNS = 512
GROUP = 192
BLOCKS = GROUP // ROWS
CONTRACT_LAST = (((1,), (1,)), ((), ()))


def swapped(value, axis, index):
    far = lax.ppermute(value, axis, SWAP)
    return jnp.where(index == 0, jnp.stack([value, far]), jnp.stack([far, value]))


def split(value, terms):
    parts = []
    for _ in range(terms):
        parts.append(value.astype(BF16))
        value = value - parts[-1].astype(F32)
    return parts


def dot(a, b, dims=(((1,), (0,)), ((), ()))):
    return lax.dot_general(a, b, dims, preferred_element_type=F32)


def early_products(place, down, p0, r1, l1, r2, l2, r3, l3, far_z, s0, s1, s2, s3, count, side_out,
                   tok_out, tok, w, counts, side, sems):
    z, yh, x = place[1], place[2], place[3]
    block = 4 * ROWS
    moves = ((0, p0), (-1, r1), (1, l1), (-2, r2), (2, l2), (-3, r3), (3, l3), (4, far_z))
    copies = []
    for n, (k, ref) in enumerate(moves):
        rows = pl.ds(pl.multiple_of(lax.rem(z + 8 + k, 8) * block, block), block)
        copies.append(pltpu.make_async_copy(ref, tok.at[rows, :], sems.at[n]))
    for j, ref in enumerate((s0, s1, s2, s3)):
        for k in range(4):
            source = lax.rem(yh + k, 4) * 4 + lax.rem(x + j, 4)
            rows = pl.ds(pl.multiple_of(source * SLICE, SLICE), SLICE)
            at = 4 * j + k
            copies.append(pltpu.make_async_copy(ref.at[pl.ds(k * PIECE, SLICE), :], w.at[rows, :], sems.at[8 + at]))
            spare = ref.at[pl.ds(k * PIECE + SLICE, PIECE - SLICE), pl.ds(0, LANES)]
            copies.append(pltpu.make_async_copy(spare, counts.at[at], sems.at[25 + at]))
    for copy in copies:
        copy.start()
    for copy in copies:
        copy.wait()
    tok_copy = pltpu.make_async_copy(tok, tok_out, sems.at[24])
    tok_copy.start()
    total = jnp.sum(counts[...].astype(F32), axis=0)[0:1, :]
    count[...] = jnp.where(lax.broadcasted_iota(jnp.int32, (1, LANES), 1) == 64, total, 0.0)
    for n in range(2):
        part = slice(n * SIDE, (n + 1) * SIDE)
        side[:, part] = dot(tok[:, 0:HALF], w[:, part])
    side[:, 2 * SIDE :] = dot(tok[:, 0:HALF], down[...])
    side_copy = pltpu.make_async_copy(side, side_out, sems.at[41])
    side_copy.start()
    tok_copy.wait()
    side_copy.wait()


def main_products(place, tok, side, w_in, far, near, rows, w, sems):
    chunks = [pl.ds(n * COLUMNS, COLUMNS) for n in range(HALF // COLUMNS)]
    last = len(chunks)
    starts, copies = [], []
    for n, (half, out) in enumerate(((1 - place[0], far), (place[0], near))):
        mine = pl.ds(pl.multiple_of(half * GROUP, GROUP), GROUP)
        starts.append(
            pltpu.make_async_copy(tok.at[mine, pl.ds(0, HALF)], rows.at[pl.ds(n * GROUP, GROUP), :], sems.at[n])
        )
        copies.append(pltpu.make_async_copy(side.at[mine, :], out.at[:, pl.ds(2 * MAIN, EXTRA)], sems.at[2 + n]))
    weights = [
        pltpu.make_async_copy(w_in.at[chunk, :], w.at[chunk, :], sems.at[4 + n]) for n, chunk in enumerate(chunks)
    ]
    for copy in starts + weights + copies:
        copy.start()
    for copy in starts:
        copy.wait()
    for n in range(last):
        weights[n].wait()
        term = dot(rows[:, chunks[n]], w[chunks[n], :])
        for out, part in ((far, term[0:GROUP]), (near, term[GROUP:])):
            out[:, 0 : 2 * MAIN] = part if n == 0 else out[:, 0 : 2 * MAIN] + part
    for copy in copies:
        copy.wait()


def products(place, tok, side, w):
    return kernel(
        main_products,
        [((GROUP, 2 * MAIN + EXTRA), F32)] * 2,
        (place, tok, side, w),
        4 * GROUP * HALF * 2 * MAIN, 56,
        scratch=[
            pltpu.VMEM((2 * GROUP, HALF), BF16),
            pltpu.VMEM((HALF, 2 * MAIN), BF16),
            pltpu.SemaphoreType.DMA((4 + HALF // COLUMNS,)),
        ],
        in_hbm=3,
    )


def score(place, near, partner, b_gate, b_up, readout, signs, count, message, low_t, k_out, k, sems):
    both = near[...] + partner[...]
    low_b = both[:, 2 * MAIN + 2 * SIDE :].astype(BF16)
    gate_ref = jnp.concatenate([both[:, 0:MAIN], both[:, 2 * MAIN : 2 * MAIN + SIDE]], axis=1)
    up_ref = jnp.concatenate(
        [both[:, MAIN : 2 * MAIN], both[:, 2 * MAIN + SIDE : 2 * MAIN + 2 * SIDE]], axis=1
    )
    gate_pol = gate_ref + dot(low_b, b_gate[...])
    up_pol = up_ref + dot(low_b, b_up[...])
    sig_ref = jax.nn.sigmoid(gate_ref)
    sig_pol = jax.nn.sigmoid(gate_pol)
    act_pol = gate_pol * sig_pol
    read = readout[...].astype(F32)
    change = act_pol * up_pol - gate_ref * sig_ref * up_ref
    k_gate = read * sig_pol * (1.0 + gate_pol * (1.0 - sig_pol)) * up_pol
    k_up = read * act_pol
    read_b = jnp.broadcast_to(readout[...], (8, UNITS))
    change_row = sum(dot(read_b, part, CONTRACT_LAST) for part in split(change, 3))
    sign = signs[place[0]]
    gaps = sum(dot(part, sign, CONTRACT_LAST) for part in split(change_row, 3))
    tail = jnp.broadcast_to(gaps[0:1, :] + count[...], (RANK, LANES))
    high, rest = split(k_gate, 2)
    k[0], k[1] = high, rest
    copies = [pltpu.make_async_copy(k.at[i], k_out.at[i], sems.at[i]) for i in range(4)]
    copies[0].start()
    copies[1].start()
    mixed = dot(b_gate[0:RANK, :], high, CONTRACT_LAST) + dot(b_gate[0:RANK, :], rest, CONTRACT_LAST)
    high, rest = split(k_up, 2)
    k[2], k[3] = high, rest
    copies[2].start()
    copies[3].start()
    mixed_up = dot(b_up[RANK : 2 * RANK, :], high, CONTRACT_LAST) + dot(b_up[RANK : 2 * RANK, :], rest, CONTRACT_LAST)
    message[...] = jnp.zeros_like(message)
    for core in range(2):
        lines = slice(RANK * core, RANK * (core + 1))
        for i, value in enumerate((mixed, mixed_up)):
            message[lines, 0, 2 * i * LANES : 2 * i * LANES + GROUP] = value
        message[lines, 0, 4 * LANES :] = tail
    low_t[...] = low_b.astype(F32).T[0 : 2 * RANK, :]
    for copy in copies:
        copy.wait()


def close(place, arrived, signs, valid, low_t, k_in, tok_in, out, total_out, k, tok, sems):
    tok_copy = pltpu.make_async_copy(tok_in, tok, sems.at[0])
    k_copy = pltpu.make_async_copy(k_in, k, sems.at[1])
    tok_copy.start()
    k_copy.start()
    core = place[0]
    sums = [jnp.sum(arrived[RANK * h : RANK * (h + 1)], axis=0) for h in range(2)]
    tails = [total[:, 4 * LANES :] for total in sums]
    line = lax.broadcasted_iota(jnp.int32, (8, GROUP), 0)
    pair_total = jnp.maximum(tails[0][:, 64:65] + tails[1][:, 64:65], 1.0)
    logs, cotangents, terms = 0.0, [], []
    for h in range(2):
        logit = DPO_BETA * tails[h]
        logs = logs + jnp.sum(
            valid[h] * (jnp.minimum(logit, 0.0) - jnp.log1p(jnp.exp(-jnp.abs(logit)))), axis=1, keepdims=True
        )
        scaled = -LOSS_SCALE * DPO_BETA * valid[h] * jax.nn.sigmoid(-logit) / pair_total
        scaled = jnp.broadcast_to(scaled, (8, LANES))
        cotangent = sum(dot(part, signs[h]) for part in split(scaled, 3))
        cotangents.append(cotangent[0:1, :])
        gate, up = (sums[h][:, i * LANES : i * LANES + GROUP] for i in (0, 2))
        projected = jnp.where(line == 0, gate, jnp.where(line == 1, up, 0.0)) * cotangent
        if h == 0:
            tok_copy.wait()
        terms.append(dot(projected.astype(BF16), tok[h * GROUP : (h + 1) * GROUP, 0:HALF]))
    grad_a = terms[0] + terms[1]
    own = jnp.where(core == 0, cotangents[0], cotangents[1])
    high, rest = split(low_t[...] * own, 2)
    k_copy.wait()
    gate = dot(high[0:RANK], k[0]) + dot(high[0:RANK], k[1]) + dot(rest[0:RANK], k[0])
    up = dot(high[RANK:], k[2]) + dot(high[RANK:], k[3]) + dot(rest[RANK:], k[2])
    out[0:RANK, 0, 0:UNITS] = gate
    out[RANK : 2 * RANK, 0, 0:UNITS] = up
    line = lax.broadcasted_iota(jnp.int32, (2 * RANK, SLICE), 0)
    for column in range(2):
        slices = jnp.zeros((2 * RANK, SLICE), F32)
        for i in range(RANK):
            here = jnp.broadcast_to(
                grad_a[column : column + 1, i * SLICE : (i + 1) * SLICE], (2 * RANK, SLICE)
            )
            slices = jnp.where(line == 2 * i + core, here, slices)
        out[:, 0, UNITS + column * SLICE : UNITS + (column + 1) * SLICE] = slices
    out[:, 0, UNITS + 2 * SLICE :] = jnp.broadcast_to(0.5 * logs, (2 * RANK, LANES))
    total_out[...] = jnp.broadcast_to(pair_total, (8, LANES))


def kernel(function, shapes, arguments, flops, grant, scratch=(), in_hbm=0, out_hbm=0):
    vmem = pl.BlockSpec(memory_space=pltpu.VMEM)
    smem = pl.BlockSpec(memory_space=pltpu.SMEM)
    hbm = pl.BlockSpec(memory_space=pltpu.HBM)
    return pl.pallas_call(
        function,
        out_shape=tuple(jax.ShapeDtypeStruct(*s) for s in shapes),
        in_specs=[smem] + [vmem] * (len(arguments) - 1 - in_hbm) + [hbm] * in_hbm,
        out_specs=(vmem,) * (len(shapes) - out_hbm) + (hbm,) * out_hbm,
        scratch_shapes=list(scratch),
        compiler_params=pltpu.CompilerParams(vmem_limit_bytes=grant * 1024 * 1024),
        cost_estimate=pl.CostEstimate(flops=flops, bytes_accessed=10_000_000, transcendentals=0),
    )(*arguments)


def along(value, axis, k):
    n = lax.axis_size(axis)
    return lax.ppermute(value, axis, [(i, (i + k) % n) for i in range(n)])


def fetch(value, axis, k):
    n = lax.axis_size(axis)
    return lax.ppermute(value, axis, [((i + k) % n, i) for i in range(n)])


def on_device(tokens, sequence_labels, response_mask, frozen, down, up, readout):
    yh, x, core, z, yl = (lax.axis_index(a) for a in AXES)
    place = jnp.stack([core, z, yh, x]).astype(jnp.int32)
    code = jnp.where(response_mask > 0, sequence_labels, SEQS)

    main = jnp.concatenate([frozen[0, :, :MAIN], frozen[1, :, :MAIN]], axis=1)
    w_main = lax.all_gather(main, ("yh", "x"), axis=0, tiled=True)

    by_core = tokens.reshape(ROWS, 16, 2, SLICE).transpose(2, 0, 1, 3).reshape(2, ROWS, HALF)
    code_lanes = jnp.pad(code.reshape(ROWS, 1).astype(BF16), ((0, 0), (0, LANES - 1)))
    keep = jnp.concatenate([jnp.where(core == 0, by_core[0], by_core[1]), code_lanes], axis=1)
    give = jnp.concatenate([jnp.where(core == 0, by_core[1], by_core[0]), code_lanes], axis=1)
    take = lax.ppermute(give, "c", SWAP)
    pair = jnp.where(
        core == 0, jnp.concatenate([keep, take], axis=0), jnp.concatenate([take, keep], axis=0)
    )
    four = swapped(pair, "yl", yl).reshape(4 * ROWS, HALF + LANES)
    has = [jnp.max((code == q).astype(F32)) for q in range(SEQS)]
    count_rows = jnp.broadcast_to((has[0] * has[1] + has[2] * has[3]).astype(BF16), (16, 2 * SIDE))
    piece = jnp.concatenate(
        [jnp.concatenate([frozen[0, :, MAIN:], frozen[1, :, MAIN:]], axis=1), count_rows], axis=0
    )
    pieces = [piece] + [fetch(piece, "yh", k) for k in (1, 2, 3)]
    four, *pieces = lax.optimization_barrier((four, *pieces))
    ring = [four, along(four, "z", 1), along(four, "z", -1)]
    stack = jnp.concatenate(pieces, axis=0)
    stacks = [stack] + [fetch(stack, "x", j) for j in (1, 2, 3)]
    for step in range(2):
        ring += [along(ring[-2], "z", 1), along(ring[-1], "z", -1)]
    ring.append(along(four, "z", 4))

    down_half = down.reshape(16, 2, SLICE, 2 * RANK)
    down_half = jnp.where(core == 0, down_half[:, 0], down_half[:, 1]).reshape(HALF, 2 * RANK)
    down_half = jnp.pad(down_half, ((0, 0), (0, LANES - 2 * RANK)))
    count_lanes, side, tok = kernel(
        early_products,
        [((1, LANES), F32), ((2 * GROUP, EXTRA), F32), ((2 * GROUP, HALF + LANES), BF16)],
        (place, down_half, *ring, *stacks),
        4 * GROUP * HALF * (2 * SIDE + LANES), 56,
        scratch=[
            pltpu.VMEM((2 * GROUP, HALF + LANES), BF16),
            pltpu.VMEM((HALF, 2 * SIDE), BF16),
            pltpu.VMEM((16, PIECE - SLICE, LANES), BF16),
            pltpu.VMEM((2 * GROUP, EXTRA), F32),
            pltpu.SemaphoreType.DMA((42,)),
        ],
        in_hbm=12, out_hbm=2,
    )
    b_gate = jnp.pad(up[:RANK], ((0, LANES - RANK), (0, 0)))
    b_up = jnp.pad(up[RANK:], ((RANK, LANES - 2 * RANK), (0, 0)))
    read = readout.reshape(1, UNITS)

    codes = tok[:, HALF].astype(jnp.int32).reshape(2, GROUP)
    pair_of = jnp.arange(LANES, dtype=jnp.int32)
    block_of = jnp.arange(GROUP, dtype=jnp.int32) // ROWS
    inside = (pair_of[:, None] // 2 == block_of[None, :])[None]
    chosen = inside & (codes[:, None, :] == 2 * (pair_of % 2)[None, :, None])
    rejected = inside & (codes[:, None, :] == 2 * (pair_of % 2)[None, :, None] + 1)
    signs = chosen.astype(BF16) - rejected.astype(BF16)
    valid = (jnp.any(chosen, axis=2) & jnp.any(rejected, axis=2)).astype(F32).reshape(2, 1, LANES)

    w_main, b_gate, b_up, read = lax.optimization_barrier((w_main, b_gate, b_up, read))
    far, near = products(place, tok, side, w_main)
    partner = lax.ppermute(far, "c", SWAP)
    message, low_t, k = kernel(
        score,
        [((2 * RANK, 1, 5 * LANES), F32), ((2 * RANK, GROUP), F32), ((4, GROUP, UNITS), BF16)],
        (place, near, partner, b_gate, b_up, read, signs, count_lanes),
        8 * GROUP * UNITS * LANES, 16,
        scratch=[pltpu.VMEM((4, GROUP, UNITS), BF16), pltpu.SemaphoreType.DMA((4,))],
        out_hbm=1,
    )
    arrived = lax.all_to_all(message, ("c", "z", "yl"), split_axis=0, concat_axis=0)
    outgoing, pair_total = kernel(
        close,
        [((2 * RANK, 1, UNITS + 2 * SLICE + LANES), F32), ((8, LANES), F32)],
        (place, arrived, signs, valid, low_t, k, tok),
        16 * GROUP * HALF * 2, 16,
        scratch=[
            pltpu.VMEM((4, GROUP, UNITS), BF16),
            pltpu.VMEM((2 * GROUP, HALF + LANES), BF16),
            pltpu.SemaphoreType.DMA((2,)),
        ],
        in_hbm=2,
    )

    summed = jnp.sum(lax.all_to_all(outgoing, DP, split_axis=0, concat_axis=0), axis=0)
    columns = summed[:, UNITS : UNITS + 2 * SLICE].reshape(1, 2, SLICE)
    grad_a = lax.all_to_all(
        jnp.broadcast_to(columns, (16, 2, SLICE)), BLK, split_axis=0, concat_axis=0
    )
    grad_a = grad_a.transpose(2, 1, 0).reshape(SLICE, 2 * RANK)
    return -summed[0, UNITS + 2 * SLICE] / pair_total[0, 0], grad_a, summed[:, :UNITS]


def solution(mesh):
    fine = Mesh(mesh.devices.reshape(SIZES), AXES)
    in_specs = (
        P(AXES, None),
        P(AXES, None),
        P(AXES, None),
        P(None, DP, BLK),
        P(),
        P(None, BLK),
        P(BLK),
    )
    out_specs = (P(), P(DP, None), P(DP, BLK))
    return jax.shard_map(
        on_device, mesh=fine, in_specs=in_specs, out_specs=out_specs, check_vma=False
    )
```

```python
import functools

import jax
import jax.numpy as jnp
from jax import lax
from jax.experimental import pallas as pl
from jax.experimental.pallas import tpu as pltpu
from jax.sharding import Mesh, PartitionSpec as P

SEQS = 4
ROWS = 12
RANK = 16
WIDTH = 4096
DPO_BETA = 0.1
LOSS_SCALE = 1024.0
F32 = jnp.float32
BF16 = jnp.bfloat16

AXES = ("yh", "x", "c", "z", "yl")
SIZES = (4, 4, 2, 8, 2)
DP = ("yh", "x", "c")
BLK = ("z", "yl")
SWAP = [(0, 1), (1, 0)]

SLICE = 128
HALF = WIDTH // 2
LANES = 128
UNITS = 896
MAIN = 640
SIDE = UNITS - MAIN
PIECE = SLICE + 16
COLUMNS = 512
GROUP = 192
BLOCKS = GROUP // ROWS
CONTRACT_LAST = (((1,), (1,)), ((), ()))


def swapped(value, axis, index):
    far = lax.ppermute(value, axis, SWAP)
    return jnp.where(index == 0, jnp.stack([value, far]), jnp.stack([far, value]))


def split(value, terms):
    parts = []
    for _ in range(terms):
        parts.append(value.astype(BF16))
        value = value - parts[-1].astype(F32)
    return parts


def dot(a, b, dims=(((1,), (0,)), ((), ()))):
    return lax.dot_general(a, b, dims, preferred_element_type=F32)


def early_products(place, down, p0, r1, l1, r2, l2, r3, l3, far_z, s0, s1, s3, s2_low, s2_high, far, near, count,
                   tok_out, tok, w, counts, sems):
    z, yh, x = place[1], place[2], place[3]
    block = 4 * ROWS
    moves = ((0, p0), (-1, r1), (1, l1), (-2, r2), (2, l2), (-3, r3), (3, l3), (4, far_z))
    copies = []
    for n, (k, ref) in enumerate(moves):
        rows = pl.ds(pl.multiple_of(lax.rem(z + 8 + k, 8) * block, block), block)
        copies.append(pltpu.make_async_copy(ref, tok.at[rows, :], sems.at[n]))
    parts = [(0, s0, range(4)), (1, s1, range(4)), (3, s3, range(4)), (2, s2_low, (0, 1)), (2, s2_high, (2, 3))]
    for j, ref, ks in parts:
        for k in ks:
            source = lax.rem(yh + k, 4) * 4 + lax.rem(x + j, 4)
            rows = pl.ds(pl.multiple_of(source * SLICE, SLICE), SLICE)
            at = 4 * j + k
            copies.append(pltpu.make_async_copy(ref.at[pl.ds((k - ks[0]) * PIECE, SLICE), :], w.at[rows, :], sems.at[8 + at]))
            spare = ref.at[pl.ds((k - ks[0]) * PIECE + SLICE, PIECE - SLICE), pl.ds(0, LANES)]
            copies.append(pltpu.make_async_copy(spare, counts.at[at], sems.at[25 + at]))
    for copy in copies:
        copy.start()
    for copy in copies:
        copy.wait()
    tok_copy = pltpu.make_async_copy(tok, tok_out, sems.at[24])
    tok_copy.start()
    total = jnp.sum(counts[...].astype(F32), axis=0)[0:1, :]
    count[...] = jnp.where(lax.broadcasted_iota(jnp.int32, (1, LANES), 1) == 64, total, 0.0)
    for half, out in ((1 - place[0], far), (place[0], near)):
        rows = pl.ds(pl.multiple_of(half * GROUP, GROUP), GROUP)
        for n in range(2):
            part = slice(n * SIDE, (n + 1) * SIDE)
            out[:, part] = dot(tok[rows, 0:HALF], w[:, part])
        out[:, 2 * SIDE :] = dot(tok[rows, 0:HALF], down[...])
    tok_copy.wait()


def main_products(place, tok, w_in, far, near, rows, w, sems):
    halves = [
        pl.ds(pl.multiple_of(half * GROUP, GROUP), GROUP) for half in (1 - place[0], place[0])
    ]
    chunks = [pl.ds(n * COLUMNS, COLUMNS) for n in range(HALF // COLUMNS)]
    row_copies = [
        pltpu.make_async_copy(tok.at[half, pl.ds(0, HALF)], rows.at[n], sems.at[n]) for n, half in enumerate(halves)
    ]
    copies = [
        pltpu.make_async_copy(w_in.at[chunk, :], w.at[chunk, :], sems.at[2 + n]) for n, chunk in enumerate(chunks)
    ]
    row_copies[0].start()
    copies[0].start()
    row_copies[1].start()
    for copy in copies[1:]:
        copy.start()
    for copy in row_copies:
        copy.wait()
    for n, (chunk, copy) in enumerate(zip(chunks, copies)):
        copy.wait()
        for at, out in enumerate((far, near)):
            term = dot(rows[at, :, chunk], w[chunk, :])
            out[...] = term if n == 0 else out[...] + term


def products(place, tok, w):
    return kernel(
        main_products,
        [((GROUP, 2 * MAIN), F32)] * 2,
        (place, tok, w),
        4 * GROUP * HALF * 2 * MAIN, 56,
        scratch=[
            pltpu.VMEM((2, GROUP, HALF), BF16),
            pltpu.VMEM((HALF, 2 * MAIN), BF16),
            pltpu.SemaphoreType.DMA((2 + HALF // COLUMNS,)),
        ],
        in_hbm=2,
    )


def score(place, near, partner, side, b_gate, b_up, readout, signs, count, message, low_t, k_out, k, sems):
    low_b = side[:, 2 * SIDE :].astype(BF16)
    main = near[...] + partner[...]
    gate_ref = jnp.concatenate([main[:, 0:MAIN], side[:, 0:SIDE]], axis=1)
    up_ref = jnp.concatenate([main[:, MAIN:], side[:, SIDE : 2 * SIDE]], axis=1)
    gate_pol = gate_ref + dot(low_b, b_gate[...])
    up_pol = up_ref + dot(low_b, b_up[...])
    sig_ref = jax.nn.sigmoid(gate_ref)
    sig_pol = jax.nn.sigmoid(gate_pol)
    act_pol = gate_pol * sig_pol
    read = readout[...].astype(F32)
    change = act_pol * up_pol - gate_ref * sig_ref * up_ref
    k_gate = read * sig_pol * (1.0 + gate_pol * (1.0 - sig_pol)) * up_pol
    k_up = read * act_pol
    read_b = jnp.broadcast_to(readout[...], (8, UNITS))
    change_row = sum(dot(read_b, part, CONTRACT_LAST) for part in split(change, 3))
    sign = signs[place[0]]
    gaps = sum(dot(part, sign, CONTRACT_LAST) for part in split(change_row, 3))
    tail = jnp.broadcast_to(gaps[0:1, :] + count[...], (RANK, LANES))
    high, rest = split(k_gate, 2)
    k[0], k[1] = high, rest
    copies = [pltpu.make_async_copy(k.at[i], k_out.at[i], sems.at[i]) for i in range(4)]
    copies[0].start()
    copies[1].start()
    mixed = dot(b_gate[0:RANK, :], high, CONTRACT_LAST) + dot(b_gate[0:RANK, :], rest, CONTRACT_LAST)
    high, rest = split(k_up, 2)
    k[2], k[3] = high, rest
    copies[2].start()
    copies[3].start()
    mixed_up = dot(b_up[RANK : 2 * RANK, :], high, CONTRACT_LAST) + dot(b_up[RANK : 2 * RANK, :], rest, CONTRACT_LAST)
    message[...] = jnp.zeros_like(message)
    for core in range(2):
        lines = slice(RANK * core, RANK * (core + 1))
        for i, value in enumerate((mixed, mixed_up)):
            message[lines, 0, 2 * i * LANES : 2 * i * LANES + GROUP] = value
        message[lines, 0, 4 * LANES :] = tail
    low_t[...] = low_b.astype(F32).T[0 : 2 * RANK, :]
    for copy in copies:
        copy.wait()


def close(place, arrived, signs, valid, low_t, k_in, tok_in, out, total_out, k, tok, sems):
    tok_copy = pltpu.make_async_copy(tok_in, tok, sems.at[0])
    k_copy = pltpu.make_async_copy(k_in, k, sems.at[1])
    tok_copy.start()
    k_copy.start()
    core = place[0]
    sums = [jnp.sum(arrived[RANK * h : RANK * (h + 1)], axis=0) for h in range(2)]
    tails = [total[:, 4 * LANES :] for total in sums]
    line = lax.broadcasted_iota(jnp.int32, (8, GROUP), 0)
    pair_total = jnp.maximum(tails[0][:, 64:65] + tails[1][:, 64:65], 1.0)
    logs, cotangents, terms = 0.0, [], []
    for h in range(2):
        logit = DPO_BETA * tails[h]
        logs = logs + jnp.sum(
            valid[h] * (jnp.minimum(logit, 0.0) - jnp.log1p(jnp.exp(-jnp.abs(logit)))), axis=1, keepdims=True
        )
        scaled = -LOSS_SCALE * DPO_BETA * valid[h] * jax.nn.sigmoid(-logit) / pair_total
        scaled = jnp.broadcast_to(scaled, (8, LANES))
        cotangent = sum(dot(part, signs[h]) for part in split(scaled, 3))
        cotangents.append(cotangent[0:1, :])
        gate, up = (sums[h][:, i * LANES : i * LANES + GROUP] for i in (0, 2))
        projected = jnp.where(line == 0, gate, jnp.where(line == 1, up, 0.0)) * cotangent
        if h == 0:
            tok_copy.wait()
        terms.append(dot(projected.astype(BF16), tok[h * GROUP : (h + 1) * GROUP, 0:HALF]))
    grad_a = terms[0] + terms[1]
    own = jnp.where(core == 0, cotangents[0], cotangents[1])
    high, rest = split(low_t[...] * own, 2)
    k_copy.wait()
    gate = dot(high[0:RANK], k[0]) + dot(high[0:RANK], k[1]) + dot(rest[0:RANK], k[0])
    up = dot(high[RANK:], k[2]) + dot(high[RANK:], k[3]) + dot(rest[RANK:], k[2])
    out[0:RANK, 0, 0:UNITS] = gate
    out[RANK : 2 * RANK, 0, 0:UNITS] = up
    line = lax.broadcasted_iota(jnp.int32, (2 * RANK, SLICE), 0)
    for column in range(2):
        slices = jnp.zeros((2 * RANK, SLICE), F32)
        for i in range(RANK):
            here = jnp.broadcast_to(
                grad_a[column : column + 1, i * SLICE : (i + 1) * SLICE], (2 * RANK, SLICE)
            )
            slices = jnp.where(line == 2 * i + core, here, slices)
        out[:, 0, UNITS + column * SLICE : UNITS + (column + 1) * SLICE] = slices
    out[:, 0, UNITS + 2 * SLICE :] = jnp.broadcast_to(0.5 * logs, (2 * RANK, LANES))
    total_out[...] = jnp.broadcast_to(pair_total, (8, LANES))


def kernel(function, shapes, arguments, flops, grant, scratch=(), in_hbm=0, out_hbm=0):
    vmem = pl.BlockSpec(memory_space=pltpu.VMEM)
    smem = pl.BlockSpec(memory_space=pltpu.SMEM)
    hbm = pl.BlockSpec(memory_space=pltpu.HBM)
    return pl.pallas_call(
        function,
        out_shape=tuple(jax.ShapeDtypeStruct(*s) for s in shapes),
        in_specs=[smem] + [vmem] * (len(arguments) - 1 - in_hbm) + [hbm] * in_hbm,
        out_specs=(vmem,) * (len(shapes) - out_hbm) + (hbm,) * out_hbm,
        scratch_shapes=list(scratch),
        compiler_params=pltpu.CompilerParams(vmem_limit_bytes=grant * 1024 * 1024),
        cost_estimate=pl.CostEstimate(flops=flops, bytes_accessed=10_000_000, transcendentals=0),
    )(*arguments)


def along(value, axis, k):
    n = lax.axis_size(axis)
    return lax.ppermute(value, axis, [(i, (i + k) % n) for i in range(n)])


def fetch(value, axis, k):
    n = lax.axis_size(axis)
    return lax.ppermute(value, axis, [((i + k) % n, i) for i in range(n)])


def on_device(tokens, sequence_labels, response_mask, frozen, down, up, readout):
    yh, x, core, z, yl = (lax.axis_index(a) for a in AXES)
    place = jnp.stack([core, z, yh, x]).astype(jnp.int32)
    code = jnp.where(response_mask > 0, sequence_labels, SEQS)

    main = jnp.concatenate([frozen[0, :, :MAIN], frozen[1, :, :MAIN]], axis=1)
    w_main = lax.all_gather(main, ("yh", "x"), axis=0, tiled=True)

    by_core = tokens.reshape(ROWS, 16, 2, SLICE).transpose(2, 0, 1, 3).reshape(2, ROWS, HALF)
    code_lanes = jnp.pad(code.reshape(ROWS, 1).astype(BF16), ((0, 0), (0, LANES - 1)))
    keep = jnp.concatenate([jnp.where(core == 0, by_core[0], by_core[1]), code_lanes], axis=1)
    give = jnp.concatenate([jnp.where(core == 0, by_core[1], by_core[0]), code_lanes], axis=1)
    take = lax.ppermute(give, "c", SWAP)
    pair = jnp.where(
        core == 0, jnp.concatenate([keep, take], axis=0), jnp.concatenate([take, keep], axis=0)
    )
    has = [jnp.max((code == q).astype(F32)) for q in range(SEQS)]
    count_rows = jnp.broadcast_to((has[0] * has[1] + has[2] * has[3]).astype(BF16), (16, 2 * SIDE))
    piece = jnp.concatenate(
        [jnp.concatenate([frozen[0, :, MAIN:], frozen[1, :, MAIN:]], axis=1), count_rows], axis=0
    )
    pieces = [piece] + [fetch(piece, "yh", k) for k in (1, 2, 3)]
    pair, *pieces = lax.optimization_barrier((pair, *pieces))
    four = swapped(pair, "yl", yl).reshape(4 * ROWS, HALF + LANES)
    ring = [four, along(four, "z", 1), along(four, "z", -1)]
    stack = jnp.concatenate(pieces, axis=0)
    next_x, last_x = fetch(stack, "x", 1), fetch(stack, "x", 3)
    stacks = [stack, next_x, last_x, fetch(last_x[: 2 * PIECE], "x", 3), fetch(next_x[2 * PIECE :], "x", 1)]
    for step in range(2):
        ring += [along(ring[-2], "z", 1), along(ring[-1], "z", -1)]
    ring.append(along(ring[-2], "z", 1))

    down_half = down.reshape(16, 2, SLICE, 2 * RANK)
    down_half = jnp.where(core == 0, down_half[:, 0], down_half[:, 1]).reshape(HALF, 2 * RANK)
    down_half = jnp.pad(down_half, ((0, 0), (0, LANES - 2 * RANK)))
    side_far, side, count_lanes, tok = kernel(
        early_products,
        [((GROUP, 2 * SIDE + LANES), F32)] * 2 + [((1, LANES), F32), ((2 * GROUP, HALF + LANES), BF16)],
        (place, down_half, *ring, *stacks),
        4 * GROUP * HALF * (2 * SIDE + LANES), 56,
        scratch=[
            pltpu.VMEM((2 * GROUP, HALF + LANES), BF16),
            pltpu.VMEM((HALF, 2 * SIDE), BF16),
            pltpu.VMEM((16, PIECE - SLICE, LANES), BF16),
            pltpu.SemaphoreType.DMA((41,)),
        ],
        in_hbm=13, out_hbm=1,
    )
    side = side + lax.ppermute(side_far, "c", SWAP)

    b_gate = jnp.pad(up[:RANK], ((0, LANES - RANK), (0, 0)))
    b_up = jnp.pad(up[RANK:], ((RANK, LANES - 2 * RANK), (0, 0)))
    read = readout.reshape(1, UNITS)

    codes = tok[:, HALF].astype(jnp.int32).reshape(2, GROUP)
    pair_of = jnp.arange(LANES, dtype=jnp.int32)
    block_of = jnp.arange(GROUP, dtype=jnp.int32) // ROWS
    inside = (pair_of[:, None] // 2 == block_of[None, :])[None]
    chosen = inside & (codes[:, None, :] == 2 * (pair_of % 2)[None, :, None])
    rejected = inside & (codes[:, None, :] == 2 * (pair_of % 2)[None, :, None] + 1)
    signs = chosen.astype(BF16) - rejected.astype(BF16)
    valid = (jnp.any(chosen, axis=2) & jnp.any(rejected, axis=2)).astype(F32).reshape(2, 1, LANES)

    w_main, side, b_gate, b_up, read, signs, valid, count_lanes = lax.optimization_barrier(
        (w_main, side, b_gate, b_up, read, signs, valid, count_lanes)
    )
    far, near = products(place, tok, w_main)
    partner = lax.ppermute(far, "c", SWAP)
    message, low_t, k = kernel(
        score,
        [((2 * RANK, 1, 5 * LANES), F32), ((2 * RANK, GROUP), F32), ((4, GROUP, UNITS), BF16)],
        (place, near, partner, side, b_gate, b_up, read, signs, count_lanes),
        8 * GROUP * UNITS * LANES, 16,
        scratch=[pltpu.VMEM((4, GROUP, UNITS), BF16), pltpu.SemaphoreType.DMA((4,))],
        out_hbm=1,
    )
    arrived = lax.all_to_all(message, ("c", "z", "yl"), split_axis=0, concat_axis=0)
    outgoing, pair_total = kernel(
        close,
        [((2 * RANK, 1, UNITS + 2 * SLICE + LANES), F32), ((8, LANES), F32)],
        (place, arrived, signs, valid, low_t, k, tok),
        16 * GROUP * HALF * 2, 16,
        scratch=[
            pltpu.VMEM((4, GROUP, UNITS), BF16),
            pltpu.VMEM((2 * GROUP, HALF + LANES), BF16),
            pltpu.SemaphoreType.DMA((2,)),
        ],
        in_hbm=2,
    )

    summed = jnp.sum(lax.all_to_all(outgoing, DP, split_axis=0, concat_axis=0), axis=0)
    columns = summed[:, UNITS : UNITS + 2 * SLICE].reshape(1, 2, SLICE)
    grad_a = lax.all_to_all(
        jnp.broadcast_to(columns, (16, 2, SLICE)), BLK, split_axis=0, concat_axis=0
    )
    grad_a = grad_a.transpose(2, 1, 0).reshape(SLICE, 2 * RANK)
    return -summed[0, UNITS + 2 * SLICE] / pair_total[0, 0], grad_a, summed[:, :UNITS]


def solution(mesh):
    fine = Mesh(mesh.devices.reshape(SIZES), AXES)
    in_specs = (
        P(AXES, None),
        P(AXES, None),
        P(AXES, None),
        P(None, DP, BLK),
        P(),
        P(None, BLK),
        P(BLK),
    )
    out_specs = (P(), P(DP, None), P(DP, BLK))
    return jax.shard_map(
        on_device, mesh=fine, in_specs=in_specs, out_specs=out_specs, check_vma=False
    )
```

```python
import functools

import jax
import jax.numpy as jnp
from jax import lax
from jax.experimental import pallas as pl
from jax.experimental.pallas import tpu as pltpu
from jax.sharding import Mesh, PartitionSpec as P

SEQS = 4
ROWS = 12
RANK = 16
WIDTH = 4096
DPO_BETA = 0.1
LOSS_SCALE = 1024.0
F32 = jnp.float32
BF16 = jnp.bfloat16

AXES = ("yh", "x", "c", "z", "yl")
SIZES = (4, 4, 2, 8, 2)
DP = ("yh", "x", "c")
BLK = ("z", "yl")
SWAP = [(0, 1), (1, 0)]

SLICE = 128
HALF = WIDTH // 2
LANES = 128
UNITS = 896
GATE, UP = 640, 512
MAIN = GATE + UP
SIDE = 2 * UNITS - MAIN
PIECE = SLICE + 16
COLUMNS = 512
GROUP = 192
BLOCKS = GROUP // ROWS
CONTRACT_LAST = (((1,), (1,)), ((), ()))


def swapped(value, axis, index):
    far = lax.ppermute(value, axis, SWAP)
    return jnp.where(index == 0, jnp.stack([value, far]), jnp.stack([far, value]))


def split(value, terms):
    parts = []
    for _ in range(terms):
        parts.append(value.astype(BF16))
        value = value - parts[-1].astype(F32)
    return parts


def dot(a, b, dims=(((1,), (0,)), ((), ()))):
    return lax.dot_general(a, b, dims, preferred_element_type=F32)


def early_products(place, down, p0, r1, l1, r2, l2, r3, l3, far_z, s0, s1, s3, s2_low, s2_high, far, near, count,
                   tok_out, tok, w, counts, sems):
    z, yh, x = place[1], place[2], place[3]
    block = 4 * ROWS
    moves = ((0, p0), (-1, r1), (1, l1), (-2, r2), (2, l2), (-3, r3), (3, l3), (4, far_z))
    copies = []
    for n, (k, ref) in enumerate(moves):
        rows = pl.ds(pl.multiple_of(lax.rem(z + 8 + k, 8) * block, block), block)
        copies.append(pltpu.make_async_copy(ref, tok.at[rows, :], sems.at[n]))
    parts = [(0, s0, range(4)), (1, s1, range(4)), (3, s3, range(4)), (2, s2_low, (0, 1)), (2, s2_high, (2, 3))]
    for j, ref, ks in parts:
        for k in ks:
            source = lax.rem(yh + k, 4) * 4 + lax.rem(x + j, 4)
            rows = pl.ds(pl.multiple_of(source * SLICE, SLICE), SLICE)
            at = 4 * j + k
            copies.append(pltpu.make_async_copy(ref.at[pl.ds((k - ks[0]) * PIECE, SLICE), :], w.at[rows, :], sems.at[8 + at]))
            spare = ref.at[pl.ds((k - ks[0]) * PIECE + SLICE, PIECE - SLICE), pl.ds(0, LANES)]
            copies.append(pltpu.make_async_copy(spare, counts.at[at], sems.at[25 + at]))
    for copy in copies:
        copy.start()
    for copy in copies[: len(moves)]:
        copy.wait()
    tok_copy = pltpu.make_async_copy(tok, tok_out, sems.at[24])
    tok_copy.start()
    halves = [
        (pl.ds(pl.multiple_of(half * GROUP, GROUP), GROUP), out) for half, out in ((1 - place[0], far), (place[0], near))
    ]
    for rows, out in halves:
        out[:, SIDE:] = dot(tok[rows, 0:HALF], down[...])
    for copy in copies[len(moves) :]:
        copy.wait()
    total = jnp.sum(counts[...].astype(F32), axis=0)[0:1, :]
    count[...] = jnp.where(lax.broadcasted_iota(jnp.int32, (1, LANES), 1) == 64, total, 0.0)
    for rows, out in halves:
        for part in (slice(0, UNITS - GATE), slice(UNITS - GATE, SIDE)):
            out[:, part] = dot(tok[rows, 0:HALF], w[:, part])
    tok_copy.wait()


def main_products(place, tok, w_in, far, near, rows, w, sems):
    halves = [
        pl.ds(pl.multiple_of(half * GROUP, GROUP), GROUP) for half in (1 - place[0], place[0])
    ]
    chunks = [pl.ds(n * COLUMNS, COLUMNS) for n in range(HALF // COLUMNS)]
    row_copies = [
        pltpu.make_async_copy(tok.at[half, pl.ds(0, HALF)], rows.at[n], sems.at[n]) for n, half in enumerate(halves)
    ]
    copies = [
        pltpu.make_async_copy(w_in.at[chunk, :], w.at[chunk, :], sems.at[2 + n]) for n, chunk in enumerate(chunks)
    ]
    row_copies[0].start()
    copies[0].start()
    row_copies[1].start()
    for copy in copies[1:]:
        copy.start()
    for copy in row_copies:
        copy.wait()
    for n, (chunk, copy) in enumerate(zip(chunks, copies)):
        copy.wait()
        for at, out in enumerate((far, near)):
            term = dot(rows[at, :, chunk], w[chunk, :])
            out[...] = term if n == 0 else out[...] + term


def products(place, tok, w):
    return kernel(
        main_products,
        [((GROUP, MAIN), F32)] * 2,
        (place, tok, w),
        4 * GROUP * HALF * MAIN, 56,
        scratch=[
            pltpu.VMEM((2, GROUP, HALF), BF16),
            pltpu.VMEM((HALF, MAIN), BF16),
            pltpu.SemaphoreType.DMA((2 + HALF // COLUMNS,)),
        ],
        in_hbm=2,
    )


def score(place, near, partner, side, b_gate, b_up, readout, signs, count, message, low_t, k_out, k, sems):
    low_b = side[:, SIDE:].astype(BF16)
    main = near[...] + partner[...]
    gate_ref = jnp.concatenate([main[:, 0:GATE], side[:, 0 : UNITS - GATE]], axis=1)
    up_ref = jnp.concatenate([main[:, GATE:], side[:, UNITS - GATE : SIDE]], axis=1)
    gate_pol = gate_ref + dot(low_b, b_gate[...])
    up_pol = up_ref + dot(low_b, b_up[...])
    sig_ref = jax.nn.sigmoid(gate_ref)
    sig_pol = jax.nn.sigmoid(gate_pol)
    act_pol = gate_pol * sig_pol
    read = readout[...].astype(F32)
    change = act_pol * up_pol - gate_ref * sig_ref * up_ref
    k_gate = read * sig_pol * (1.0 + gate_pol * (1.0 - sig_pol)) * up_pol
    k_up = read * act_pol
    read_b = jnp.broadcast_to(readout[...], (8, UNITS))
    change_row = sum(dot(read_b, part, CONTRACT_LAST) for part in split(change, 3))
    sign = signs[place[0]]
    gaps = sum(dot(part, sign, CONTRACT_LAST) for part in split(change_row, 3))
    tail = jnp.broadcast_to(gaps[0:1, :] + count[...], (RANK, LANES))
    high, rest = split(k_gate, 2)
    k[0], k[1] = high, rest
    copies = [pltpu.make_async_copy(k.at[i], k_out.at[i], sems.at[i]) for i in range(4)]
    copies[0].start()
    copies[1].start()
    mixed = dot(b_gate[0:RANK, :], high, CONTRACT_LAST) + dot(b_gate[0:RANK, :], rest, CONTRACT_LAST)
    high, rest = split(k_up, 2)
    k[2], k[3] = high, rest
    copies[2].start()
    copies[3].start()
    mixed_up = dot(b_up[RANK : 2 * RANK, :], high, CONTRACT_LAST) + dot(b_up[RANK : 2 * RANK, :], rest, CONTRACT_LAST)
    message[...] = jnp.zeros_like(message)
    for core in range(2):
        lines = slice(RANK * core, RANK * (core + 1))
        for i, value in enumerate((mixed, mixed_up)):
            message[lines, 0, 2 * i * LANES : 2 * i * LANES + GROUP] = value
        message[lines, 0, 4 * LANES :] = tail
    low_t[...] = low_b.astype(F32).T[0 : 2 * RANK, :]
    for copy in copies:
        copy.wait()


def close(place, arrived, signs, valid, low_t, k_in, tok_in, out, total_out, k, tok, sems):
    tok_copy = pltpu.make_async_copy(tok_in, tok, sems.at[0])
    k_copy = pltpu.make_async_copy(k_in, k, sems.at[1])
    tok_copy.start()
    k_copy.start()
    core = place[0]
    sums = [jnp.sum(arrived[RANK * h : RANK * (h + 1)], axis=0) for h in range(2)]
    tails = [total[:, 4 * LANES :] for total in sums]
    line = lax.broadcasted_iota(jnp.int32, (8, GROUP), 0)
    pair_total = jnp.maximum(tails[0][:, 64:65] + tails[1][:, 64:65], 1.0)
    logs, cotangents, terms = 0.0, [], []
    for h in range(2):
        logit = DPO_BETA * tails[h]
        logs = logs + jnp.sum(
            valid[h] * (jnp.minimum(logit, 0.0) - jnp.log1p(jnp.exp(-jnp.abs(logit)))), axis=1, keepdims=True
        )
        scaled = -LOSS_SCALE * DPO_BETA * valid[h] * jax.nn.sigmoid(-logit) / pair_total
        scaled = jnp.broadcast_to(scaled, (8, LANES))
        cotangent = sum(dot(part, signs[h]) for part in split(scaled, 3))
        cotangents.append(cotangent[0:1, :])
        gate, up = (sums[h][:, i * LANES : i * LANES + GROUP] for i in (0, 2))
        projected = jnp.where(line == 0, gate, jnp.where(line == 1, up, 0.0)) * cotangent
        if h == 0:
            tok_copy.wait()
        terms.append(dot(projected.astype(BF16), tok[h * GROUP : (h + 1) * GROUP, 0:HALF]))
    grad_a = terms[0] + terms[1]
    own = jnp.where(core == 0, cotangents[0], cotangents[1])
    high, rest = split(low_t[...] * own, 2)
    k_copy.wait()
    gate = dot(high[0:RANK], k[0]) + dot(high[0:RANK], k[1]) + dot(rest[0:RANK], k[0])
    up = dot(high[RANK:], k[2]) + dot(high[RANK:], k[3]) + dot(rest[RANK:], k[2])
    out[0:RANK, 0, 0:UNITS] = gate
    out[RANK : 2 * RANK, 0, 0:UNITS] = up
    line = lax.broadcasted_iota(jnp.int32, (2 * RANK, SLICE), 0)
    for column in range(2):
        slices = jnp.zeros((2 * RANK, SLICE), F32)
        for i in range(RANK):
            here = jnp.broadcast_to(
                grad_a[column : column + 1, i * SLICE : (i + 1) * SLICE], (2 * RANK, SLICE)
            )
            slices = jnp.where(line == 2 * i + core, here, slices)
        out[:, 0, UNITS + column * SLICE : UNITS + (column + 1) * SLICE] = slices
    out[:, 0, UNITS + 2 * SLICE :] = jnp.broadcast_to(0.5 * logs, (2 * RANK, LANES))
    total_out[...] = jnp.broadcast_to(pair_total, (8, LANES))


def kernel(function, shapes, arguments, flops, grant, scratch=(), in_hbm=0, out_hbm=0):
    vmem = pl.BlockSpec(memory_space=pltpu.VMEM)
    smem = pl.BlockSpec(memory_space=pltpu.SMEM)
    hbm = pl.BlockSpec(memory_space=pltpu.HBM)
    return pl.pallas_call(
        function,
        out_shape=tuple(jax.ShapeDtypeStruct(*s) for s in shapes),
        in_specs=[smem] + [vmem] * (len(arguments) - 1 - in_hbm) + [hbm] * in_hbm,
        out_specs=(vmem,) * (len(shapes) - out_hbm) + (hbm,) * out_hbm,
        scratch_shapes=list(scratch),
        compiler_params=pltpu.CompilerParams(vmem_limit_bytes=grant * 1024 * 1024),
        cost_estimate=pl.CostEstimate(flops=flops, bytes_accessed=10_000_000, transcendentals=0),
    )(*arguments)


def along(value, axis, k):
    n = lax.axis_size(axis)
    return lax.ppermute(value, axis, [(i, (i + k) % n) for i in range(n)])


def fetch(value, axis, k):
    n = lax.axis_size(axis)
    return lax.ppermute(value, axis, [((i + k) % n, i) for i in range(n)])


def on_device(tokens, sequence_labels, response_mask, frozen, down, up, readout):
    yh, x, core, z, yl = (lax.axis_index(a) for a in AXES)
    place = jnp.stack([core, z, yh, x]).astype(jnp.int32)
    code = jnp.where(response_mask > 0, sequence_labels, SEQS)

    main = jnp.concatenate([frozen[0, :, :GATE], frozen[1, :, :UP]], axis=1)
    w_main = lax.all_gather(main, ("yh", "x"), axis=0, tiled=True)

    by_core = tokens.reshape(ROWS, 16, 2, SLICE).transpose(2, 0, 1, 3).reshape(2, ROWS, HALF)
    code_lanes = jnp.pad(code.reshape(ROWS, 1).astype(BF16), ((0, 0), (0, LANES - 1)))
    keep = jnp.concatenate([jnp.where(core == 0, by_core[0], by_core[1]), code_lanes], axis=1)
    give = jnp.concatenate([jnp.where(core == 0, by_core[1], by_core[0]), code_lanes], axis=1)
    take = lax.ppermute(give, "c", SWAP)
    pair = jnp.where(
        core == 0, jnp.concatenate([keep, take], axis=0), jnp.concatenate([take, keep], axis=0)
    )
    has = [jnp.max((code == q).astype(F32)) for q in range(SEQS)]
    count_rows = jnp.broadcast_to((has[0] * has[1] + has[2] * has[3]).astype(BF16), (16, SIDE))
    piece = jnp.concatenate(
        [jnp.concatenate([frozen[0, :, GATE:], frozen[1, :, UP:]], axis=1), count_rows], axis=0
    )
    pieces = [piece] + [fetch(piece, "yh", k) for k in (1, 2, 3)]
    pair, *pieces = lax.optimization_barrier((pair, *pieces))
    four = swapped(pair, "yl", yl).reshape(4 * ROWS, HALF + LANES)
    ring = [four, along(four, "z", 1), along(four, "z", -1)]
    stack = jnp.concatenate(pieces, axis=0)
    next_x, last_x = fetch(stack, "x", 1), fetch(stack, "x", 3)
    stacks = [stack, next_x, last_x, fetch(last_x[: 2 * PIECE], "x", 3), fetch(next_x[2 * PIECE :], "x", 1)]
    for step in range(2):
        ring += [along(ring[-2], "z", 1), along(ring[-1], "z", -1)]
    ring.append(along(ring[-2], "z", 1))

    down_half = down.reshape(16, 2, SLICE, 2 * RANK)
    down_half = jnp.where(core == 0, down_half[:, 0], down_half[:, 1]).reshape(HALF, 2 * RANK)
    down_half = jnp.pad(down_half, ((0, 0), (0, LANES - 2 * RANK)))
    side_far, side, count_lanes, tok = kernel(
        early_products,
        [((GROUP, SIDE + LANES), F32)] * 2 + [((1, LANES), F32), ((2 * GROUP, HALF + LANES), BF16)],
        (place, down_half, *ring, *stacks),
        4 * GROUP * HALF * (SIDE + LANES), 56,
        scratch=[
            pltpu.VMEM((2 * GROUP, HALF + LANES), BF16),
            pltpu.VMEM((HALF, SIDE), BF16),
            pltpu.VMEM((16, PIECE - SLICE, LANES), BF16),
            pltpu.SemaphoreType.DMA((41,)),
        ],
        in_hbm=13, out_hbm=1,
    )
    side = side + lax.ppermute(side_far, "c", SWAP)

    b_gate = jnp.pad(up[:RANK], ((0, LANES - RANK), (0, 0)))
    b_up = jnp.pad(up[RANK:], ((RANK, LANES - 2 * RANK), (0, 0)))
    read = readout.reshape(1, UNITS)

    codes = tok[:, HALF].astype(jnp.int32).reshape(2, GROUP)
    pair_of = jnp.arange(LANES, dtype=jnp.int32)
    block_of = jnp.arange(GROUP, dtype=jnp.int32) // ROWS
    inside = (pair_of[:, None] // 2 == block_of[None, :])[None]
    chosen = inside & (codes[:, None, :] == 2 * (pair_of % 2)[None, :, None])
    rejected = inside & (codes[:, None, :] == 2 * (pair_of % 2)[None, :, None] + 1)
    signs = chosen.astype(BF16) - rejected.astype(BF16)
    valid = (jnp.any(chosen, axis=2) & jnp.any(rejected, axis=2)).astype(F32).reshape(2, 1, LANES)

    w_main, side, b_gate, b_up, read, signs, valid, count_lanes = lax.optimization_barrier(
        (w_main, side, b_gate, b_up, read, signs, valid, count_lanes)
    )
    far, near = products(place, tok, w_main)
    partner = lax.ppermute(far, "c", SWAP)
    message, low_t, k = kernel(
        score,
        [((2 * RANK, 1, 5 * LANES), F32), ((2 * RANK, GROUP), F32), ((4, GROUP, UNITS), BF16)],
        (place, near, partner, side, b_gate, b_up, read, signs, count_lanes),
        8 * GROUP * UNITS * LANES, 16,
        scratch=[pltpu.VMEM((4, GROUP, UNITS), BF16), pltpu.SemaphoreType.DMA((4,))],
        out_hbm=1,
    )
    arrived = lax.all_to_all(message, ("c", "z", "yl"), split_axis=0, concat_axis=0)
    outgoing, pair_total = kernel(
        close,
        [((2 * RANK, 1, UNITS + 2 * SLICE + LANES), F32), ((8, LANES), F32)],
        (place, arrived, signs, valid, low_t, k, tok),
        16 * GROUP * HALF * 2, 16,
        scratch=[
            pltpu.VMEM((4, GROUP, UNITS), BF16),
            pltpu.VMEM((2 * GROUP, HALF + LANES), BF16),
            pltpu.SemaphoreType.DMA((2,)),
        ],
        in_hbm=2,
    )

    summed = jnp.sum(lax.all_to_all(outgoing, DP, split_axis=0, concat_axis=0), axis=0)
    columns = summed[:, UNITS : UNITS + 2 * SLICE].reshape(1, 2, SLICE)
    grad_a = lax.all_to_all(
        jnp.broadcast_to(columns, (16, 2, SLICE)), BLK, split_axis=0, concat_axis=0
    )
    grad_a = grad_a.transpose(2, 1, 0).reshape(SLICE, 2 * RANK)
    return -summed[0, UNITS + 2 * SLICE] / pair_total[0, 0], grad_a, summed[:, :UNITS]


def solution(mesh):
    fine = Mesh(mesh.devices.reshape(SIZES), AXES)
    in_specs = (
        P(AXES, None),
        P(AXES, None),
        P(AXES, None),
        P(None, DP, BLK),
        P(),
        P(None, BLK),
        P(BLK),
    )
    out_specs = (P(), P(DP, None), P(DP, BLK))
    return jax.shard_map(
        on_device, mesh=fine, in_specs=in_specs, out_specs=out_specs, check_vma=False
    )
```

```python
import functools

import jax
import jax.numpy as jnp
from jax import lax
from jax.experimental import pallas as pl
from jax.experimental.pallas import tpu as pltpu
from jax.sharding import Mesh, PartitionSpec as P

SEQS = 4
ROWS = 12
RANK = 16
WIDTH = 4096
DPO_BETA = 0.1
LOSS_SCALE = 1024.0
F32 = jnp.float32
BF16 = jnp.bfloat16

AXES = ("yh", "x", "c", "z", "yl")
SIZES = (4, 4, 2, 8, 2)
DP = ("yh", "x", "c")
BLK = ("z", "yl")
SWAP = [(0, 1), (1, 0)]

SLICE = 128
HALF = WIDTH // 2
LANES = 128
UNITS = 896
GATE, UP = 768, 640
MAIN = GATE + UP
SIDE = 2 * UNITS - MAIN
PIECE = SLICE + 16
COLUMNS = 512
GROUP = 192
BLOCKS = GROUP // ROWS
CONTRACT_LAST = (((1,), (1,)), ((), ()))


def swapped(value, axis, index):
    far = lax.ppermute(value, axis, SWAP)
    return jnp.where(index == 0, jnp.stack([value, far]), jnp.stack([far, value]))


def split(value, terms):
    parts = []
    for _ in range(terms):
        parts.append(value.astype(BF16))
        value = value - parts[-1].astype(F32)
    return parts


def dot(a, b, dims=(((1,), (0,)), ((), ()))):
    return lax.dot_general(a, b, dims, preferred_element_type=F32)


def early_products(place, down, p0, r1, l1, r2, l2, r3, l3, far_z, s0, s1, s3, s2_low, s2_high, far, near, count,
                   tok_out, tok, w, counts, sems):
    z, yh, x = place[1], place[2], place[3]
    block = 4 * ROWS
    moves = ((0, p0), (-1, r1), (1, l1), (-2, r2), (2, l2), (-3, r3), (3, l3), (4, far_z))
    copies = []
    for n, (k, ref) in enumerate(moves):
        rows = pl.ds(pl.multiple_of(lax.rem(z + 8 + k, 8) * block, block), block)
        copies.append(pltpu.make_async_copy(ref, tok.at[rows, :], sems.at[n]))
    parts = [(0, s0, range(4)), (1, s1, range(4)), (3, s3, range(4)), (2, s2_low, (0, 1)), (2, s2_high, (2, 3))]
    for j, ref, ks in parts:
        for k in ks:
            source = lax.rem(yh + k, 4) * 4 + lax.rem(x + j, 4)
            rows = pl.ds(pl.multiple_of(source * SLICE, SLICE), SLICE)
            at = 4 * j + k
            copies.append(pltpu.make_async_copy(ref.at[pl.ds((k - ks[0]) * PIECE, SLICE), :], w.at[rows, :], sems.at[8 + at]))
            spare = ref.at[pl.ds((k - ks[0]) * PIECE + SLICE, PIECE - SLICE), pl.ds(0, LANES)]
            copies.append(pltpu.make_async_copy(spare, counts.at[at], sems.at[25 + at]))
    for copy in copies:
        copy.start()
    for copy in copies[: len(moves)]:
        copy.wait()
    tok_copy = pltpu.make_async_copy(tok, tok_out, sems.at[24])
    tok_copy.start()
    halves = [
        (pl.ds(pl.multiple_of(half * GROUP, GROUP), GROUP), out) for half, out in ((1 - place[0], far), (place[0], near))
    ]
    for rows, out in halves:
        out[:, SIDE:] = dot(tok[rows, 0:HALF], down[...])
    for copy in copies[len(moves) :]:
        copy.wait()
    total = jnp.sum(counts[...].astype(F32), axis=0)[0:1, :]
    count[...] = jnp.where(lax.broadcasted_iota(jnp.int32, (1, LANES), 1) == 64, total, 0.0)
    for rows, out in halves:
        for part in (slice(0, UNITS - GATE), slice(UNITS - GATE, SIDE)):
            out[:, part] = dot(tok[rows, 0:HALF], w[:, part])
    tok_copy.wait()


def main_products(place, tok, w_in, far, near, rows, w, sems):
    halves = [
        pl.ds(pl.multiple_of(half * GROUP, GROUP), GROUP) for half in (1 - place[0], place[0])
    ]
    chunks = [pl.ds(n * COLUMNS, COLUMNS) for n in range(HALF // COLUMNS)]
    row_copies = [
        pltpu.make_async_copy(tok.at[half, pl.ds(0, HALF)], rows.at[n], sems.at[n]) for n, half in enumerate(halves)
    ]
    copies = [
        pltpu.make_async_copy(w_in.at[chunk, :], w.at[chunk, :], sems.at[2 + n]) for n, chunk in enumerate(chunks)
    ]
    row_copies[0].start()
    copies[0].start()
    row_copies[1].start()
    for copy in copies[1:]:
        copy.start()
    for copy in row_copies:
        copy.wait()
    for n, (chunk, copy) in enumerate(zip(chunks, copies)):
        copy.wait()
        for at, out in enumerate((far, near)):
            term = dot(rows[at, :, chunk], w[chunk, :])
            out[...] = term if n == 0 else out[...] + term


def products(place, tok, w):
    return kernel(
        main_products,
        [((GROUP, MAIN), F32)] * 2,
        (place, tok, w),
        4 * GROUP * HALF * MAIN, 56,
        scratch=[
            pltpu.VMEM((2, GROUP, HALF), BF16),
            pltpu.VMEM((HALF, MAIN), BF16),
            pltpu.SemaphoreType.DMA((2 + HALF // COLUMNS,)),
        ],
        in_hbm=2,
    )


def score(place, near, partner, side, b_gate, b_up, readout, signs, count, message, low_t, k_out, k, sems):
    low_b = side[:, SIDE:].astype(BF16)
    main = near[...] + partner[...]
    gate_ref = jnp.concatenate([main[:, 0:GATE], side[:, 0 : UNITS - GATE]], axis=1)
    up_ref = jnp.concatenate([main[:, GATE:], side[:, UNITS - GATE : SIDE]], axis=1)
    gate_pol = gate_ref + dot(low_b, b_gate[...])
    up_pol = up_ref + dot(low_b, b_up[...])
    sig_ref = jax.nn.sigmoid(gate_ref)
    sig_pol = jax.nn.sigmoid(gate_pol)
    act_pol = gate_pol * sig_pol
    read = readout[...].astype(F32)
    change = act_pol * up_pol - gate_ref * sig_ref * up_ref
    k_gate = read * sig_pol * (1.0 + gate_pol * (1.0 - sig_pol)) * up_pol
    k_up = read * act_pol
    read_b = jnp.broadcast_to(readout[...], (8, UNITS))
    change_row = sum(dot(read_b, part, CONTRACT_LAST) for part in split(change, 3))
    sign = signs[place[0]]
    gaps = sum(dot(part, sign, CONTRACT_LAST) for part in split(change_row, 3))
    tail = jnp.broadcast_to(gaps[0:1, :] + count[...], (RANK, LANES))
    high, rest = split(k_gate, 2)
    k[0], k[1] = high, rest
    copies = [pltpu.make_async_copy(k.at[i], k_out.at[i], sems.at[i]) for i in range(4)]
    copies[0].start()
    copies[1].start()
    mixed = dot(b_gate[0:RANK, :], high, CONTRACT_LAST) + dot(b_gate[0:RANK, :], rest, CONTRACT_LAST)
    high, rest = split(k_up, 2)
    k[2], k[3] = high, rest
    copies[2].start()
    copies[3].start()
    mixed_up = dot(b_up[RANK : 2 * RANK, :], high, CONTRACT_LAST) + dot(b_up[RANK : 2 * RANK, :], rest, CONTRACT_LAST)
    message[...] = jnp.zeros_like(message)
    for core in range(2):
        lines = slice(RANK * core, RANK * (core + 1))
        for i, value in enumerate((mixed, mixed_up)):
            message[lines, 0, 2 * i * LANES : 2 * i * LANES + GROUP] = value
        message[lines, 0, 4 * LANES :] = tail
    low_t[...] = low_b.astype(F32).T[0 : 2 * RANK, :]
    for copy in copies:
        copy.wait()


def close(place, arrived, signs, valid, low_t, k_in, tok_in, out, total_out, k, tok, sems):
    tok_copy = pltpu.make_async_copy(tok_in, tok, sems.at[0])
    k_copy = pltpu.make_async_copy(k_in, k, sems.at[1])
    tok_copy.start()
    k_copy.start()
    core = place[0]
    sums = [jnp.sum(arrived[RANK * h : RANK * (h + 1)], axis=0) for h in range(2)]
    tails = [total[:, 4 * LANES :] for total in sums]
    line = lax.broadcasted_iota(jnp.int32, (8, GROUP), 0)
    pair_total = jnp.maximum(tails[0][:, 64:65] + tails[1][:, 64:65], 1.0)
    logs, cotangents, terms = 0.0, [], []
    for h in range(2):
        logit = DPO_BETA * tails[h]
        logs = logs + jnp.sum(
            valid[h] * (jnp.minimum(logit, 0.0) - jnp.log1p(jnp.exp(-jnp.abs(logit)))), axis=1, keepdims=True
        )
        scaled = -LOSS_SCALE * DPO_BETA * valid[h] * jax.nn.sigmoid(-logit) / pair_total
        scaled = jnp.broadcast_to(scaled, (8, LANES))
        cotangent = sum(dot(part, signs[h]) for part in split(scaled, 3))
        cotangents.append(cotangent[0:1, :])
        gate, up = (sums[h][:, i * LANES : i * LANES + GROUP] for i in (0, 2))
        projected = jnp.where(line == 0, gate, jnp.where(line == 1, up, 0.0)) * cotangent
        if h == 0:
            tok_copy.wait()
        terms.append(dot(projected.astype(BF16), tok[h * GROUP : (h + 1) * GROUP, 0:HALF]))
    grad_a = terms[0] + terms[1]
    own = jnp.where(core == 0, cotangents[0], cotangents[1])
    high, rest = split(low_t[...] * own, 2)
    k_copy.wait()
    gate = dot(high[0:RANK], k[0]) + dot(high[0:RANK], k[1]) + dot(rest[0:RANK], k[0])
    up = dot(high[RANK:], k[2]) + dot(high[RANK:], k[3]) + dot(rest[RANK:], k[2])
    out[0:RANK, 0, 0:UNITS] = gate
    out[RANK : 2 * RANK, 0, 0:UNITS] = up
    line = lax.broadcasted_iota(jnp.int32, (2 * RANK, SLICE), 0)
    for column in range(2):
        slices = jnp.zeros((2 * RANK, SLICE), F32)
        for i in range(RANK):
            here = jnp.broadcast_to(
                grad_a[column : column + 1, i * SLICE : (i + 1) * SLICE], (2 * RANK, SLICE)
            )
            slices = jnp.where(line == 2 * i + core, here, slices)
        out[:, 0, UNITS + column * SLICE : UNITS + (column + 1) * SLICE] = slices
    out[:, 0, UNITS + 2 * SLICE :] = jnp.broadcast_to(0.5 * logs, (2 * RANK, LANES))
    total_out[...] = jnp.broadcast_to(pair_total, (8, LANES))


def kernel(function, shapes, arguments, flops, grant, scratch=(), in_hbm=0, out_hbm=0):
    vmem = pl.BlockSpec(memory_space=pltpu.VMEM)
    smem = pl.BlockSpec(memory_space=pltpu.SMEM)
    hbm = pl.BlockSpec(memory_space=pltpu.HBM)
    return pl.pallas_call(
        function,
        out_shape=tuple(jax.ShapeDtypeStruct(*s) for s in shapes),
        in_specs=[smem] + [vmem] * (len(arguments) - 1 - in_hbm) + [hbm] * in_hbm,
        out_specs=(vmem,) * (len(shapes) - out_hbm) + (hbm,) * out_hbm,
        scratch_shapes=list(scratch),
        compiler_params=pltpu.CompilerParams(vmem_limit_bytes=grant * 1024 * 1024),
        cost_estimate=pl.CostEstimate(flops=flops, bytes_accessed=10_000_000, transcendentals=0),
    )(*arguments)


def along(value, axis, k):
    n = lax.axis_size(axis)
    return lax.ppermute(value, axis, [(i, (i + k) % n) for i in range(n)])


def fetch(value, axis, k):
    n = lax.axis_size(axis)
    return lax.ppermute(value, axis, [((i + k) % n, i) for i in range(n)])


def on_device(tokens, sequence_labels, response_mask, frozen, down, up, readout):
    yh, x, core, z, yl = (lax.axis_index(a) for a in AXES)
    place = jnp.stack([core, z, yh, x]).astype(jnp.int32)
    code = jnp.where(response_mask > 0, sequence_labels, SEQS)

    main = jnp.concatenate([frozen[0, :, :GATE], frozen[1, :, :UP]], axis=1)
    w_main = lax.all_gather(main, ("yh", "x"), axis=0, tiled=True)

    by_core = tokens.reshape(ROWS, 16, 2, SLICE).transpose(2, 0, 1, 3).reshape(2, ROWS, HALF)
    code_lanes = jnp.pad(code.reshape(ROWS, 1).astype(BF16), ((0, 0), (0, LANES - 1)))
    keep = jnp.concatenate([jnp.where(core == 0, by_core[0], by_core[1]), code_lanes], axis=1)
    give = jnp.concatenate([jnp.where(core == 0, by_core[1], by_core[0]), code_lanes], axis=1)
    take = lax.ppermute(give, "c", SWAP)
    pair = jnp.where(
        core == 0, jnp.concatenate([keep, take], axis=0), jnp.concatenate([take, keep], axis=0)
    )
    has = [jnp.max((code == q).astype(F32)) for q in range(SEQS)]
    count_rows = jnp.broadcast_to((has[0] * has[1] + has[2] * has[3]).astype(BF16), (16, SIDE))
    piece = jnp.concatenate(
        [jnp.concatenate([frozen[0, :, GATE:], frozen[1, :, UP:]], axis=1), count_rows], axis=0
    )
    pieces = [piece] + [fetch(piece, "yh", k) for k in (1, 2, 3)]
    pair, *pieces = lax.optimization_barrier((pair, *pieces))
    four = swapped(pair, "yl", yl).reshape(4 * ROWS, HALF + LANES)
    ring = [four, along(four, "z", 1), along(four, "z", -1)]
    stack = jnp.concatenate(pieces, axis=0)
    next_x, last_x = fetch(stack, "x", 1), fetch(stack, "x", 3)
    stacks = [stack, next_x, last_x, fetch(last_x[: 2 * PIECE], "x", 3), fetch(next_x[2 * PIECE :], "x", 1)]
    for step in range(2):
        ring += [along(ring[-2], "z", 1), along(ring[-1], "z", -1)]
    ring.append(along(ring[-2], "z", 1))

    down_half = down.reshape(16, 2, SLICE, 2 * RANK)
    down_half = jnp.where(core == 0, down_half[:, 0], down_half[:, 1]).reshape(HALF, 2 * RANK)
    down_half = jnp.pad(down_half, ((0, 0), (0, LANES - 2 * RANK)))
    side_far, side, count_lanes, tok = kernel(
        early_products,
        [((GROUP, SIDE + LANES), F32)] * 2 + [((1, LANES), F32), ((2 * GROUP, HALF + LANES), BF16)],
        (place, down_half, *ring, *stacks),
        4 * GROUP * HALF * (SIDE + LANES), 56,
        scratch=[
            pltpu.VMEM((2 * GROUP, HALF + LANES), BF16),
            pltpu.VMEM((HALF, SIDE), BF16),
            pltpu.VMEM((16, PIECE - SLICE, LANES), BF16),
            pltpu.SemaphoreType.DMA((41,)),
        ],
        in_hbm=13, out_hbm=1,
    )
    side = side + lax.ppermute(side_far, "c", SWAP)

    b_gate = jnp.pad(up[:RANK], ((0, LANES - RANK), (0, 0)))
    b_up = jnp.pad(up[RANK:], ((RANK, LANES - 2 * RANK), (0, 0)))
    read = readout.reshape(1, UNITS)

    codes = tok[:, HALF].astype(jnp.int32).reshape(2, GROUP)
    pair_of = jnp.arange(LANES, dtype=jnp.int32)
    block_of = jnp.arange(GROUP, dtype=jnp.int32) // ROWS
    inside = (pair_of[:, None] // 2 == block_of[None, :])[None]
    chosen = inside & (codes[:, None, :] == 2 * (pair_of % 2)[None, :, None])
    rejected = inside & (codes[:, None, :] == 2 * (pair_of % 2)[None, :, None] + 1)
    signs = chosen.astype(BF16) - rejected.astype(BF16)
    valid = (jnp.any(chosen, axis=2) & jnp.any(rejected, axis=2)).astype(F32).reshape(2, 1, LANES)

    w_main, side, b_gate, b_up, read, signs, valid, count_lanes = lax.optimization_barrier(
        (w_main, side, b_gate, b_up, read, signs, valid, count_lanes)
    )
    far, near = products(place, tok, w_main)
    partner = lax.ppermute(far, "c", SWAP)
    message, low_t, k = kernel(
        score,
        [((2 * RANK, 1, 5 * LANES), F32), ((2 * RANK, GROUP), F32), ((4, GROUP, UNITS), BF16)],
        (place, near, partner, side, b_gate, b_up, read, signs, count_lanes),
        8 * GROUP * UNITS * LANES, 16,
        scratch=[pltpu.VMEM((4, GROUP, UNITS), BF16), pltpu.SemaphoreType.DMA((4,))],
        out_hbm=1,
    )
    arrived = lax.all_to_all(message, ("c", "z", "yl"), split_axis=0, concat_axis=0)
    outgoing, pair_total = kernel(
        close,
        [((2 * RANK, 1, UNITS + 2 * SLICE + LANES), F32), ((8, LANES), F32)],
        (place, arrived, signs, valid, low_t, k, tok),
        16 * GROUP * HALF * 2, 16,
        scratch=[
            pltpu.VMEM((4, GROUP, UNITS), BF16),
            pltpu.VMEM((2 * GROUP, HALF + LANES), BF16),
            pltpu.SemaphoreType.DMA((2,)),
        ],
        in_hbm=2,
    )

    summed = jnp.sum(lax.all_to_all(outgoing, DP, split_axis=0, concat_axis=0), axis=0)
    columns = summed[:, UNITS : UNITS + 2 * SLICE].reshape(1, 2, SLICE)
    grad_a = lax.all_to_all(
        jnp.broadcast_to(columns, (16, 2, SLICE)), BLK, split_axis=0, concat_axis=0
    )
    grad_a = grad_a.transpose(2, 1, 0).reshape(SLICE, 2 * RANK)
    return -summed[0, UNITS + 2 * SLICE] / pair_total[0, 0], grad_a, summed[:, :UNITS]


def solution(mesh):
    fine = Mesh(mesh.devices.reshape(SIZES), AXES)
    in_specs = (
        P(AXES, None),
        P(AXES, None),
        P(AXES, None),
        P(None, DP, BLK),
        P(),
        P(None, BLK),
        P(BLK),
    )
    out_specs = (P(), P(DP, None), P(DP, BLK))
    return jax.shard_map(
        on_device, mesh=fine, in_specs=in_specs, out_specs=out_specs, check_vma=False
    )
```

```python
import functools

import jax
import jax.numpy as jnp
from jax import lax
from jax.experimental import pallas as pl
from jax.experimental.pallas import tpu as pltpu
from jax.sharding import Mesh, PartitionSpec as P

SEQS = 4
ROWS = 12
RANK = 16
WIDTH = 4096
DPO_BETA = 0.1
LOSS_SCALE = 1024.0
F32 = jnp.float32
BF16 = jnp.bfloat16

AXES = ("yh", "x", "c", "z", "yl")
SIZES = (4, 4, 2, 8, 2)
DP = ("yh", "x", "c")
BLK = ("z", "yl")
SWAP = [(0, 1), (1, 0)]

SLICE = 128
HALF = WIDTH // 2
LANES = 128
UNITS = 896
GATE, UP = 640, 640
MAIN = GATE + UP
SIDE = 2 * UNITS - MAIN
PIECE = SLICE + 16
COLUMNS = 512
GROUP = 192
BLOCKS = GROUP // ROWS
CONTRACT_LAST = (((1,), (1,)), ((), ()))


def swapped(value, axis, index):
    far = lax.ppermute(value, axis, SWAP)
    return jnp.where(index == 0, jnp.stack([value, far]), jnp.stack([far, value]))


def split(value, terms):
    parts = []
    for _ in range(terms):
        parts.append(value.astype(BF16))
        value = value - parts[-1].astype(F32)
    return parts


def dot(a, b, dims=(((1,), (0,)), ((), ()))):
    return lax.dot_general(a, b, dims, preferred_element_type=F32)


def early_products(place, down, p0, r1, l1, r2, l2, r3, l3, far_z, s0, s1, s3, s2_low, s2_high, far, near, count,
                   tok_out, tok, w, counts, sems):
    z, yh, x = place[1], place[2], place[3]
    block = 4 * ROWS
    moves = ((0, p0), (-1, r1), (1, l1), (-2, r2), (2, l2), (-3, r3), (3, l3), (4, far_z))
    copies = []
    for n, (k, ref) in enumerate(moves):
        rows = pl.ds(pl.multiple_of(lax.rem(z + 8 + k, 8) * block, block), block)
        copies.append(pltpu.make_async_copy(ref, tok.at[rows, :], sems.at[n]))
    parts = [(0, s0, range(4)), (1, s1, range(4)), (3, s3, range(4)), (2, s2_low, (0, 1)), (2, s2_high, (2, 3))]
    for j, ref, ks in parts:
        for k in ks:
            source = lax.rem(yh + k, 4) * 4 + lax.rem(x + j, 4)
            rows = pl.ds(pl.multiple_of(source * SLICE, SLICE), SLICE)
            at = 4 * j + k
            copies.append(pltpu.make_async_copy(ref.at[pl.ds((k - ks[0]) * PIECE, SLICE), :], w.at[rows, :], sems.at[8 + at]))
            spare = ref.at[pl.ds((k - ks[0]) * PIECE + SLICE, PIECE - SLICE), pl.ds(0, LANES)]
            copies.append(pltpu.make_async_copy(spare, counts.at[at], sems.at[25 + at]))
    for copy in copies:
        copy.start()
    for copy in copies[: len(moves)]:
        copy.wait()
    tok_copy = pltpu.make_async_copy(tok, tok_out, sems.at[24])
    tok_copy.start()
    halves = [
        (pl.ds(pl.multiple_of(half * GROUP, GROUP), GROUP), out) for half, out in ((1 - place[0], far), (place[0], near))
    ]
    for rows, out in halves:
        out[:, SIDE:] = dot(tok[rows, 0:HALF], down[...])
    for copy in copies[len(moves) :]:
        copy.wait()
    total = jnp.sum(counts[...].astype(F32), axis=0)[0:1, :]
    count[...] = jnp.where(lax.broadcasted_iota(jnp.int32, (1, LANES), 1) == 64, total, 0.0)
    for rows, out in halves:
        for part in (slice(0, UNITS - GATE), slice(UNITS - GATE, SIDE)):
            out[:, part] = dot(tok[rows, 0:HALF], w[:, part])
    tok_copy.wait()


def main_products(place, tok, w_in, far, near, rows, w, sems):
    halves = [
        pl.ds(pl.multiple_of(half * GROUP, GROUP), GROUP) for half in (1 - place[0], place[0])
    ]
    chunks = [pl.ds(n * COLUMNS, COLUMNS) for n in range(HALF // COLUMNS)]
    row_copies = [
        pltpu.make_async_copy(tok.at[half, pl.ds(0, HALF)], rows.at[n], sems.at[n]) for n, half in enumerate(halves)
    ]
    copies = [
        pltpu.make_async_copy(w_in.at[chunk, :], w.at[chunk, :], sems.at[2 + n]) for n, chunk in enumerate(chunks)
    ]
    row_copies[0].start()
    copies[0].start()
    row_copies[1].start()
    for copy in copies[1:]:
        copy.start()
    for copy in row_copies:
        copy.wait()
    for n, (chunk, copy) in enumerate(zip(chunks, copies)):
        copy.wait()
        for at, out in enumerate((far, near)):
            term = dot(rows[at, :, chunk], w[chunk, :])
            out[...] = term if n == 0 else out[...] + term


def products(place, tok, w):
    return kernel(
        main_products,
        [((GROUP, MAIN), F32)] * 2,
        (place, tok, w),
        4 * GROUP * HALF * MAIN, 56,
        scratch=[
            pltpu.VMEM((2, GROUP, HALF), BF16),
            pltpu.VMEM((HALF, MAIN), BF16),
            pltpu.SemaphoreType.DMA((2 + HALF // COLUMNS,)),
        ],
        in_hbm=2,
    )


def score(place, near, partner, side, b_gate, b_up, readout, signs, count, message, low_t, k_out, k, sems):
    low_b = side[:, SIDE:].astype(BF16)
    main = near[...] + partner[...]
    gate_ref = jnp.concatenate([main[:, 0:GATE], side[:, 0 : UNITS - GATE]], axis=1)
    up_ref = jnp.concatenate([main[:, GATE:], side[:, UNITS - GATE : SIDE]], axis=1)
    gate_pol = gate_ref + dot(low_b, b_gate[...])
    up_pol = up_ref + dot(low_b, b_up[...])
    sig_ref = jax.nn.sigmoid(gate_ref)
    sig_pol = jax.nn.sigmoid(gate_pol)
    act_pol = gate_pol * sig_pol
    read = readout[...].astype(F32)
    change = act_pol * up_pol - gate_ref * sig_ref * up_ref
    k_gate = read * sig_pol * (1.0 + gate_pol * (1.0 - sig_pol)) * up_pol
    k_up = read * act_pol
    read_b = jnp.broadcast_to(readout[...], (8, UNITS))
    change_row = sum(dot(read_b, part, CONTRACT_LAST) for part in split(change, 3))
    sign = signs[place[0]]
    gaps = sum(dot(part, sign, CONTRACT_LAST) for part in split(change_row, 3))
    tail = jnp.broadcast_to(gaps[0:1, :] + count[...], (RANK, LANES))
    high, rest = split(k_gate, 2)
    k[0], k[1] = high, rest
    copies = [pltpu.make_async_copy(k.at[i], k_out.at[i], sems.at[i]) for i in range(4)]
    copies[0].start()
    copies[1].start()
    mixed = dot(b_gate[0:RANK, :], high, CONTRACT_LAST) + dot(b_gate[0:RANK, :], rest, CONTRACT_LAST)
    high, rest = split(k_up, 2)
    k[2], k[3] = high, rest
    copies[2].start()
    copies[3].start()
    mixed_up = dot(b_up[RANK : 2 * RANK, :], high, CONTRACT_LAST) + dot(b_up[RANK : 2 * RANK, :], rest, CONTRACT_LAST)
    for core in range(2):
        lines = slice(RANK * core, RANK * (core + 1))
        for i, value in enumerate((mixed, mixed_up)):
            message[lines, 0, i * GROUP : (i + 1) * GROUP] = value
        message[lines, 0, 2 * GROUP :] = tail
    low_t[...] = low_b.astype(F32).T[0 : 2 * RANK, :]
    for copy in copies:
        copy.wait()


def close(place, arrived, signs, valid, low_t, k_in, tok_in, out, total_out, k, tok, sems):
    tok_copy = pltpu.make_async_copy(tok_in, tok, sems.at[0])
    k_copy = pltpu.make_async_copy(k_in, k, sems.at[1])
    tok_copy.start()
    k_copy.start()
    core = place[0]
    sums = [jnp.sum(arrived[RANK * h : RANK * (h + 1)], axis=0) for h in range(2)]
    tails = [total[:, 2 * GROUP :] for total in sums]
    line = lax.broadcasted_iota(jnp.int32, (8, GROUP), 0)
    pair_total = jnp.maximum(tails[0][:, 64:65] + tails[1][:, 64:65], 1.0)
    logs, cotangents, terms = 0.0, [], []
    for h in range(2):
        logit = DPO_BETA * tails[h]
        logs = logs + jnp.sum(
            valid[h] * (jnp.minimum(logit, 0.0) - jnp.log1p(jnp.exp(-jnp.abs(logit)))), axis=1, keepdims=True
        )
        scaled = -LOSS_SCALE * DPO_BETA * valid[h] * jax.nn.sigmoid(-logit) / pair_total
        scaled = jnp.broadcast_to(scaled, (8, LANES))
        cotangent = sum(dot(part, signs[h]) for part in split(scaled, 3))
        cotangents.append(cotangent[0:1, :])
        gate, up = (sums[h][:, i * GROUP : (i + 1) * GROUP] for i in range(2))
        projected = jnp.where(line == 0, gate, jnp.where(line == 1, up, 0.0)) * cotangent
        if h == 0:
            tok_copy.wait()
        terms.append(dot(projected.astype(BF16), tok[h * GROUP : (h + 1) * GROUP, 0:HALF]))
    grad_a = terms[0] + terms[1]
    own = jnp.where(core == 0, cotangents[0], cotangents[1])
    high, rest = split(low_t[...] * own, 2)
    k_copy.wait()
    gate = dot(high[0:RANK], k[0]) + dot(high[0:RANK], k[1]) + dot(rest[0:RANK], k[0])
    up = dot(high[RANK:], k[2]) + dot(high[RANK:], k[3]) + dot(rest[RANK:], k[2])
    out[0:RANK, 0, 0:UNITS] = gate
    out[RANK : 2 * RANK, 0, 0:UNITS] = up
    line = lax.broadcasted_iota(jnp.int32, (2 * RANK, SLICE), 0)
    for column in range(2):
        slices = jnp.zeros((2 * RANK, SLICE), F32)
        for i in range(RANK):
            here = jnp.broadcast_to(
                grad_a[column : column + 1, i * SLICE : (i + 1) * SLICE], (2 * RANK, SLICE)
            )
            slices = jnp.where(line == 2 * i + core, here, slices)
        out[:, 0, UNITS + column * SLICE : UNITS + (column + 1) * SLICE] = slices
    out[:, 0, UNITS + 2 * SLICE :] = jnp.broadcast_to(0.5 * logs, (2 * RANK, LANES))
    total_out[...] = jnp.broadcast_to(pair_total, (8, LANES))


def kernel(function, shapes, arguments, flops, grant, scratch=(), in_hbm=0, out_hbm=0):
    vmem = pl.BlockSpec(memory_space=pltpu.VMEM)
    smem = pl.BlockSpec(memory_space=pltpu.SMEM)
    hbm = pl.BlockSpec(memory_space=pltpu.HBM)
    return pl.pallas_call(
        function,
        out_shape=tuple(jax.ShapeDtypeStruct(*s) for s in shapes),
        in_specs=[smem] + [vmem] * (len(arguments) - 1 - in_hbm) + [hbm] * in_hbm,
        out_specs=(vmem,) * (len(shapes) - out_hbm) + (hbm,) * out_hbm,
        scratch_shapes=list(scratch),
        compiler_params=pltpu.CompilerParams(vmem_limit_bytes=grant * 1024 * 1024),
        cost_estimate=pl.CostEstimate(flops=flops, bytes_accessed=10_000_000, transcendentals=0),
    )(*arguments)


def along(value, axis, k):
    n = lax.axis_size(axis)
    return lax.ppermute(value, axis, [(i, (i + k) % n) for i in range(n)])


def fetch(value, axis, k):
    n = lax.axis_size(axis)
    return lax.ppermute(value, axis, [((i + k) % n, i) for i in range(n)])


def on_device(tokens, sequence_labels, response_mask, frozen, down, up, readout):
    yh, x, core, z, yl = (lax.axis_index(a) for a in AXES)
    place = jnp.stack([core, z, yh, x]).astype(jnp.int32)
    code = jnp.where(response_mask > 0, sequence_labels, SEQS)

    main = jnp.concatenate([frozen[0, :, :GATE], frozen[1, :, :UP]], axis=1)
    w_main = lax.all_gather(main, ("yh", "x"), axis=0, tiled=True)

    by_core = tokens.reshape(ROWS, 16, 2, SLICE).transpose(2, 0, 1, 3).reshape(2, ROWS, HALF)
    code_lanes = jnp.pad(code.reshape(ROWS, 1).astype(BF16), ((0, 0), (0, LANES - 1)))
    keep = jnp.concatenate([jnp.where(core == 0, by_core[0], by_core[1]), code_lanes], axis=1)
    give = jnp.concatenate([jnp.where(core == 0, by_core[1], by_core[0]), code_lanes], axis=1)
    take = lax.ppermute(give, "c", SWAP)
    pair = jnp.where(
        core == 0, jnp.concatenate([keep, take], axis=0), jnp.concatenate([take, keep], axis=0)
    )
    has = [jnp.max((code == q).astype(F32)) for q in range(SEQS)]
    count_rows = jnp.broadcast_to((has[0] * has[1] + has[2] * has[3]).astype(BF16), (16, SIDE))
    piece = jnp.concatenate(
        [jnp.concatenate([frozen[0, :, GATE:], frozen[1, :, UP:]], axis=1), count_rows], axis=0
    )
    pieces = [piece] + [fetch(piece, "yh", k) for k in (1, 2, 3)]
    pair, *pieces = lax.optimization_barrier((pair, *pieces))
    four = swapped(pair, "yl", yl).reshape(4 * ROWS, HALF + LANES)
    ring = [four, along(four, "z", 1), along(four, "z", -1)]
    stack = jnp.concatenate(pieces, axis=0)
    next_x, last_x = fetch(stack, "x", 1), fetch(stack, "x", 3)
    stacks = [stack, next_x, last_x, fetch(last_x[: 2 * PIECE], "x", 3), fetch(next_x[2 * PIECE :], "x", 1)]
    for step in range(2):
        ring += [along(ring[-2], "z", 1), along(ring[-1], "z", -1)]
    ring.append(along(ring[-2], "z", 1))

    down_half = down.reshape(16, 2, SLICE, 2 * RANK)
    down_half = jnp.where(core == 0, down_half[:, 0], down_half[:, 1]).reshape(HALF, 2 * RANK)
    down_half = jnp.pad(down_half, ((0, 0), (0, LANES - 2 * RANK)))
    side_far, side, count_lanes, tok = kernel(
        early_products,
        [((GROUP, SIDE + LANES), F32)] * 2 + [((1, LANES), F32), ((2 * GROUP, HALF + LANES), BF16)],
        (place, down_half, *ring, *stacks),
        4 * GROUP * HALF * (SIDE + LANES), 56,
        scratch=[
            pltpu.VMEM((2 * GROUP, HALF + LANES), BF16),
            pltpu.VMEM((HALF, SIDE), BF16),
            pltpu.VMEM((16, PIECE - SLICE, LANES), BF16),
            pltpu.SemaphoreType.DMA((41,)),
        ],
        in_hbm=13, out_hbm=1,
    )
    side = side + lax.ppermute(side_far, "c", SWAP)

    b_gate = jnp.pad(up[:RANK], ((0, LANES - RANK), (0, 0)))
    b_up = jnp.pad(up[RANK:], ((RANK, LANES - 2 * RANK), (0, 0)))
    read = readout.reshape(1, UNITS)

    codes = tok[:, HALF].astype(jnp.int32).reshape(2, GROUP)
    pair_of = jnp.arange(LANES, dtype=jnp.int32)
    block_of = jnp.arange(GROUP, dtype=jnp.int32) // ROWS
    inside = (pair_of[:, None] // 2 == block_of[None, :])[None]
    chosen = inside & (codes[:, None, :] == 2 * (pair_of % 2)[None, :, None])
    rejected = inside & (codes[:, None, :] == 2 * (pair_of % 2)[None, :, None] + 1)
    signs = chosen.astype(BF16) - rejected.astype(BF16)
    valid = (jnp.any(chosen, axis=2) & jnp.any(rejected, axis=2)).astype(F32).reshape(2, 1, LANES)

    w_main, side, b_gate, b_up, read, signs, valid, count_lanes = lax.optimization_barrier(
        (w_main, side, b_gate, b_up, read, signs, valid, count_lanes)
    )
    far, near = products(place, tok, w_main)
    partner = lax.ppermute(far, "c", SWAP)
    message, low_t, k = kernel(
        score,
        [((2 * RANK, 1, 2 * GROUP + LANES), F32), ((2 * RANK, GROUP), F32), ((4, GROUP, UNITS), BF16)],
        (place, near, partner, side, b_gate, b_up, read, signs, count_lanes),
        8 * GROUP * UNITS * LANES, 16,
        scratch=[pltpu.VMEM((4, GROUP, UNITS), BF16), pltpu.SemaphoreType.DMA((4,))],
        out_hbm=1,
    )
    arrived = lax.all_to_all(message, ("c", "z", "yl"), split_axis=0, concat_axis=0)
    outgoing, pair_total = kernel(
        close,
        [((2 * RANK, 1, UNITS + 2 * SLICE + LANES), F32), ((8, LANES), F32)],
        (place, arrived, signs, valid, low_t, k, tok),
        16 * GROUP * HALF * 2, 16,
        scratch=[
            pltpu.VMEM((4, GROUP, UNITS), BF16),
            pltpu.VMEM((2 * GROUP, HALF + LANES), BF16),
            pltpu.SemaphoreType.DMA((2,)),
        ],
        in_hbm=2,
    )

    summed = jnp.sum(lax.all_to_all(outgoing, DP, split_axis=0, concat_axis=0), axis=0)
    columns = summed[:, UNITS : UNITS + 2 * SLICE].reshape(1, 2, SLICE)
    grad_a = lax.all_to_all(
        jnp.broadcast_to(columns, (16, 2, SLICE)), BLK, split_axis=0, concat_axis=0
    )
    grad_a = grad_a.transpose(2, 1, 0).reshape(SLICE, 2 * RANK)
    return -summed[0, UNITS + 2 * SLICE] / pair_total[0, 0], grad_a, summed[:, :UNITS]


def solution(mesh):
    fine = Mesh(mesh.devices.reshape(SIZES), AXES)
    in_specs = (
        P(AXES, None),
        P(AXES, None),
        P(AXES, None),
        P(None, DP, BLK),
        P(),
        P(None, BLK),
        P(BLK),
    )
    out_specs = (P(), P(DP, None), P(DP, BLK))
    return jax.shard_map(
        on_device, mesh=fine, in_specs=in_specs, out_specs=out_specs, check_vma=False
    )
```

```python
import functools

import jax
import jax.numpy as jnp
from jax import lax
from jax.experimental import pallas as pl
from jax.experimental.pallas import tpu as pltpu
from jax.sharding import Mesh, PartitionSpec as P

SEQS = 4
ROWS = 12
RANK = 16
WIDTH = 4096
DPO_BETA = 0.1
LOSS_SCALE = 1024.0
F32 = jnp.float32
BF16 = jnp.bfloat16

AXES = ("yh", "x", "c", "z", "yl")
SIZES = (4, 4, 2, 8, 2)
DP = ("yh", "x", "c")
BLK = ("z", "yl")
SWAP = [(0, 1), (1, 0)]

SLICE = 128
HALF = WIDTH // 2
LANES = 128
UNITS = 896
GATE, UP = 640, 640
MAIN = GATE + UP
SIDE = 2 * UNITS - MAIN
PIECE = SLICE + 16
COLUMNS = 512
GROUP = 192
BLOCKS = GROUP // ROWS
CONTRACT_LAST = (((1,), (1,)), ((), ()))


def swapped(value, axis, index):
    far = lax.ppermute(value, axis, SWAP)
    return jnp.where(index == 0, jnp.stack([value, far]), jnp.stack([far, value]))


def split(value, terms):
    parts = []
    for _ in range(terms):
        parts.append(value.astype(BF16))
        value = value - parts[-1].astype(F32)
    return parts


def dot(a, b, dims=(((1,), (0,)), ((), ()))):
    return lax.dot_general(a, b, dims, preferred_element_type=F32)


def early_products(place, down, p0, r1, l1, r2, l2, r3, l3, far_z, s0, s1, s3, s2_low, s2_high, far, near, count,
                   tok_out, tok, w, counts, sems):
    z, yh, x = place[1], place[2], place[3]
    block = 4 * ROWS
    moves = ((0, p0), (-1, r1), (1, l1), (-2, r2), (2, l2), (-3, r3), (3, l3), (4, far_z))
    copies = []
    for n, (k, ref) in enumerate(moves):
        rows = pl.ds(pl.multiple_of(lax.rem(z + 8 + k, 8) * block, block), block)
        copies.append(pltpu.make_async_copy(ref, tok.at[rows, :], sems.at[n]))
    parts = [(0, s0, range(4)), (1, s1, range(4)), (3, s3, range(4)), (2, s2_low, (0, 1)), (2, s2_high, (2, 3))]
    for j, ref, ks in parts:
        for k in ks:
            source = lax.rem(yh + k, 4) * 4 + lax.rem(x + j, 4)
            rows = pl.ds(pl.multiple_of(source * SLICE, SLICE), SLICE)
            at = 4 * j + k
            copies.append(pltpu.make_async_copy(ref.at[pl.ds((k - ks[0]) * PIECE, SLICE), :], w.at[rows, :], sems.at[8 + at]))
            spare = ref.at[pl.ds((k - ks[0]) * PIECE + SLICE, PIECE - SLICE), pl.ds(0, LANES)]
            copies.append(pltpu.make_async_copy(spare, counts.at[at], sems.at[25 + at]))
    for copy in copies:
        copy.start()
    for copy in copies[: len(moves)]:
        copy.wait()
    tok_copy = pltpu.make_async_copy(tok, tok_out, sems.at[24])
    tok_copy.start()
    halves = [
        (pl.ds(pl.multiple_of(half * GROUP, GROUP), GROUP), out) for half, out in ((1 - place[0], far), (place[0], near))
    ]
    for rows, out in halves:
        out[:, SIDE:] = dot(tok[rows, 0:HALF], down[...])
    for copy in copies[len(moves) :]:
        copy.wait()
    total = jnp.sum(counts[...].astype(F32), axis=0)[0:1, :]
    count[...] = jnp.where(lax.broadcasted_iota(jnp.int32, (1, LANES), 1) == 64, total, 0.0)
    for rows, out in halves:
        for part in (slice(0, UNITS - GATE), slice(UNITS - GATE, SIDE)):
            out[:, part] = dot(tok[rows, 0:HALF], w[:, part])
    tok_copy.wait()


def main_products(place, tok, w_in, far, near, rows, w, sems):
    halves = [
        pl.ds(pl.multiple_of(half * GROUP, GROUP), GROUP) for half in (1 - place[0], place[0])
    ]
    chunks = [pl.ds(n * COLUMNS, COLUMNS) for n in range(HALF // COLUMNS)]
    row_copies = [
        pltpu.make_async_copy(tok.at[half, pl.ds(0, HALF)], rows.at[n], sems.at[n]) for n, half in enumerate(halves)
    ]
    copies = [
        [
            pltpu.make_async_copy(
                w_in.at[pl.ds((4 * x + yh) * SLICE, SLICE), :], w.at[pl.ds((4 * yh + x) * SLICE, SLICE), :],
                sems.at[2 + 4 * yh + x],
            )
            for x in range(4)
        ]
        for yh in range(4)
    ]
    row_copies[0].start()
    for copy in copies[0]:
        copy.start()
    row_copies[1].start()
    for copy in copies[1] + copies[2] + copies[3]:
        copy.start()
    for copy in row_copies:
        copy.wait()
    for n, (chunk, group) in enumerate(zip(chunks, copies)):
        for copy in group:
            copy.wait()
        for at, out in enumerate((far, near)):
            term = dot(rows[at, :, chunk], w[chunk, :])
            out[...] = term if n == 0 else out[...] + term


def products(place, tok, w):
    return kernel(
        main_products,
        [((GROUP, MAIN), F32)] * 2,
        (place, tok, w),
        4 * GROUP * HALF * MAIN, 56,
        scratch=[
            pltpu.VMEM((2, GROUP, HALF), BF16),
            pltpu.VMEM((HALF, MAIN), BF16),
            pltpu.SemaphoreType.DMA((18,)),
        ],
        in_hbm=2,
    )


def score(place, near, partner, side, b_gate, b_up, readout, signs, count, message, low_t, k_out, k, sems):
    low_b = side[:, SIDE:].astype(BF16)
    main = near[...] + partner[...]
    gate_ref = jnp.concatenate([main[:, 0:GATE], side[:, 0 : UNITS - GATE]], axis=1)
    up_ref = jnp.concatenate([main[:, GATE:], side[:, UNITS - GATE : SIDE]], axis=1)
    gate_pol = gate_ref + dot(low_b, b_gate[...])
    up_pol = up_ref + dot(low_b, b_up[...])
    sig_ref = jax.nn.sigmoid(gate_ref)
    sig_pol = jax.nn.sigmoid(gate_pol)
    act_pol = gate_pol * sig_pol
    read = readout[...].astype(F32)
    change = act_pol * up_pol - gate_ref * sig_ref * up_ref
    k_gate = read * sig_pol * (1.0 + gate_pol * (1.0 - sig_pol)) * up_pol
    k_up = read * act_pol
    read_b = jnp.broadcast_to(readout[...], (8, UNITS))
    change_row = sum(dot(read_b, part, CONTRACT_LAST) for part in split(change, 3))
    sign = signs[place[0]]
    gaps = sum(dot(part, sign, CONTRACT_LAST) for part in split(change_row, 3))
    tail = jnp.broadcast_to(gaps[0:1, :] + count[...], (RANK, LANES))
    high, rest = split(k_gate, 2)
    k[0], k[1] = high, rest
    copies = [pltpu.make_async_copy(k.at[i], k_out.at[i], sems.at[i]) for i in range(4)]
    copies[0].start()
    copies[1].start()
    mixed = dot(b_gate[0:RANK, :], high, CONTRACT_LAST) + dot(b_gate[0:RANK, :], rest, CONTRACT_LAST)
    high, rest = split(k_up, 2)
    k[2], k[3] = high, rest
    copies[2].start()
    copies[3].start()
    mixed_up = dot(b_up[RANK : 2 * RANK, :], high, CONTRACT_LAST) + dot(b_up[RANK : 2 * RANK, :], rest, CONTRACT_LAST)
    for core in range(2):
        lines = slice(RANK * core, RANK * (core + 1))
        for i, value in enumerate((mixed, mixed_up)):
            message[lines, 0, i * GROUP : (i + 1) * GROUP] = value
        message[lines, 0, 2 * GROUP :] = tail
    low_t[...] = low_b.astype(F32).T[0 : 2 * RANK, :]
    for copy in copies:
        copy.wait()


def close(place, arrived, signs, valid, low_t, k_in, tok_in, out, total_out, k, tok, sems):
    tok_copy = pltpu.make_async_copy(tok_in, tok, sems.at[0])
    k_copy = pltpu.make_async_copy(k_in, k, sems.at[1])
    tok_copy.start()
    k_copy.start()
    core = place[0]
    sums = [jnp.sum(arrived[RANK * h : RANK * (h + 1)], axis=0) for h in range(2)]
    tails = [total[:, 2 * GROUP :] for total in sums]
    line = lax.broadcasted_iota(jnp.int32, (8, GROUP), 0)
    pair_total = jnp.maximum(tails[0][:, 64:65] + tails[1][:, 64:65], 1.0)
    logs, cotangents, terms = 0.0, [], []
    for h in range(2):
        logit = DPO_BETA * tails[h]
        logs = logs + jnp.sum(
            valid[h] * (jnp.minimum(logit, 0.0) - jnp.log1p(jnp.exp(-jnp.abs(logit)))), axis=1, keepdims=True
        )
        scaled = -LOSS_SCALE * DPO_BETA * valid[h] * jax.nn.sigmoid(-logit) / pair_total
        scaled = jnp.broadcast_to(scaled, (8, LANES))
        cotangent = sum(dot(part, signs[h]) for part in split(scaled, 3))
        cotangents.append(cotangent[0:1, :])
        gate, up = (sums[h][:, i * GROUP : (i + 1) * GROUP] for i in range(2))
        projected = jnp.where(line == 0, gate, jnp.where(line == 1, up, 0.0)) * cotangent
        if h == 0:
            tok_copy.wait()
        terms.append(dot(projected.astype(BF16), tok[h * GROUP : (h + 1) * GROUP, 0:HALF]))
    grad_a = terms[0] + terms[1]
    own = jnp.where(core == 0, cotangents[0], cotangents[1])
    high, rest = split(low_t[...] * own, 2)
    k_copy.wait()
    gate = dot(high[0:RANK], k[0]) + dot(high[0:RANK], k[1]) + dot(rest[0:RANK], k[0])
    up = dot(high[RANK:], k[2]) + dot(high[RANK:], k[3]) + dot(rest[RANK:], k[2])
    out[0:RANK, 0, 0:UNITS] = gate
    out[RANK : 2 * RANK, 0, 0:UNITS] = up
    line = lax.broadcasted_iota(jnp.int32, (2 * RANK, SLICE), 0)
    for column in range(2):
        slices = jnp.zeros((2 * RANK, SLICE), F32)
        for i in range(RANK):
            here = jnp.broadcast_to(
                grad_a[column : column + 1, i * SLICE : (i + 1) * SLICE], (2 * RANK, SLICE)
            )
            slices = jnp.where(line == 2 * i + core, here, slices)
        out[:, 0, UNITS + column * SLICE : UNITS + (column + 1) * SLICE] = slices
    out[:, 0, UNITS + 2 * SLICE :] = jnp.broadcast_to(0.5 * logs, (2 * RANK, LANES))
    total_out[...] = jnp.broadcast_to(pair_total, (8, LANES))


def kernel(function, shapes, arguments, flops, grant, scratch=(), in_hbm=0, out_hbm=0):
    vmem = pl.BlockSpec(memory_space=pltpu.VMEM)
    smem = pl.BlockSpec(memory_space=pltpu.SMEM)
    hbm = pl.BlockSpec(memory_space=pltpu.HBM)
    return pl.pallas_call(
        function,
        out_shape=tuple(jax.ShapeDtypeStruct(*s) for s in shapes),
        in_specs=[smem] + [vmem] * (len(arguments) - 1 - in_hbm) + [hbm] * in_hbm,
        out_specs=(vmem,) * (len(shapes) - out_hbm) + (hbm,) * out_hbm,
        scratch_shapes=list(scratch),
        compiler_params=pltpu.CompilerParams(vmem_limit_bytes=grant * 1024 * 1024),
        cost_estimate=pl.CostEstimate(flops=flops, bytes_accessed=10_000_000, transcendentals=0),
    )(*arguments)


def along(value, axis, k):
    n = lax.axis_size(axis)
    return lax.ppermute(value, axis, [(i, (i + k) % n) for i in range(n)])


def fetch(value, axis, k):
    n = lax.axis_size(axis)
    return lax.ppermute(value, axis, [((i + k) % n, i) for i in range(n)])


def on_device(tokens, sequence_labels, response_mask, frozen, down, up, readout):
    yh, x, core, z, yl = (lax.axis_index(a) for a in AXES)
    place = jnp.stack([core, z, yh, x]).astype(jnp.int32)
    code = jnp.where(response_mask > 0, sequence_labels, SEQS)

    main = jnp.concatenate([frozen[0, :, :GATE], frozen[1, :, :UP]], axis=1)
    w_main = lax.all_gather(main, ("x", "yh"), axis=0, tiled=True)

    by_core = tokens.reshape(ROWS, 16, 2, SLICE).transpose(2, 0, 1, 3).reshape(2, ROWS, HALF)
    code_lanes = jnp.pad(code.reshape(ROWS, 1).astype(BF16), ((0, 0), (0, LANES - 1)))
    keep = jnp.concatenate([jnp.where(core == 0, by_core[0], by_core[1]), code_lanes], axis=1)
    give = jnp.concatenate([jnp.where(core == 0, by_core[1], by_core[0]), code_lanes], axis=1)
    take = lax.ppermute(give, "c", SWAP)
    pair = jnp.where(
        core == 0, jnp.concatenate([keep, take], axis=0), jnp.concatenate([take, keep], axis=0)
    )
    has = [jnp.max((code == q).astype(F32)) for q in range(SEQS)]
    count_rows = jnp.broadcast_to((has[0] * has[1] + has[2] * has[3]).astype(BF16), (16, SIDE))
    piece = jnp.concatenate(
        [jnp.concatenate([frozen[0, :, GATE:], frozen[1, :, UP:]], axis=1), count_rows], axis=0
    )
    pieces = [piece] + [fetch(piece, "yh", k) for k in (1, 2, 3)]
    pair, *pieces = lax.optimization_barrier((pair, *pieces))
    four = swapped(pair, "yl", yl).reshape(4 * ROWS, HALF + LANES)
    ring = [four, along(four, "z", 1), along(four, "z", -1)]
    stack = jnp.concatenate(pieces, axis=0)
    next_x, last_x = fetch(stack, "x", 1), fetch(stack, "x", 3)
    stacks = [stack, next_x, last_x, fetch(last_x[: 2 * PIECE], "x", 3), fetch(next_x[2 * PIECE :], "x", 1)]
    for step in range(2):
        ring += [along(ring[-2], "z", 1), along(ring[-1], "z", -1)]
    ring.append(along(ring[-2], "z", 1))

    down_half = down.reshape(16, 2, SLICE, 2 * RANK)
    down_half = jnp.where(core == 0, down_half[:, 0], down_half[:, 1]).reshape(HALF, 2 * RANK)
    down_half = jnp.pad(down_half, ((0, 0), (0, LANES - 2 * RANK)))
    side_far, side, count_lanes, tok = kernel(
        early_products,
        [((GROUP, SIDE + LANES), F32)] * 2 + [((1, LANES), F32), ((2 * GROUP, HALF + LANES), BF16)],
        (place, down_half, *ring, *stacks),
        4 * GROUP * HALF * (SIDE + LANES), 56,
        scratch=[
            pltpu.VMEM((2 * GROUP, HALF + LANES), BF16),
            pltpu.VMEM((HALF, SIDE), BF16),
            pltpu.VMEM((16, PIECE - SLICE, LANES), BF16),
            pltpu.SemaphoreType.DMA((41,)),
        ],
        in_hbm=13, out_hbm=1,
    )
    side = side + lax.ppermute(side_far, "c", SWAP)

    b_gate = jnp.pad(up[:RANK], ((0, LANES - RANK), (0, 0)))
    b_up = jnp.pad(up[RANK:], ((RANK, LANES - 2 * RANK), (0, 0)))
    read = readout.reshape(1, UNITS)

    codes = tok[:, HALF].astype(jnp.int32).reshape(2, GROUP)
    pair_of = jnp.arange(LANES, dtype=jnp.int32)
    block_of = jnp.arange(GROUP, dtype=jnp.int32) // ROWS
    inside = (pair_of[:, None] // 2 == block_of[None, :])[None]
    chosen = inside & (codes[:, None, :] == 2 * (pair_of % 2)[None, :, None])
    rejected = inside & (codes[:, None, :] == 2 * (pair_of % 2)[None, :, None] + 1)
    signs = chosen.astype(BF16) - rejected.astype(BF16)
    valid = (jnp.any(chosen, axis=2) & jnp.any(rejected, axis=2)).astype(F32).reshape(2, 1, LANES)

    w_main, side, b_gate, b_up, read, signs, valid, count_lanes = lax.optimization_barrier(
        (w_main, side, b_gate, b_up, read, signs, valid, count_lanes)
    )
    far, near = products(place, tok, w_main)
    partner = lax.ppermute(far, "c", SWAP)
    message, low_t, k = kernel(
        score,
        [((2 * RANK, 1, 2 * GROUP + LANES), F32), ((2 * RANK, GROUP), F32), ((4, GROUP, UNITS), BF16)],
        (place, near, partner, side, b_gate, b_up, read, signs, count_lanes),
        8 * GROUP * UNITS * LANES, 16,
        scratch=[pltpu.VMEM((4, GROUP, UNITS), BF16), pltpu.SemaphoreType.DMA((4,))],
        out_hbm=1,
    )
    arrived = lax.all_to_all(message, ("c", "z", "yl"), split_axis=0, concat_axis=0)
    outgoing, pair_total = kernel(
        close,
        [((2 * RANK, 1, UNITS + 2 * SLICE + LANES), F32), ((8, LANES), F32)],
        (place, arrived, signs, valid, low_t, k, tok),
        16 * GROUP * HALF * 2, 16,
        scratch=[
            pltpu.VMEM((4, GROUP, UNITS), BF16),
            pltpu.VMEM((2 * GROUP, HALF + LANES), BF16),
            pltpu.SemaphoreType.DMA((2,)),
        ],
        in_hbm=2,
    )

    summed = jnp.sum(lax.all_to_all(outgoing, DP, split_axis=0, concat_axis=0), axis=0)
    columns = summed[:, UNITS : UNITS + 2 * SLICE].reshape(1, 2, SLICE)
    grad_a = lax.all_to_all(
        jnp.broadcast_to(columns, (16, 2, SLICE)), BLK, split_axis=0, concat_axis=0
    )
    grad_a = grad_a.transpose(2, 1, 0).reshape(SLICE, 2 * RANK)
    return -summed[0, UNITS + 2 * SLICE] / pair_total[0, 0], grad_a, summed[:, :UNITS]


def solution(mesh):
    fine = Mesh(mesh.devices.reshape(SIZES), AXES)
    in_specs = (
        P(AXES, None),
        P(AXES, None),
        P(AXES, None),
        P(None, DP, BLK),
        P(),
        P(None, BLK),
        P(BLK),
    )
    out_specs = (P(), P(DP, None), P(DP, BLK))
    return jax.shard_map(
        on_device, mesh=fine, in_specs=in_specs, out_specs=out_specs, check_vma=False
    )
```

```python
import functools

import jax
import jax.numpy as jnp
from jax import lax
from jax.experimental import pallas as pl
from jax.experimental.pallas import tpu as pltpu
from jax.sharding import Mesh, PartitionSpec as P

SEQS = 4
ROWS = 12
RANK = 16
WIDTH = 4096
DPO_BETA = 0.1
LOSS_SCALE = 1024.0
F32 = jnp.float32
BF16 = jnp.bfloat16

AXES = ("yh", "x", "c", "z", "yl")
SIZES = (4, 4, 2, 8, 2)
DP = ("yh", "x", "c")
BLK = ("z", "yl")
SWAP = [(0, 1), (1, 0)]

SLICE = 128
HALF = WIDTH // 2
LANES = 128
UNITS = 896
GATE, UP = 640, 640
MAIN = GATE + UP
SIDE = 2 * UNITS - MAIN
PIECE = SLICE + 16
COLUMNS = 512
GROUP = 192
BLOCKS = GROUP // ROWS
CONTRACT_LAST = (((1,), (1,)), ((), ()))


def swapped(value, axis, index):
    far = lax.ppermute(value, axis, SWAP)
    return jnp.where(index == 0, jnp.stack([value, far]), jnp.stack([far, value]))


def split(value, terms):
    parts = []
    for _ in range(terms):
        parts.append(value.astype(BF16))
        value = value - parts[-1].astype(F32)
    return parts


def dot(a, b, dims=(((1,), (0,)), ((), ()))):
    return lax.dot_general(a, b, dims, preferred_element_type=F32)


def early_products(place, down, p0, r1, l1, r2, l2, r3, l3, far_z, s0, s1, s3, s2_low, s2_high, far, near, count,
                   tok_out, tok, w, counts, sems):
    z, yh, x = place[1], place[2], place[3]
    block = 4 * ROWS
    moves = ((0, p0), (-1, r1), (1, l1), (-2, r2), (2, l2), (-3, r3), (3, l3), (4, far_z))
    copies = []
    for n, (k, ref) in enumerate(moves):
        rows = pl.ds(pl.multiple_of(lax.rem(z + 8 + k, 8) * block, block), block)
        copies.append(pltpu.make_async_copy(ref, tok.at[rows, :], sems.at[n]))
    parts = [(0, s0, range(4)), (1, s1, range(4)), (3, s3, range(4)), (2, s2_low, (0, 1)), (2, s2_high, (2, 3))]
    for j, ref, ks in parts:
        for k in ks:
            source = lax.rem(yh + k, 4) * 4 + lax.rem(x + j, 4)
            rows = pl.ds(pl.multiple_of(source * SLICE, SLICE), SLICE)
            at = 4 * j + k
            copies.append(pltpu.make_async_copy(ref.at[pl.ds((k - ks[0]) * PIECE, SLICE), :], w.at[rows, :], sems.at[8 + at]))
            spare = ref.at[pl.ds((k - ks[0]) * PIECE + SLICE, PIECE - SLICE), pl.ds(0, LANES)]
            copies.append(pltpu.make_async_copy(spare, counts.at[at], sems.at[25 + at]))
    for copy in copies:
        copy.start()
    for copy in copies[: len(moves)]:
        copy.wait()
    tok_copy = pltpu.make_async_copy(tok, tok_out, sems.at[24])
    tok_copy.start()
    halves = [
        (pl.ds(pl.multiple_of(half * GROUP, GROUP), GROUP), out) for half, out in ((1 - place[0], far), (place[0], near))
    ]
    for rows, out in halves:
        out[:, SIDE:] = dot(tok[rows, 0:HALF], down[...])
    for copy in copies[len(moves) :]:
        copy.wait()
    total = jnp.sum(counts[...].astype(F32), axis=0)[0:1, :]
    count[...] = jnp.where(lax.broadcasted_iota(jnp.int32, (1, LANES), 1) == 64, total, 0.0)
    for rows, out in halves:
        for part in (slice(0, UNITS - GATE), slice(UNITS - GATE, SIDE)):
            out[:, part] = dot(tok[rows, 0:HALF], w[:, part])
    tok_copy.wait()


def main_products(place, tok, w_in, far, near, rows, w, sems):
    halves = [
        pl.ds(pl.multiple_of(half * GROUP, GROUP), GROUP) for half in (1 - place[0], place[0])
    ]
    chunks = [pl.ds(n * COLUMNS, COLUMNS) for n in range(HALF // COLUMNS)]
    row_copies = [
        pltpu.make_async_copy(tok.at[half, pl.ds(0, HALF)], rows.at[n], sems.at[n]) for n, half in enumerate(halves)
    ]
    copies = [
        pltpu.make_async_copy(w_in.at[chunk, :], w.at[chunk, :], sems.at[2 + n]) for n, chunk in enumerate(chunks)
    ]
    row_copies[0].start()
    copies[0].start()
    row_copies[1].start()
    for copy in copies[1:]:
        copy.start()
    for copy in row_copies:
        copy.wait()
    for n, (chunk, copy) in enumerate(zip(chunks, copies)):
        copy.wait()
        for at, out in enumerate((far, near)):
            term = dot(rows[at, :, chunk], w[chunk, :])
            out[...] = term if n == 0 else out[...] + term


def products(place, tok, w):
    return kernel(
        main_products,
        [((GROUP, MAIN), F32)] * 2,
        (place, tok, w),
        4 * GROUP * HALF * MAIN, 56,
        scratch=[
            pltpu.VMEM((2, GROUP, HALF), BF16),
            pltpu.VMEM((HALF, MAIN), BF16),
            pltpu.SemaphoreType.DMA((2 + HALF // COLUMNS,)),
        ],
        in_hbm=2,
    )


def score(place, near, partner, side, b_gate, b_up, readout, signs, count, message, low_t, k_out, k, sems):
    low_b = side[:, SIDE:].astype(BF16)
    main = near[...] + partner[...]
    gate_ref = jnp.concatenate([main[:, 0:GATE], side[:, 0 : UNITS - GATE]], axis=1)
    up_ref = jnp.concatenate([main[:, GATE:], side[:, UNITS - GATE : SIDE]], axis=1)
    gate_pol = gate_ref + dot(low_b, b_gate[...])
    up_pol = up_ref + dot(low_b, b_up[...])
    sig_ref = jax.nn.sigmoid(gate_ref)
    sig_pol = jax.nn.sigmoid(gate_pol)
    act_pol = gate_pol * sig_pol
    read = readout[...].astype(F32)
    change = act_pol * up_pol - gate_ref * sig_ref * up_ref
    k_gate = read * sig_pol * (1.0 + gate_pol * (1.0 - sig_pol)) * up_pol
    k_up = read * act_pol
    read_b = jnp.broadcast_to(readout[...], (8, UNITS))
    change_row = sum(dot(read_b, part, CONTRACT_LAST) for part in split(change, 3))
    sign = signs[place[0]]
    gaps = sum(dot(part, sign, CONTRACT_LAST) for part in split(change_row, 3))
    tail = jnp.broadcast_to(gaps[0:1, :] + count[...], (RANK, LANES))
    high, rest = split(k_gate, 2)
    k[0], k[1] = high, rest
    copies = [pltpu.make_async_copy(k.at[i], k_out.at[i], sems.at[i]) for i in range(4)]
    copies[0].start()
    copies[1].start()
    mixed = dot(b_gate[0:RANK, :], high, CONTRACT_LAST) + dot(b_gate[0:RANK, :], rest, CONTRACT_LAST)
    high, rest = split(k_up, 2)
    k[2], k[3] = high, rest
    copies[2].start()
    copies[3].start()
    mixed_up = dot(b_up[RANK : 2 * RANK, :], high, CONTRACT_LAST) + dot(b_up[RANK : 2 * RANK, :], rest, CONTRACT_LAST)
    for core in range(2):
        lines = slice(RANK * core, RANK * (core + 1))
        for i, value in enumerate((mixed, mixed_up)):
            message[lines, 0, i * GROUP : (i + 1) * GROUP] = value
        message[lines, 0, 2 * GROUP :] = tail
    low_t[...] = low_b.astype(F32).T[0 : 2 * RANK, :]
    for copy in copies:
        copy.wait()


def close(place, arrived, signs, valid, low_t, k_in, tok_in, out, total_out, k, tok, sems):
    tok_copy = pltpu.make_async_copy(tok_in, tok, sems.at[0])
    k_copy = pltpu.make_async_copy(k_in, k, sems.at[1])
    tok_copy.start()
    k_copy.start()
    core = place[0]
    sums = [jnp.sum(arrived[RANK * h : RANK * (h + 1)], axis=0) for h in range(2)]
    tails = [total[:, 2 * GROUP :] for total in sums]
    line = lax.broadcasted_iota(jnp.int32, (8, GROUP), 0)
    pair_total = jnp.maximum(tails[0][:, 64:65] + tails[1][:, 64:65], 1.0)
    logs, cotangents, terms = 0.0, [], []
    for h in range(2):
        logit = DPO_BETA * tails[h]
        logs = logs + jnp.sum(
            valid[h] * (jnp.minimum(logit, 0.0) - jnp.log1p(jnp.exp(-jnp.abs(logit)))), axis=1, keepdims=True
        )
        scaled = -LOSS_SCALE * DPO_BETA * valid[h] * jax.nn.sigmoid(-logit) / pair_total
        scaled = jnp.broadcast_to(scaled, (8, LANES))
        cotangent = sum(dot(part, signs[h]) for part in split(scaled, 3))
        cotangents.append(cotangent[0:1, :])
        gate, up = (sums[h][:, i * GROUP : (i + 1) * GROUP] for i in range(2))
        projected = jnp.where(line == 0, gate, jnp.where(line == 1, up, 0.0)) * cotangent
        if h == 0:
            tok_copy.wait()
        terms.append(dot(projected.astype(BF16), tok[h * GROUP : (h + 1) * GROUP, 0:HALF]))
    grad_a = terms[0] + terms[1]
    own = jnp.where(core == 0, cotangents[0], cotangents[1])
    high, rest = split(low_t[...] * own, 2)
    k_copy.wait()
    gate = dot(high[0:RANK], k[0]) + dot(high[0:RANK], k[1]) + dot(rest[0:RANK], k[0])
    up = dot(high[RANK:], k[2]) + dot(high[RANK:], k[3]) + dot(rest[RANK:], k[2])
    out[0:RANK, 0, 0:UNITS] = gate
    out[RANK : 2 * RANK, 0, 0:UNITS] = up
    line = lax.broadcasted_iota(jnp.int32, (2 * RANK, SLICE), 0)
    for column in range(2):
        slices = jnp.zeros((2 * RANK, SLICE), F32)
        for i in range(RANK):
            here = jnp.broadcast_to(
                grad_a[column : column + 1, i * SLICE : (i + 1) * SLICE], (2 * RANK, SLICE)
            )
            slices = jnp.where(line == 2 * i + core, here, slices)
        out[:, 0, UNITS + column * SLICE : UNITS + (column + 1) * SLICE] = slices
    out[:, 0, UNITS + 2 * SLICE :] = jnp.broadcast_to(0.5 * logs, (2 * RANK, LANES))
    total_out[...] = jnp.broadcast_to(pair_total, (8, LANES))


def kernel(function, shapes, arguments, flops, grant, scratch=(), in_hbm=0, out_hbm=0):
    vmem = pl.BlockSpec(memory_space=pltpu.VMEM)
    smem = pl.BlockSpec(memory_space=pltpu.SMEM)
    hbm = pl.BlockSpec(memory_space=pltpu.HBM)
    return pl.pallas_call(
        function,
        out_shape=tuple(jax.ShapeDtypeStruct(*s) for s in shapes),
        in_specs=[smem] + [vmem] * (len(arguments) - 1 - in_hbm) + [hbm] * in_hbm,
        out_specs=(vmem,) * (len(shapes) - out_hbm) + (hbm,) * out_hbm,
        scratch_shapes=list(scratch),
        compiler_params=pltpu.CompilerParams(vmem_limit_bytes=grant * 1024 * 1024),
        cost_estimate=pl.CostEstimate(flops=flops, bytes_accessed=10_000_000, transcendentals=0),
    )(*arguments)


def along(value, axis, k):
    n = lax.axis_size(axis)
    return lax.ppermute(value, axis, [(i, (i + k) % n) for i in range(n)])


def fetch(value, axis, k):
    n = lax.axis_size(axis)
    return lax.ppermute(value, axis, [((i + k) % n, i) for i in range(n)])


def on_device(tokens, sequence_labels, response_mask, frozen, down, up, readout):
    yh, x, core, z, yl = (lax.axis_index(a) for a in AXES)
    place = jnp.stack([core, z, yh, x]).astype(jnp.int32)
    code = jnp.where(response_mask > 0, sequence_labels, SEQS)

    main = jnp.concatenate([frozen[0, :, :GATE], frozen[1, :, :UP]], axis=1)
    w_main = lax.all_gather(main, ("yh", "x"), axis=0, tiled=True)

    by_core = tokens.reshape(ROWS, 16, 2, SLICE).transpose(2, 0, 1, 3).reshape(2, ROWS, HALF)
    code_lanes = jnp.pad(code.reshape(ROWS, 1).astype(BF16), ((0, 0), (0, LANES - 1)))
    keep = jnp.concatenate([jnp.where(core == 0, by_core[0], by_core[1]), code_lanes], axis=1)
    give = jnp.concatenate([jnp.where(core == 0, by_core[1], by_core[0]), code_lanes], axis=1)
    take = lax.ppermute(give, "c", SWAP)
    pair = jnp.where(
        core == 0, jnp.concatenate([keep, take], axis=0), jnp.concatenate([take, keep], axis=0)
    )
    has = [jnp.max((code == q).astype(F32)) for q in range(SEQS)]
    count_rows = jnp.broadcast_to((has[0] * has[1] + has[2] * has[3]).astype(BF16), (16, SIDE))
    piece = jnp.concatenate(
        [jnp.concatenate([frozen[0, :, GATE:], frozen[1, :, UP:]], axis=1), count_rows], axis=0
    )
    pieces = [piece] + [fetch(piece, "yh", k) for k in (1, 2, 3)]
    pair, *pieces = lax.optimization_barrier((pair, *pieces))
    four = swapped(pair, "yl", yl).reshape(4 * ROWS, HALF + LANES)
    ring = [four, along(four, "z", 1), along(four, "z", -1)]
    stack = jnp.concatenate(pieces, axis=0)
    next_x, last_x = fetch(stack, "x", 1), fetch(stack, "x", 3)
    stacks = [stack, next_x, last_x, fetch(last_x[: 2 * PIECE], "x", 3), fetch(next_x[2 * PIECE :], "x", 1)]
    for step in range(2):
        ring += [along(ring[-2], "z", 1), along(ring[-1], "z", -1)]
    ring.append(along(ring[-2], "z", 1))

    down_half = down.reshape(16, 2, SLICE, 2 * RANK)
    down_half = jnp.where(core == 0, down_half[:, 0], down_half[:, 1]).reshape(HALF, 2 * RANK)
    down_half = jnp.pad(down_half, ((0, 0), (0, LANES - 2 * RANK)))
    side_far, side, count_lanes, tok = kernel(
        early_products,
        [((GROUP, SIDE + LANES), F32)] * 2 + [((1, LANES), F32), ((2 * GROUP, HALF + LANES), BF16)],
        (place, down_half, *ring, *stacks),
        4 * GROUP * HALF * (SIDE + LANES), 56,
        scratch=[
            pltpu.VMEM((2 * GROUP, HALF + LANES), BF16),
            pltpu.VMEM((HALF, SIDE), BF16),
            pltpu.VMEM((16, PIECE - SLICE, LANES), BF16),
            pltpu.SemaphoreType.DMA((41,)),
        ],
        in_hbm=13, out_hbm=1,
    )
    side = side + lax.ppermute(side_far, "c", SWAP)

    b_gate = jnp.pad(up[:RANK], ((0, LANES - RANK), (0, 0)))
    b_up = jnp.pad(up[RANK:], ((RANK, LANES - 2 * RANK), (0, 0)))
    read = readout.reshape(1, UNITS)

    codes = tok[:, HALF].astype(jnp.int32).reshape(2, GROUP)
    pair_of = jnp.arange(LANES, dtype=jnp.int32)
    block_of = jnp.arange(GROUP, dtype=jnp.int32) // ROWS
    inside = (pair_of[:, None] // 2 == block_of[None, :])[None]
    chosen = inside & (codes[:, None, :] == 2 * (pair_of % 2)[None, :, None])
    rejected = inside & (codes[:, None, :] == 2 * (pair_of % 2)[None, :, None] + 1)
    signs = chosen.astype(BF16) - rejected.astype(BF16)
    valid = (jnp.any(chosen, axis=2) & jnp.any(rejected, axis=2)).astype(F32).reshape(2, 1, LANES)

    w_main, side, b_gate, b_up, read, count_lanes = lax.optimization_barrier(
        (w_main, side, b_gate, b_up, read, count_lanes)
    )
    far, near = products(place, tok, w_main)
    partner = lax.ppermute(far, "c", SWAP)
    message, low_t, k = kernel(
        score,
        [((2 * RANK, 1, 2 * GROUP + LANES), F32), ((2 * RANK, GROUP), F32), ((4, GROUP, UNITS), BF16)],
        (place, near, partner, side, b_gate, b_up, read, signs, count_lanes),
        8 * GROUP * UNITS * LANES, 16,
        scratch=[pltpu.VMEM((4, GROUP, UNITS), BF16), pltpu.SemaphoreType.DMA((4,))],
        out_hbm=1,
    )
    arrived = lax.all_to_all(message, ("c", "z", "yl"), split_axis=0, concat_axis=0)
    outgoing, pair_total = kernel(
        close,
        [((2 * RANK, 1, UNITS + 2 * SLICE + LANES), F32), ((8, LANES), F32)],
        (place, arrived, signs, valid, low_t, k, tok),
        16 * GROUP * HALF * 2, 16,
        scratch=[
            pltpu.VMEM((4, GROUP, UNITS), BF16),
            pltpu.VMEM((2 * GROUP, HALF + LANES), BF16),
            pltpu.SemaphoreType.DMA((2,)),
        ],
        in_hbm=2,
    )

    summed = jnp.sum(lax.all_to_all(outgoing, DP, split_axis=0, concat_axis=0), axis=0)
    columns = summed[:, UNITS : UNITS + 2 * SLICE].reshape(1, 2, SLICE)
    grad_a = lax.all_to_all(
        jnp.broadcast_to(columns, (16, 2, SLICE)), BLK, split_axis=0, concat_axis=0
    )
    grad_a = grad_a.transpose(2, 1, 0).reshape(SLICE, 2 * RANK)
    return -summed[0, UNITS + 2 * SLICE] / pair_total[0, 0], grad_a, summed[:, :UNITS]


def solution(mesh):
    fine = Mesh(mesh.devices.reshape(SIZES), AXES)
    in_specs = (
        P(AXES, None),
        P(AXES, None),
        P(AXES, None),
        P(None, DP, BLK),
        P(),
        P(None, BLK),
        P(BLK),
    )
    out_specs = (P(), P(DP, None), P(DP, BLK))
    return jax.shard_map(
        on_device, mesh=fine, in_specs=in_specs, out_specs=out_specs, check_vma=False
    )
```
